32 devices in a mesh: seq: 16 (over z, y, core), head: 2 (over x).
Axes of the slice: x: 2, y: 2, z: 4, core: 2. Of those that a mesh axis runs over, the one named last changes fastest.
Arguments:
- queries: bfloat16 [4096, 32, 128], P('seq', 'head'), may hold values from -16 to 16
- keys: bfloat16 [4096, 32, 128], P('seq', 'head'), may hold values from -40 to 40
- values: bfloat16 [4096, 32, 128], P('seq', 'head'), may hold values from -6 to 6
- cluster_ids: int32 [4096, 32], P('seq', 'head'), may hold values from 0 to 511, as said below
- out_weight: bfloat16 [4096, 4096], P('seq', 'head'), may hold values from -0.09375 to 0.09375
Outputs:
- mixed: bfloat16 [4096, 4096], P('seq', 'head')
The draws below stay inside these ranges and needn't reach their ends.
Inputs may be any that keep to these rules, and one draw needn't show every extreme that they name: `cluster_ids`: in each head h, the ids j with j % 16 equal to one residue, drawn from the seed for that head, are never used.
All inputs are finite; a program needn't handle non-finite values.
Results may differ from the reference program's by a relative error of at most 0.008.
The reference program's roundings to bfloat16 on the way (of `centroid`, `attended` and `features`) count: a program that leaves them out, or rounds other values in their place, can miss the bound.
Values may be sent and summed in bfloat16 or wider, within the bound.
No kernel may reach another device: no remote copies, remote signals or barrier semaphores. Data moves between devices by JAX's collectives and lax.ppermute only.
A program may use at most 320 MiB of HBM per device.

```python
import math
import jax
import jax.numpy as jnp
from jax import lax

HEADS = 32
E = 128
C = 512
D = 4096
TOKENS = 4096


def make_ids(key):
    base = jax.random.fold_in(key, 101)
    raw = jax.random.randint(jax.random.fold_in(base, 1), (TOKENS, HEADS), 0, C)
    skipped = jax.random.randint(jax.random.fold_in(base, 2), (HEADS,), 0, 16)
    hit = raw % 16 == skipped[None, :]
    return jnp.where(hit, jnp.bitwise_xor(raw, 1), raw).astype(jnp.int32)


def make_centers(key):
    draws = jax.random.normal(jax.random.fold_in(key, 111), (HEADS, C, E), jnp.float32)
    return 3.0 * jnp.clip(draws, -4.0, 4.0)


def draw_cluster_ids(key, part):
    return make_ids(key)


def draw_queries(key, part):
    labels = make_ids(key)
    centers = make_centers(key)
    noise = jnp.clip(jax.random.normal(jax.random.fold_in(key, 201), (TOKENS, HEADS, E), jnp.float32), -4.0, 4.0)
    picked = centers[jnp.arange(HEADS)[None, :], labels]
    return (noise + picked).astype(jnp.bfloat16)


def draw_keys(key, part):
    result = jnp.clip(jax.random.normal(jax.random.fold_in(key, 301), (TOKENS, HEADS, E), jnp.float32), -4.0, 4.0)
    return result.astype(jnp.bfloat16)


def level_of(key, shape, cuts, low, largest):
    factor_of, own = 1.0, jax.random.fold_in(key, 6)
    for axis_at, parts in cuts:
        heights = jnp.exp(jax.random.uniform(jax.random.fold_in(own, axis_at), (parts,), jnp.float32, low / len(cuts), largest / len(cuts)))
        factor_of = factor_of * jnp.repeat(heights, shape[axis_at] // parts).reshape([-1 if axis == axis_at else 1 for axis in range(len(shape))])
    return factor_of


def bell_draw(key, dims, scale, limit, shards=(), kind=jnp.bfloat16):
    entries = jax.random.normal(key, dims, jnp.float32) * scale
    if len(shards) > 0:
        entries = level_of(key, dims, shards, -0.22, 0.18) * entries
    return jnp.clip(entries, min=-limit, max=limit).astype(kind)


def setup_inputs(seed: int = 0) -> dict:
    arg_keys = jax.random.split(jax.random.key(seed), 6)
    return {
        "queries": draw_queries(jax.random.fold_in(arg_keys[5], 71), 0),
        "keys": draw_keys(jax.random.fold_in(arg_keys[5], 71), 0),
        "values": bell_draw(arg_keys[2], (TOKENS, HEADS, E), 1.0, 6.0, ((0, 16), (1, 2))),
        "cluster_ids": draw_cluster_ids(jax.random.fold_in(arg_keys[5], 71), 0),
        "out_weight": bell_draw(arg_keys[4], (D, D), D ** -0.5, 0.09375, ((0, 16), (1, 2))),
    }


def one_head(operands):
    q_head, k_head, v_head, id_head = operands
    ones = jnp.ones((q_head.shape[0],), jnp.float32)
    counts = jax.ops.segment_sum(ones, id_head, num_segments=C)
    totals = jax.ops.segment_sum(q_head.astype(jnp.float32), id_head, num_segments=C)
    centroid = (totals / jnp.maximum(counts, 1.0)[:, None]).astype(jnp.bfloat16)
    scores = jnp.dot(centroid, k_head.T, preferred_element_type=jnp.float32) * (1.0 / math.sqrt(E))
    top = lax.optimization_barrier(jnp.max(scores, axis=1))
    weights = jnp.exp(scores - top[:, None])
    total = lax.optimization_barrier(jnp.sum(weights, axis=1))
    summed = jnp.dot(weights.astype(jnp.bfloat16), v_head, preferred_element_type=jnp.float32)
    attended = (summed / total[:, None]).astype(jnp.bfloat16)
    return attended[id_head]

def reference(queries, keys, values, cluster_ids, out_weight):
    heads_out = lax.map(one_head, (jnp.transpose(queries, (1, 0, 2)), jnp.transpose(keys, (1, 0, 2)), jnp.transpose(values, (1, 0, 2)), cluster_ids.T))
    features = jnp.transpose(heads_out, (1, 0, 2)).reshape(queries.shape[0], HEADS * E)
    return jnp.dot(features, out_weight, preferred_element_type=jnp.float32).astype(jnp.bfloat16)
```

```python
import math

import jax
import jax.numpy as jnp
from jax import lax
from jax.sharding import PartitionSpec as P

C = 512


def expand_and_project(ids, attended, weight):
    tok_rows = ids.shape[0]
    heads, _, e_width = attended.shape
    labels = lax.broadcasted_iota(jnp.int32, (heads, tok_rows, C), 2)
    onehot = (ids.T[:, :, None] == labels).astype(jnp.bfloat16)
    features = jnp.einsum("htc,hce->the", onehot, attended, preferred_element_type=jnp.float32).astype(
        jnp.bfloat16
    )
    flat = features.reshape(tok_rows, heads * e_width)
    return jnp.dot(flat, weight, preferred_element_type=jnp.float32).astype(jnp.bfloat16)


def by_reduction(queries, keys, values, cluster_ids, out_weight):
    tok_rows, head_count, e_width = queries.shape
    score_scale = 1.0 / math.sqrt(e_width)
    labels = lax.broadcasted_iota(jnp.int32, (head_count, tok_rows, C), 2)
    onehot = (cluster_ids.T[:, :, None] == labels).astype(jnp.bfloat16)
    totals = jnp.einsum("htc,the->hce", onehot, queries, preferred_element_type=jnp.float32)
    counts = jnp.sum(onehot, axis=1, dtype=jnp.float32)
    all_totals, all_counts = lax.psum((totals, counts), "seq")
    centroid = (all_totals / jnp.maximum(all_counts, 1.0)[:, :, None]).astype(jnp.bfloat16)
    scores = jnp.einsum("hce,the->hct", centroid, keys, preferred_element_type=jnp.float32) * score_scale
    local_max = jnp.max(scores, axis=2)
    weights = jnp.exp(scores - local_max[:, :, None])
    local_total = jnp.sum(weights, axis=2)
    local_out = jnp.einsum(
        "hct,the->hce", weights.astype(jnp.bfloat16), values, preferred_element_type=jnp.float32
    )
    global_max = lax.pmax(local_max, "seq")
    factor = jnp.exp(local_max - global_max)
    share_out = lax.psum_scatter(local_out * factor[:, :, None], "seq", scatter_dimension=1, tiled=True)
    share_total = lax.psum_scatter(local_total * factor, "seq", scatter_dimension=1, tiled=True)
    share_attended = (share_out / share_total[:, :, None]).astype(jnp.bfloat16)
    attended = lax.all_gather(share_attended, "seq", axis=1, tiled=True)
    attended = lax.all_gather(attended, "head", axis=0, tiled=True)
    ids = lax.all_gather(cluster_ids, "head", axis=1, tiled=True)
    weight = lax.all_gather(out_weight, "seq", axis=0, tiled=True)
    return expand_and_project(ids, attended, weight)


def by_head(queries, keys, values, cluster_ids, out_weight):
    tok_rows, head_count, e_width = queries.shape
    n_seq = lax.axis_size("seq")
    per = head_count // n_seq
    score_scale = 1.0 / math.sqrt(e_width)
    weight = lax.all_gather(out_weight, "seq", axis=0, tiled=True)
    ids = lax.all_gather(cluster_ids, "head", axis=1, tiled=True)

    packed = jnp.stack([queries, keys, values]).transpose(2, 0, 1, 3)
    moved = lax.all_to_all(packed, "seq", split_axis=0, concat_axis=2, tiled=True)
    q, k, v = moved[:, 0], moved[:, 1], moved[:, 2]
    own_ids = lax.all_to_all(cluster_ids.T, "seq", split_axis=0, concat_axis=1, tiled=True)

    labels = lax.broadcasted_iota(jnp.int32, (per, C, own_ids.shape[1]), 1)
    onehot = (own_ids[:, None, :] == labels).astype(jnp.bfloat16)
    totals = jnp.einsum("hct,hte->hce", onehot, q, preferred_element_type=jnp.float32)
    counts = jnp.sum(onehot, axis=2, dtype=jnp.float32)
    centroid = (totals / jnp.maximum(counts, 1.0)[:, :, None]).astype(jnp.bfloat16)
    scores = jnp.einsum("hce,hte->hct", centroid, k, preferred_element_type=jnp.float32) * score_scale
    weights = jnp.exp(scores - jnp.max(scores, axis=2)[:, :, None])
    total = jnp.sum(weights, axis=2)
    summed = jnp.einsum("hct,hte->hce", weights.astype(jnp.bfloat16), v, preferred_element_type=jnp.float32)
    own = (summed / total[:, :, None]).astype(jnp.bfloat16)
    attended = lax.all_gather(own, ("head", "seq"), axis=0, tiled=True)
    return expand_and_project(ids, attended, weight)


def on_device(queries, keys, values, cluster_ids, out_weight):
    if queries.shape[1] % lax.axis_size("seq") == 0:
        return by_head(queries, keys, values, cluster_ids, out_weight)
    return by_reduction(queries, keys, values, cluster_ids, out_weight)


def solution(mesh):
    placed = (
        P("seq", "head", None),
        P("seq", "head", None),
        P("seq", "head", None),
        P("seq", "head"),
        P("seq", "head"),
    )
    return jax.shard_map(
        on_device, mesh=mesh, in_specs=placed, out_specs=P("seq", "head"), check_vma=False
    )
```

```python
import math

import jax
import jax.numpy as jnp
from jax import lax
from jax.sharding import PartitionSpec as P

C = 512


def expand_and_project(ids, attended, weight):
    tok_rows = ids.shape[0]
    heads, _, e_width = attended.shape
    labels = lax.broadcasted_iota(jnp.int32, (heads, tok_rows, C), 2)
    onehot = (ids.T[:, :, None] == labels).astype(jnp.bfloat16)
    features = jnp.einsum("htc,hce->the", onehot, attended, preferred_element_type=jnp.float32).astype(
        jnp.bfloat16
    )
    flat = features.reshape(tok_rows, heads * e_width)
    return jnp.dot(flat, weight, preferred_element_type=jnp.float32).astype(jnp.bfloat16)


def by_reduction(queries, keys, values, cluster_ids, out_weight):
    tok_rows, head_count, e_width = queries.shape
    score_scale = 1.0 / math.sqrt(e_width)
    labels = lax.broadcasted_iota(jnp.int32, (head_count, tok_rows, C), 2)
    onehot = (cluster_ids.T[:, :, None] == labels).astype(jnp.bfloat16)
    totals = jnp.einsum("htc,the->hce", onehot, queries, preferred_element_type=jnp.float32)
    counts = jnp.sum(onehot, axis=1, dtype=jnp.float32)
    all_totals, all_counts = lax.psum((totals, counts), "seq")
    centroid = (all_totals / jnp.maximum(all_counts, 1.0)[:, :, None]).astype(jnp.bfloat16)
    scores = jnp.einsum("hce,the->hct", centroid, keys, preferred_element_type=jnp.float32) * score_scale
    local_max = jnp.max(scores, axis=2)
    weights = jnp.exp(scores - local_max[:, :, None])
    local_total = jnp.sum(weights, axis=2)
    local_out = jnp.einsum(
        "hct,the->hce", weights.astype(jnp.bfloat16), values, preferred_element_type=jnp.float32
    )
    global_max = lax.pmax(local_max, "seq")
    factor = jnp.exp(local_max - global_max)
    share_out = lax.psum_scatter(local_out * factor[:, :, None], "seq", scatter_dimension=1, tiled=True)
    share_total = lax.psum_scatter(local_total * factor, "seq", scatter_dimension=1, tiled=True)
    share_attended = (share_out / share_total[:, :, None]).astype(jnp.bfloat16)
    attended = lax.all_gather(share_attended, "seq", axis=1, tiled=True)
    attended = lax.all_gather(attended, "head", axis=0, tiled=True)
    ids = lax.all_gather(cluster_ids, "head", axis=1, tiled=True)
    weight = lax.all_gather(out_weight, "seq", axis=0, tiled=True)
    return expand_and_project(ids, attended, weight)


def gather_heads(part):
    n_head = lax.axis_size("head")
    me = lax.axis_index("head")
    whole = jnp.zeros((n_head,) + part.shape, part.dtype)
    whole = lax.dynamic_update_index_in_dim(whole, part, me, 0)
    for shift in range(1, n_head):
        moved = lax.ppermute(part, "head", [(i, (i + shift) % n_head) for i in range(n_head)])
        whole = lax.dynamic_update_index_in_dim(whole, moved, lax.rem(me + n_head - shift, n_head), 0)
    return whole


def by_head(queries, keys, values, cluster_ids, out_weight):
    tok_rows, head_count, e_width = queries.shape
    n_seq = lax.axis_size("seq")
    n_head = lax.axis_size("head")
    per = head_count // n_seq
    tokens = n_seq * tok_rows
    score_scale = 1.0 / math.sqrt(e_width)
    weight = lax.all_gather(out_weight, "seq", axis=0, tiled=True)

    ids_t = cluster_ids.T
    high, low = ids_t // 16, ids_t % 16
    id_rows = -(-2 * tok_rows // (16 * e_width)) * 16
    coded = jnp.concatenate([high, low], axis=1).astype(jnp.bfloat16)
    coded = jnp.pad(coded, ((0, 0), (0, id_rows * e_width - 2 * tok_rows)))
    packed = jnp.concatenate(
        [x.transpose(1, 0, 2) for x in (queries, keys, values)] + [coded.reshape(head_count, id_rows, e_width)],
        axis=1,
    )
    rows = packed.shape[1]
    packed = packed.reshape(n_seq, per, rows, e_width)
    moved = lax.all_to_all(packed, "seq", split_axis=0, concat_axis=0)
    moved = moved.reshape(n_seq, per, rows, e_width).transpose(1, 0, 2, 3)
    q, k, v = (
        moved[:, :, i * tok_rows : (i + 1) * tok_rows].reshape(per, tokens, e_width) for i in range(3)
    )
    coded = moved[:, :, 3 * tok_rows :].reshape(per, n_seq, id_rows * e_width)[:, :, : 2 * tok_rows]
    coded = coded.reshape(per, n_seq, 2, tok_rows).astype(jnp.int32)
    own_ids = (coded[:, :, 0] * 16 + coded[:, :, 1]).reshape(per, tokens)

    labels = lax.broadcasted_iota(jnp.int32, (per, C, tokens), 1)
    onehot = (own_ids[:, None, :] == labels).astype(jnp.bfloat16)
    totals = jnp.einsum("hct,hte->hce", onehot, q, preferred_element_type=jnp.float32)
    counts = jnp.sum(onehot, axis=2, dtype=jnp.float32)
    centroid = (totals / jnp.maximum(counts, 1.0)[:, :, None]).astype(jnp.bfloat16)
    scores = jnp.einsum("hce,hte->hct", centroid, k, preferred_element_type=jnp.float32) * score_scale
    weights = jnp.exp(scores - jnp.max(scores, axis=2)[:, :, None])
    total = jnp.sum(weights, axis=2)
    summed = jnp.einsum("hct,hte->hce", weights.astype(jnp.bfloat16), v, preferred_element_type=jnp.float32)
    own = (summed / total[:, :, None]).astype(jnp.bfloat16)
    labels = lax.broadcasted_iota(jnp.int32, (per, tokens, C), 2)
    onehot = (own_ids[:, :, None] == labels).astype(jnp.bfloat16)
    expanded = jnp.einsum("htc,hce->hte", onehot, own, preferred_element_type=jnp.float32).astype(jnp.bfloat16)
    sent = expanded.reshape(per, n_seq, tok_rows, e_width).transpose(1, 0, 2, 3)
    received = lax.all_to_all(sent, "seq", split_axis=0, concat_axis=0).reshape(head_count, tok_rows, e_width)
    features = gather_heads(received.transpose(1, 0, 2).reshape(tok_rows, head_count * e_width))
    features = features.transpose(1, 0, 2).reshape(tok_rows, n_head * head_count * e_width)
    mixed = jnp.dot(features, weight, preferred_element_type=jnp.float32)
    return mixed.astype(jnp.bfloat16)


def on_device(queries, keys, values, cluster_ids, out_weight):
    if queries.shape[1] % lax.axis_size("seq") == 0:
        return by_head(queries, keys, values, cluster_ids, out_weight)
    return by_reduction(queries, keys, values, cluster_ids, out_weight)


def solution(mesh):
    placed = (
        P("seq", "head", None),
        P("seq", "head", None),
        P("seq", "head", None),
        P("seq", "head"),
        P("seq", "head"),
    )
    return jax.shard_map(
        on_device, mesh=mesh, in_specs=placed, out_specs=P("seq", "head"), check_vma=False
    )
```

```python
import math

import jax
import jax.numpy as jnp
from jax import lax
from jax.experimental import pallas as pl
from jax.experimental.pallas import tpu as pltpu
from jax.sharding import PartitionSpec as P

C = 512


def expand_and_project(ids, attended, weight):
    tok_rows = ids.shape[0]
    heads, _, e_width = attended.shape
    labels = lax.broadcasted_iota(jnp.int32, (heads, tok_rows, C), 2)
    onehot = (ids.T[:, :, None] == labels).astype(jnp.bfloat16)
    features = jnp.einsum("htc,hce->the", onehot, attended, preferred_element_type=jnp.float32).astype(
        jnp.bfloat16
    )
    flat = features.reshape(tok_rows, heads * e_width)
    return jnp.dot(flat, weight, preferred_element_type=jnp.float32).astype(jnp.bfloat16)


def by_reduction(queries, keys, values, cluster_ids, out_weight):
    tok_rows, head_count, e_width = queries.shape
    score_scale = 1.0 / math.sqrt(e_width)
    labels = lax.broadcasted_iota(jnp.int32, (head_count, tok_rows, C), 2)
    onehot = (cluster_ids.T[:, :, None] == labels).astype(jnp.bfloat16)
    totals = jnp.einsum("htc,the->hce", onehot, queries, preferred_element_type=jnp.float32)
    counts = jnp.sum(onehot, axis=1, dtype=jnp.float32)
    all_totals, all_counts = lax.psum((totals, counts), "seq")
    centroid = (all_totals / jnp.maximum(all_counts, 1.0)[:, :, None]).astype(jnp.bfloat16)
    scores = jnp.einsum("hce,the->hct", centroid, keys, preferred_element_type=jnp.float32) * score_scale
    local_max = jnp.max(scores, axis=2)
    weights = jnp.exp(scores - local_max[:, :, None])
    local_total = jnp.sum(weights, axis=2)
    local_out = jnp.einsum(
        "hct,the->hce", weights.astype(jnp.bfloat16), values, preferred_element_type=jnp.float32
    )
    global_max = lax.pmax(local_max, "seq")
    factor = jnp.exp(local_max - global_max)
    share_out = lax.psum_scatter(local_out * factor[:, :, None], "seq", scatter_dimension=1, tiled=True)
    share_total = lax.psum_scatter(local_total * factor, "seq", scatter_dimension=1, tiled=True)
    share_attended = (share_out / share_total[:, :, None]).astype(jnp.bfloat16)
    attended = lax.all_gather(share_attended, "seq", axis=1, tiled=True)
    attended = lax.all_gather(attended, "head", axis=0, tiled=True)
    ids = lax.all_gather(cluster_ids, "head", axis=1, tiled=True)
    weight = lax.all_gather(out_weight, "seq", axis=0, tiled=True)
    return expand_and_project(ids, attended, weight)


def attend_kernel(tok_rows, moved_ref, out_ref, sums_ref, scores_ref, acc_ref):
    n_src, _, e_width = moved_ref.shape
    lanes = e_width
    blocks = tok_rows // lanes
    scale = 1.0 / math.sqrt(e_width)
    cluster = lax.broadcasted_iota(jnp.int32, (C, lanes), 0)
    ones = jnp.ones((tok_rows, e_width), jnp.bfloat16)

    sums_ref[...] = jnp.zeros_like(sums_ref)

    @pl.loop(0, n_src)
    def _(src):
        coded = moved_ref[src, 3 * tok_rows :, :].astype(jnp.float32).astype(jnp.int32)
        parts = []
        for i in range(blocks):
            ids = coded[i : i + 1] * 16 + coded[blocks + i : blocks + i + 1]
            parts.append(jnp.where(cluster == ids, 1.0, 0.0).astype(jnp.bfloat16))
        onehot = jnp.concatenate(parts, axis=1)
        wide = jnp.concatenate([moved_ref[src, :tok_rows, :], ones], axis=1)
        sums_ref[...] += jnp.dot(onehot, wide, preferred_element_type=jnp.float32)

    centroid = (sums_ref[:, :e_width] / jnp.maximum(sums_ref[:, e_width:], 1.0)).astype(jnp.bfloat16)

    def score(src, top):
        keys = moved_ref[src, tok_rows : 2 * tok_rows, :]
        scores = lax.dot_general(centroid, keys, (((1,), (1,)), ((), ())), preferred_element_type=jnp.float32)
        scores_ref[src] = scores
        for i in range(blocks):
            top = jnp.maximum(top, scores[:, i * lanes : (i + 1) * lanes])
        return top

    top = lax.fori_loop(0, n_src, score, jnp.full((C, lanes), -jnp.inf, jnp.float32))
    top = jnp.broadcast_to(jnp.max(top, axis=1, keepdims=True), (C, tok_rows))

    acc_ref[...] = jnp.zeros_like(acc_ref)

    def weigh(src, total):
        weights = jnp.exp((scores_ref[src] - top) * scale)
        for i in range(blocks):
            total += weights[:, i * lanes : (i + 1) * lanes]
        values = moved_ref[src, 2 * tok_rows : 3 * tok_rows, :]
        acc_ref[...] += jnp.dot(weights.astype(jnp.bfloat16), values, preferred_element_type=jnp.float32)
        return total

    total = lax.fori_loop(0, n_src, weigh, jnp.zeros((C, lanes), jnp.float32))
    out_ref[...] = (acc_ref[...] / jnp.sum(total, axis=1, keepdims=True)).astype(jnp.bfloat16)


def attend(moved, tok_rows):
    n_src, _, e_width = moved.shape
    tokens = n_src * tok_rows
    return pl.pallas_call(
        lambda *refs: attend_kernel(tok_rows, *refs),
        out_shape=jax.ShapeDtypeStruct((C, e_width), jnp.bfloat16),
        in_specs=[pl.BlockSpec(memory_space=pltpu.VMEM)],
        out_specs=pl.BlockSpec(memory_space=pltpu.VMEM),
        scratch_shapes=[
            pltpu.VMEM((C, 2 * e_width), jnp.float32),
            pltpu.VMEM((n_src, C, tok_rows), jnp.float32),
            pltpu.VMEM((C, e_width), jnp.float32),
        ],
        compiler_params=pltpu.CompilerParams(vmem_limit_bytes=40 * 2**20),
        cost_estimate=pl.CostEstimate(
            flops=8 * C * tokens * e_width, bytes_accessed=moved.size * 2, transcendentals=C * tokens
        ),
        name="attend",
    )(moved)


def lookup_kernel(ids_ref, attended_ref, weight_ref, out_ref, table_ref):
    heads, clusters, e_width = attended_ref.shape
    tok_tile = ids_ref.shape[0]

    @pl.when(pl.program_id(0) == 0)
    def _():
        @pl.loop(0, heads)
        def _(h):
            part = weight_ref[pl.ds(pl.multiple_of(h * e_width, e_width), e_width), :]
            product = jnp.dot(attended_ref[h], part, preferred_element_type=jnp.float32)
            table_ref[pl.ds(pl.multiple_of(h * clusters, clusters), clusters), :] = product.astype(jnp.bfloat16)

    labels = lax.broadcasted_iota(jnp.int32, (tok_tile, clusters), 1)
    total = None
    for h in range(0, heads, 2):
        onehot = jnp.concatenate(
            [jnp.where(ids_ref[:, i : i + 1] == labels, 1.0, 0.0).astype(jnp.bfloat16) for i in (h, h + 1)], axis=1
        )
        term = jnp.dot(
            onehot, table_ref[h * clusters : (h + 2) * clusters, :], preferred_element_type=jnp.float32
        )
        total = term if total is None else total + term
    out_ref[...] = total.astype(jnp.bfloat16)


def lookup(ids, attended, weight, tok_tile):
    tokens, heads = ids.shape
    _, clusters, e_width = attended.shape
    cols = weight.shape[1]
    return pl.pallas_call(
        lookup_kernel,
        out_shape=jax.ShapeDtypeStruct((tokens, cols), jnp.bfloat16),
        grid=(tokens // tok_tile,),
        in_specs=[
            pl.BlockSpec((tok_tile, heads), lambda i: (i, 0)),
            pl.BlockSpec((heads, clusters, e_width), lambda i: (0, 0, 0)),
            pl.BlockSpec((heads * e_width, cols), lambda i: (0, 0)),
        ],
        out_specs=pl.BlockSpec((tok_tile, cols), lambda i: (i, 0)),
        scratch_shapes=[pltpu.VMEM((heads * clusters, cols), jnp.bfloat16)],
        compiler_params=pltpu.CompilerParams(vmem_limit_bytes=48 * 2**20),
        cost_estimate=pl.CostEstimate(
            flops=2 * tokens * heads * clusters * cols,
            bytes_accessed=2 * (attended.size + weight.size + tokens * cols),
            transcendentals=0,
        ),
        name="lookup",
    )(ids, attended, weight)


def by_head(queries, keys, values, cluster_ids, out_weight):
    tok_rows, head_count, e_width = queries.shape
    n_seq = lax.axis_size("seq")
    n_head = lax.axis_size("head")
    half = n_seq // 2
    rows, cols = out_weight.shape
    cols_each = cols // half
    seq_at = lax.axis_index("seq")

    ids_t = cluster_ids.T
    all_ids = lax.all_gather(ids_t, ("head", "seq"), axis=0, tiled=False)
    all_ids = all_ids.reshape(n_head, n_seq, head_count, tok_rows)
    near_ids = lax.dynamic_slice_in_dim(all_ids, (seq_at // half) * half, half, axis=1)
    near_ids = near_ids.transpose(1, 3, 0, 2).reshape(half * tok_rows, n_head * head_count)

    high, low = ids_t // 16, ids_t % 16
    id_rows = -(-2 * tok_rows // (16 * e_width)) * 16
    coded = jnp.concatenate([high, low], axis=1).astype(jnp.bfloat16)
    coded = jnp.pad(coded, ((0, 0), (0, id_rows * e_width - 2 * tok_rows)))
    packed = jnp.concatenate(
        [x.transpose(1, 0, 2) for x in (queries, keys, values)] + [coded.reshape(head_count, id_rows, e_width)],
        axis=1,
    )
    moved = lax.all_to_all(packed, "seq", split_axis=0, concat_axis=0, tiled=True)

    moved, out_weight = lax.optimization_barrier((moved, out_weight))
    blocks = out_weight.reshape(rows, half, cols_each).transpose(1, 0, 2)
    blocks = jnp.concatenate([blocks, blocks], axis=0)
    weight = lax.all_to_all(blocks, "seq", split_axis=0, concat_axis=0, tiled=True)
    weight = weight.reshape(n_seq * rows, cols_each)

    own = attend(moved, tok_rows)
    attended = lax.all_gather(own, ("head", "seq"), axis=0, tiled=False)
    near = lookup(near_ids, attended, weight, 2 * tok_rows)

    groups = [list(range(half)), list(range(half, n_seq))]
    mixed = lax.all_to_all(
        near.reshape(half, tok_rows, cols_each),
        "seq",
        split_axis=0,
        concat_axis=0,
        axis_index_groups=groups,
        tiled=True,
    )
    return mixed.transpose(1, 0, 2).reshape(tok_rows, cols)


def fits(queries, out_weight):
    n_seq = lax.axis_size("seq")
    tok_rows, head_count, e_width = queries.shape
    return (
        head_count == n_seq
        and n_seq % 2 == 0
        and e_width == 128
        and tok_rows % e_width == 0
        and out_weight.shape[1] % (n_seq // 2 * 128) == 0
    )


def on_device(queries, keys, values, cluster_ids, out_weight):
    if fits(queries, out_weight):
        return by_head(queries, keys, values, cluster_ids, out_weight)
    return by_reduction(queries, keys, values, cluster_ids, out_weight)


def solution(mesh):
    placed = (
        P("seq", "head", None),
        P("seq", "head", None),
        P("seq", "head", None),
        P("seq", "head"),
        P("seq", "head"),
    )
    return jax.shard_map(
        on_device, mesh=mesh, in_specs=placed, out_specs=P("seq", "head"), check_vma=False
    )
```

```python
import math

import jax
import jax.numpy as jnp
from jax import lax
from jax.experimental import pallas as pl
from jax.experimental.pallas import tpu as pltpu
from jax.sharding import PartitionSpec as P

C = 512


def expand_and_project(ids, attended, weight):
    tok_rows = ids.shape[0]
    heads, _, e_width = attended.shape
    labels = lax.broadcasted_iota(jnp.int32, (heads, tok_rows, C), 2)
    onehot = (ids.T[:, :, None] == labels).astype(jnp.bfloat16)
    features = jnp.einsum("htc,hce->the", onehot, attended, preferred_element_type=jnp.float32).astype(
        jnp.bfloat16
    )
    flat = features.reshape(tok_rows, heads * e_width)
    return jnp.dot(flat, weight, preferred_element_type=jnp.float32).astype(jnp.bfloat16)


def by_reduction(queries, keys, values, cluster_ids, out_weight):
    tok_rows, head_count, e_width = queries.shape
    score_scale = 1.0 / math.sqrt(e_width)
    labels = lax.broadcasted_iota(jnp.int32, (head_count, tok_rows, C), 2)
    onehot = (cluster_ids.T[:, :, None] == labels).astype(jnp.bfloat16)
    totals = jnp.einsum("htc,the->hce", onehot, queries, preferred_element_type=jnp.float32)
    counts = jnp.sum(onehot, axis=1, dtype=jnp.float32)
    all_totals, all_counts = lax.psum((totals, counts), "seq")
    centroid = (all_totals / jnp.maximum(all_counts, 1.0)[:, :, None]).astype(jnp.bfloat16)
    scores = jnp.einsum("hce,the->hct", centroid, keys, preferred_element_type=jnp.float32) * score_scale
    local_max = jnp.max(scores, axis=2)
    weights = jnp.exp(scores - local_max[:, :, None])
    local_total = jnp.sum(weights, axis=2)
    local_out = jnp.einsum(
        "hct,the->hce", weights.astype(jnp.bfloat16), values, preferred_element_type=jnp.float32
    )
    global_max = lax.pmax(local_max, "seq")
    factor = jnp.exp(local_max - global_max)
    share_out = lax.psum_scatter(local_out * factor[:, :, None], "seq", scatter_dimension=1, tiled=True)
    share_total = lax.psum_scatter(local_total * factor, "seq", scatter_dimension=1, tiled=True)
    share_attended = (share_out / share_total[:, :, None]).astype(jnp.bfloat16)
    attended = lax.all_gather(share_attended, "seq", axis=1, tiled=True)
    attended = lax.all_gather(attended, "head", axis=0, tiled=True)
    ids = lax.all_gather(cluster_ids, "head", axis=1, tiled=True)
    weight = lax.all_gather(out_weight, "seq", axis=0, tiled=True)
    return expand_and_project(ids, attended, weight)


def attend_kernel(tok_rows, moved_ref, out_ref, sums_ref, scores_ref, acc_ref):
    n_src, _, e_width = moved_ref.shape
    lanes = e_width
    blocks = tok_rows // lanes
    scale = 1.0 / math.sqrt(e_width)
    cluster = lax.broadcasted_iota(jnp.int32, (C, lanes), 0)
    ones = jnp.ones((tok_rows, e_width), jnp.bfloat16)

    sums_ref[...] = jnp.zeros_like(sums_ref)

    @pl.loop(0, n_src)
    def _(src):
        coded = moved_ref[src, 3 * tok_rows :, :].astype(jnp.float32).astype(jnp.int32)
        parts = []
        for i in range(blocks):
            ids = coded[i : i + 1] * 16 + coded[blocks + i : blocks + i + 1]
            parts.append(jnp.where(cluster == ids, 1.0, 0.0).astype(jnp.bfloat16))
        onehot = jnp.concatenate(parts, axis=1)
        wide = jnp.concatenate([moved_ref[src, :tok_rows, :], ones], axis=1)
        sums_ref[...] += jnp.dot(onehot, wide, preferred_element_type=jnp.float32)

    centroid = (sums_ref[:, :e_width] / jnp.maximum(sums_ref[:, e_width:], 1.0)).astype(jnp.bfloat16)

    def score(src, top):
        keys = moved_ref[src, tok_rows : 2 * tok_rows, :]
        scores = lax.dot_general(centroid, keys, (((1,), (1,)), ((), ())), preferred_element_type=jnp.float32)
        scores_ref[src] = scores
        for i in range(blocks):
            top = jnp.maximum(top, scores[:, i * lanes : (i + 1) * lanes])
        return top

    top = lax.fori_loop(0, n_src, score, jnp.full((C, lanes), -jnp.inf, jnp.float32))
    top = jnp.broadcast_to(jnp.max(top, axis=1, keepdims=True), (C, tok_rows))

    acc_ref[...] = jnp.zeros_like(acc_ref)

    def weigh(src, total):
        weights = jnp.exp((scores_ref[src] - top) * scale)
        for i in range(blocks):
            total += weights[:, i * lanes : (i + 1) * lanes]
        values = moved_ref[src, 2 * tok_rows : 3 * tok_rows, :]
        acc_ref[...] += jnp.dot(weights.astype(jnp.bfloat16), values, preferred_element_type=jnp.float32)
        return total

    total = lax.fori_loop(0, n_src, weigh, jnp.zeros((C, lanes), jnp.float32))
    out_ref[...] = (acc_ref[...] / jnp.sum(total, axis=1, keepdims=True)).astype(jnp.bfloat16)


def attend(moved, tok_rows):
    n_src, _, e_width = moved.shape
    tokens = n_src * tok_rows
    return pl.pallas_call(
        lambda *refs: attend_kernel(tok_rows, *refs),
        out_shape=jax.ShapeDtypeStruct((C, e_width), jnp.bfloat16),
        in_specs=[pl.BlockSpec(memory_space=pltpu.VMEM)],
        out_specs=pl.BlockSpec(memory_space=pltpu.VMEM),
        scratch_shapes=[
            pltpu.VMEM((C, 2 * e_width), jnp.float32),
            pltpu.VMEM((n_src, C, tok_rows), jnp.float32),
            pltpu.VMEM((C, e_width), jnp.float32),
        ],
        compiler_params=pltpu.CompilerParams(vmem_limit_bytes=40 * 2**20),
        cost_estimate=pl.CostEstimate(
            flops=8 * C * tokens * e_width, bytes_accessed=moved.size * 2, transcendentals=C * tokens
        ),
        name="attend",
    )(moved)


def expand_kernel(ids_ref, attended_ref, *refs):
    out_ref = refs[-1]
    heads, clusters, e_width = attended_ref.shape
    tok_tile = ids_ref.shape[0]
    labels = lax.broadcasted_iota(jnp.int32, (tok_tile, e_width), 1).astype(jnp.int16)
    one, zero = jnp.bfloat16(1.0), jnp.bfloat16(0.0)
    for h in range(heads):
        ids = jnp.broadcast_to(ids_ref[:, h : h + 1], (tok_tile, e_width)).astype(jnp.int16)
        parts = [
            jnp.where(ids == labels + jnp.int16(at), one, zero) for at in range(0, clusters, e_width)
        ]
        onehot = jnp.concatenate(parts, axis=1)
        found = jnp.dot(onehot, attended_ref[h], preferred_element_type=jnp.float32)
        out_ref[h] = found.astype(jnp.bfloat16)


def expand(ids, attended, store, piece, pieces, tok_tile):
    tokens, heads = ids.shape
    _, clusters, e_width = attended.shape
    held = () if store is None else (store,)
    return pl.pallas_call(
        expand_kernel,
        out_shape=jax.ShapeDtypeStruct((pieces * heads, tokens, e_width), jnp.bfloat16),
        grid=(tokens // tok_tile,),
        in_specs=[
            pl.BlockSpec((tok_tile, heads), lambda i: (i, 0)),
            pl.BlockSpec((heads, clusters, e_width), lambda i: (0, 0, 0)),
        ]
        + [pl.BlockSpec(memory_space=pl.ANY) for _ in held],
        out_specs=pl.BlockSpec((heads, tok_tile, e_width), lambda i: (piece, i, 0)),
        input_output_aliases={2: 0} if held else {},
        compiler_params=pltpu.CompilerParams(vmem_limit_bytes=50 * 2**20),
        cost_estimate=pl.CostEstimate(
            flops=4 * tokens * heads * clusters * e_width,
            bytes_accessed=2 * (attended.size + heads * tokens * e_width),
            transcendentals=0,
        ),
        name="expand",
    )(ids, attended, *held)


def project_kernel(heads_ref, features_ref, weight_ref, out_ref):
    heads, _, e_width = features_ref.shape
    total = None
    for slot in range(0, heads, 2):
        left = jnp.concatenate([features_ref[slot], features_ref[slot + 1]], axis=1)
        starts = [pl.multiple_of(heads_ref[slot + j] * e_width, e_width) for j in range(2)]
        right = jnp.concatenate([weight_ref[pl.ds(at, e_width), :] for at in starts], axis=0)
        term = jnp.dot(left, right, preferred_element_type=jnp.float32)
        total = term if total is None else total + term
    out_ref[...] = total.astype(jnp.bfloat16)


def project(slot_heads, features, weight, tok_tile):
    heads, tokens, e_width = features.shape
    cols = weight.shape[1]
    return pl.pallas_call(
        project_kernel,
        out_shape=jax.ShapeDtypeStruct((tokens, cols), jnp.bfloat16),
        grid_spec=pltpu.PrefetchScalarGridSpec(
            num_scalar_prefetch=1,
            grid=(tokens // tok_tile,),
            in_specs=[
                pl.BlockSpec((heads, tok_tile, e_width), lambda i, _: (0, i, 0)),
                pl.BlockSpec(weight.shape, lambda i, _: (0, 0)),
            ],
            out_specs=pl.BlockSpec((tok_tile, cols), lambda i, _: (i, 0)),
        ),
        compiler_params=pltpu.CompilerParams(vmem_limit_bytes=50 * 2**20),
        cost_estimate=pl.CostEstimate(
            flops=2 * tokens * weight.size,
            bytes_accessed=2 * (features.size + weight.size + tokens * cols),
            transcendentals=0,
        ),
        name="project",
    )(slot_heads, features, weight)


def by_head(queries, keys, values, cluster_ids, out_weight):
    tok_rows, head_count, e_width = queries.shape
    n_seq = lax.axis_size("seq")
    half = n_seq // 2
    rows, cols = out_weight.shape
    cols_each = cols // half
    seq_at = lax.axis_index("seq")
    head_at = lax.axis_index("head")
    core = lax.rem(seq_at, 2)
    swap_heads = [(0, 1), (1, 0)]
    swap_cores = [(i, i ^ 1) for i in range(n_seq)]

    ids_t = cluster_ids.T
    groups = [list(range(half)), list(range(half, n_seq))]
    near_ids = lax.all_to_all(
        jnp.broadcast_to(ids_t[None], (half,) + ids_t.shape),
        "seq",
        split_axis=0,
        concat_axis=0,
        axis_index_groups=groups,
        tiled=True,
    )
    chips = 2 * jnp.arange(half, dtype=jnp.int32)
    slot_heads = jnp.concatenate(
        [plane * head_count + chips + at for plane in (head_at, 1 - head_at) for at in (core, 1 - core)]
    )

    high, low = ids_t // 16, ids_t % 16
    id_rows = -(-2 * tok_rows // (16 * e_width)) * 16
    coded = jnp.concatenate([high, low], axis=1).astype(jnp.bfloat16)
    coded = jnp.pad(coded, ((0, 0), (0, id_rows * e_width - 2 * tok_rows)))
    packed = jnp.concatenate(
        [x.transpose(1, 0, 2) for x in (queries, keys, values)] + [coded.reshape(head_count, id_rows, e_width)],
        axis=1,
    )
    near_ids, packed = lax.optimization_barrier((near_ids, packed))
    near_ids = near_ids.transpose(1, 0, 2).reshape(half, 2, half * tok_rows)
    far_ids = lax.ppermute(near_ids, "head", swap_heads)
    moved = lax.all_to_all(packed, "seq", split_axis=0, concat_axis=0, tiled=True)
    own = attend(moved, tok_rows)
    own, far_ids = lax.optimization_barrier((own, far_ids))
    slot_ids = [
        lax.dynamic_index_in_dim(x, at, 1, keepdims=False).T for x in (near_ids, far_ids) for at in (core, 1 - core)
    ]

    same_core = [list(range(at, n_seq, 2)) for at in range(2)]
    spread = jnp.broadcast_to(own[None], (half,) + own.shape)
    first = lax.all_to_all(
        spread, "seq", split_axis=0, concat_axis=0, axis_index_groups=same_core, tiled=True
    )

    blocks = out_weight.reshape(rows, half, cols_each).transpose(1, 0, 2)
    blocks = jnp.concatenate([blocks, blocks], axis=0)
    first, blocks, slot_ids = lax.optimization_barrier((first, blocks, slot_ids))
    weight = lax.all_to_all(blocks, "seq", split_axis=0, concat_axis=0, tiled=True)
    weight = weight.reshape(n_seq * rows, cols_each)

    third = lax.ppermute(first, "head", swap_heads)
    second = lax.ppermute(first, "seq", swap_cores)
    pieces = len(slot_ids)
    tok_tile = 2 * tok_rows
    features = expand(slot_ids[0], first, None, 0, pieces, tok_tile)
    features = expand(slot_ids[1], second, features, 1, pieces, tok_tile)
    features, third = lax.optimization_barrier((features, third))
    fourth = lax.ppermute(third, "seq", swap_cores)
    features = expand(slot_ids[2], third, features, 2, pieces, tok_tile)
    features = expand(slot_ids[3], fourth, features, 3, pieces, tok_tile)
    near = project(slot_heads, features, weight, 2 * tok_rows)
    mixed = lax.all_to_all(
        near.reshape(half, tok_rows, cols_each),
        "seq",
        split_axis=0,
        concat_axis=0,
        axis_index_groups=groups,
        tiled=True,
    )
    return mixed.transpose(1, 0, 2).reshape(tok_rows, cols)


def fits(queries, out_weight):
    n_seq = lax.axis_size("seq")
    tok_rows, head_count, e_width = queries.shape
    return (
        head_count == n_seq
        and lax.axis_size("head") == 2
        and n_seq % 4 == 0
        and e_width == 128
        and tok_rows % e_width == 0
        and out_weight.shape[1] % (n_seq // 2 * 128) == 0
    )


def on_device(queries, keys, values, cluster_ids, out_weight):
    if fits(queries, out_weight):
        return by_head(queries, keys, values, cluster_ids, out_weight)
    return by_reduction(queries, keys, values, cluster_ids, out_weight)


def solution(mesh):
    placed = (
        P("seq", "head", None),
        P("seq", "head", None),
        P("seq", "head", None),
        P("seq", "head"),
        P("seq", "head"),
    )
    return jax.shard_map(
        on_device, mesh=mesh, in_specs=placed, out_specs=P("seq", "head"), check_vma=False
    )
```

```python
import math

import jax
import jax.numpy as jnp
from jax import lax
from jax.experimental import pallas as pl
from jax.experimental.pallas import tpu as pltpu
from jax.sharding import PartitionSpec as P

C = 512


def expand_and_project(ids, attended, weight):
    tok_rows = ids.shape[0]
    heads, _, e_width = attended.shape
    labels = lax.broadcasted_iota(jnp.int32, (heads, tok_rows, C), 2)
    onehot = (ids.T[:, :, None] == labels).astype(jnp.bfloat16)
    features = jnp.einsum("htc,hce->the", onehot, attended, preferred_element_type=jnp.float32).astype(
        jnp.bfloat16
    )
    flat = features.reshape(tok_rows, heads * e_width)
    return jnp.dot(flat, weight, preferred_element_type=jnp.float32).astype(jnp.bfloat16)


def by_reduction(queries, keys, values, cluster_ids, out_weight):
    tok_rows, head_count, e_width = queries.shape
    score_scale = 1.0 / math.sqrt(e_width)
    labels = lax.broadcasted_iota(jnp.int32, (head_count, tok_rows, C), 2)
    onehot = (cluster_ids.T[:, :, None] == labels).astype(jnp.bfloat16)
    totals = jnp.einsum("htc,the->hce", onehot, queries, preferred_element_type=jnp.float32)
    counts = jnp.sum(onehot, axis=1, dtype=jnp.float32)
    all_totals, all_counts = lax.psum((totals, counts), "seq")
    centroid = (all_totals / jnp.maximum(all_counts, 1.0)[:, :, None]).astype(jnp.bfloat16)
    scores = jnp.einsum("hce,the->hct", centroid, keys, preferred_element_type=jnp.float32) * score_scale
    local_max = jnp.max(scores, axis=2)
    weights = jnp.exp(scores - local_max[:, :, None])
    local_total = jnp.sum(weights, axis=2)
    local_out = jnp.einsum(
        "hct,the->hce", weights.astype(jnp.bfloat16), values, preferred_element_type=jnp.float32
    )
    global_max = lax.pmax(local_max, "seq")
    factor = jnp.exp(local_max - global_max)
    share_out = lax.psum_scatter(local_out * factor[:, :, None], "seq", scatter_dimension=1, tiled=True)
    share_total = lax.psum_scatter(local_total * factor, "seq", scatter_dimension=1, tiled=True)
    share_attended = (share_out / share_total[:, :, None]).astype(jnp.bfloat16)
    attended = lax.all_gather(share_attended, "seq", axis=1, tiled=True)
    attended = lax.all_gather(attended, "head", axis=0, tiled=True)
    ids = lax.all_gather(cluster_ids, "head", axis=1, tiled=True)
    weight = lax.all_gather(out_weight, "seq", axis=0, tiled=True)
    return expand_and_project(ids, attended, weight)


def attend_kernel(tok_rows, moved_ref, out_ref, sums_ref, scores_ref, acc_ref):
    n_src, _, e_width = moved_ref.shape
    lanes = e_width
    blocks = tok_rows // lanes
    scale = 1.0 / math.sqrt(e_width)
    cluster = lax.broadcasted_iota(jnp.int32, (C, lanes), 0)
    ones = jnp.ones((tok_rows, e_width), jnp.bfloat16)

    sums_ref[...] = jnp.zeros_like(sums_ref)

    @pl.loop(0, n_src)
    def _(src):
        coded = moved_ref[src, 3 * tok_rows :, :].astype(jnp.float32).astype(jnp.int32)
        parts = []
        for i in range(blocks):
            ids = coded[i : i + 1] * 16 + coded[blocks + i : blocks + i + 1]
            parts.append(jnp.where(cluster == ids, 1.0, 0.0).astype(jnp.bfloat16))
        onehot = jnp.concatenate(parts, axis=1)
        wide = jnp.concatenate([moved_ref[src, :tok_rows, :], ones], axis=1)
        sums_ref[...] += jnp.dot(onehot, wide, preferred_element_type=jnp.float32)

    centroid = (sums_ref[:, :e_width] / jnp.maximum(sums_ref[:, e_width:], 1.0)).astype(jnp.bfloat16)

    def score(src, top):
        keys = moved_ref[src, tok_rows : 2 * tok_rows, :]
        scores = lax.dot_general(centroid, keys, (((1,), (1,)), ((), ())), preferred_element_type=jnp.float32)
        scores_ref[src] = scores
        for i in range(blocks):
            top = jnp.maximum(top, scores[:, i * lanes : (i + 1) * lanes])
        return top

    top = lax.fori_loop(0, n_src, score, jnp.full((C, lanes), -jnp.inf, jnp.float32))
    top = jnp.broadcast_to(jnp.max(top, axis=1, keepdims=True), (C, tok_rows))

    acc_ref[...] = jnp.zeros_like(acc_ref)

    def weigh(src, total):
        weights = jnp.exp((scores_ref[src] - top) * scale)
        for i in range(blocks):
            total += weights[:, i * lanes : (i + 1) * lanes]
        values = moved_ref[src, 2 * tok_rows : 3 * tok_rows, :]
        acc_ref[...] += jnp.dot(weights.astype(jnp.bfloat16), values, preferred_element_type=jnp.float32)
        return total

    total = lax.fori_loop(0, n_src, weigh, jnp.zeros((C, lanes), jnp.float32))
    out_ref[...] = (acc_ref[...] / jnp.sum(total, axis=1, keepdims=True)).astype(jnp.bfloat16)


def attend(moved, tok_rows):
    n_src, _, e_width = moved.shape
    tokens = n_src * tok_rows
    return pl.pallas_call(
        lambda *refs: attend_kernel(tok_rows, *refs),
        out_shape=jax.ShapeDtypeStruct((C, e_width), jnp.bfloat16),
        in_specs=[pl.BlockSpec(memory_space=pltpu.VMEM)],
        out_specs=pl.BlockSpec(memory_space=pltpu.VMEM),
        scratch_shapes=[
            pltpu.VMEM((C, 2 * e_width), jnp.float32),
            pltpu.VMEM((n_src, C, tok_rows), jnp.float32),
            pltpu.VMEM((C, e_width), jnp.float32),
        ],
        compiler_params=pltpu.CompilerParams(vmem_limit_bytes=40 * 2**20),
        cost_estimate=pl.CostEstimate(
            flops=8 * C * tokens * e_width, bytes_accessed=moved.size * 2, transcendentals=C * tokens
        ),
        name="attend",
    )(moved)


def expand_kernel(ids_ref, attended_ref, *refs):
    out_ref = refs[-1]
    heads, clusters, e_width = attended_ref.shape
    tok_tile = ids_ref.shape[0]
    labels = lax.broadcasted_iota(jnp.int32, (tok_tile, e_width), 1).astype(jnp.int16)
    one, zero = jnp.bfloat16(1.0), jnp.bfloat16(0.0)
    for h in range(heads):
        ids = jnp.broadcast_to(ids_ref[:, h : h + 1], (tok_tile, e_width)).astype(jnp.int16)
        parts = [
            jnp.where(ids == labels + jnp.int16(at), one, zero) for at in range(0, clusters, e_width)
        ]
        onehot = jnp.concatenate(parts, axis=1)
        found = jnp.dot(onehot, attended_ref[h], preferred_element_type=jnp.float32)
        out_ref[h] = found.astype(jnp.bfloat16)


def expand(ids, attended, store, piece, pieces, tok_tile):
    tokens, heads = ids.shape
    _, clusters, e_width = attended.shape
    held = () if store is None else (store,)
    return pl.pallas_call(
        expand_kernel,
        out_shape=jax.ShapeDtypeStruct((pieces * heads, tokens, e_width), jnp.bfloat16),
        grid=(tokens // tok_tile,),
        in_specs=[
            pl.BlockSpec((tok_tile, heads), lambda i: (i, 0)),
            pl.BlockSpec((heads, clusters, e_width), lambda i: (0, 0, 0)),
        ]
        + [pl.BlockSpec(memory_space=pl.ANY) for _ in held],
        out_specs=pl.BlockSpec((heads, tok_tile, e_width), lambda i: (piece, i, 0)),
        input_output_aliases={2: 0} if held else {},
        compiler_params=pltpu.CompilerParams(vmem_limit_bytes=50 * 2**20),
        cost_estimate=pl.CostEstimate(
            flops=4 * tokens * heads * clusters * e_width,
            bytes_accessed=2 * (attended.size + heads * tokens * e_width),
            transcendentals=0,
        ),
        name="expand",
    )(ids, attended, *held)


def project_kernel(places_ref, features_ref, early_ref, late_ref, out_ref):
    heads = features_ref.shape[0]
    each = heads // 4
    plane_at, core = places_ref[0], places_ref[1]
    total = None
    for plane in range(2):
        first = (plane_at + plane - 2 * plane * plane_at) * each
        for i in range(each):
            slots = [(2 * plane + at) * each + i for at in (core, 1 - core)]
            left = jnp.concatenate([features_ref[at] for at in slots], axis=1)
            right = jnp.concatenate([early_ref[first + i], late_ref[first + i]], axis=0)
            term = jnp.dot(left, right, preferred_element_type=jnp.float32)
            total = term if total is None else total + term
    out_ref[...] = total.astype(jnp.bfloat16)


def project(places, features, early, late, tok_tile):
    heads, tokens, e_width = features.shape
    cols = early.shape[2]
    return pl.pallas_call(
        project_kernel,
        out_shape=jax.ShapeDtypeStruct((tokens, cols), jnp.bfloat16),
        grid_spec=pltpu.PrefetchScalarGridSpec(
            num_scalar_prefetch=1,
            grid=(tokens // tok_tile,),
            in_specs=[
                pl.BlockSpec((heads, tok_tile, e_width), lambda i, _: (0, i, 0)),
                pl.BlockSpec(early.shape, lambda i, _: (0, 0, 0)),
                pl.BlockSpec(late.shape, lambda i, _: (0, 0, 0)),
            ],
            out_specs=pl.BlockSpec((tok_tile, cols), lambda i, _: (i, 0)),
        ),
        compiler_params=pltpu.CompilerParams(vmem_limit_bytes=50 * 2**20),
        cost_estimate=pl.CostEstimate(
            flops=2 * tokens * heads * e_width * cols,
            bytes_accessed=2 * (features.size + heads * e_width * cols + tokens * cols),
            transcendentals=0,
        ),
        name="project",
    )(places, features, early, late)


def by_slot(ids, core):
    return [lax.dynamic_index_in_dim(ids, at, 1, keepdims=False).T for at in (core, 1 - core)]


def by_head(queries, keys, values, cluster_ids, out_weight):
    tok_rows, head_count, e_width = queries.shape
    n_seq = lax.axis_size("seq")
    half = n_seq // 2
    rows, cols = out_weight.shape
    cols_each = cols // half
    seq_at = lax.axis_index("seq")
    head_at = lax.axis_index("head")
    core = lax.rem(seq_at, 2)
    swap_heads = [(0, 1), (1, 0)]
    swap_halves = [(i, (i + half) % n_seq) for i in range(n_seq)]
    swap_cores = [(i, i ^ 1) for i in range(n_seq)]

    groups = [list(range(half)), list(range(half, n_seq))]
    ids_t = cluster_ids.T
    high, low = (ids_t // 16).astype(jnp.bfloat16), (ids_t % 16).astype(jnp.bfloat16)

    cut = rows // 4 // 16 * 16
    ahead = out_weight[:cut].reshape(cut, half, cols_each).transpose(1, 0, 2)
    coded = jnp.broadcast_to(jnp.concatenate([high, low], axis=0)[None], (half, 2 * head_count, tok_rows))
    early = lax.all_to_all(
        jnp.concatenate([ahead, coded], axis=1),
        "seq",
        split_axis=0,
        concat_axis=0,
        axis_index_groups=groups,
        tiled=True,
    )

    id_rows = -(-2 * tok_rows // (16 * e_width)) * 16
    coded = jnp.concatenate([high, low], axis=1)
    coded = jnp.pad(coded, ((0, 0), (0, id_rows * e_width - 2 * tok_rows)))
    packed = jnp.concatenate(
        [x.transpose(1, 0, 2) for x in (queries, keys, values)] + [coded.reshape(head_count, id_rows, e_width)],
        axis=1,
    )
    early, packed = lax.optimization_barrier((early, packed))
    coded = early[:, cut:]
    early = early[:, :cut]
    moved = lax.all_to_all(packed, "seq", split_axis=0, concat_axis=0, tiled=True)
    moved, early = lax.optimization_barrier((moved, early))
    crossed = lax.ppermute(early, "seq", swap_halves)
    own = attend(moved, tok_rows)
    own, crossed, coded, behind = lax.optimization_barrier((own, crossed, coded, out_weight[cut:]))
    coded = coded.astype(jnp.int32)
    near_ids = coded[:, :head_count] * 16 + coded[:, head_count:]
    near_ids = near_ids.transpose(1, 0, 2).reshape(half, 2, half * tok_rows)
    far_ids = lax.ppermute(near_ids, "head", swap_heads)
    slot_ids = by_slot(near_ids, core)
    late = behind.reshape(rows - cut, half, cols_each).transpose(1, 0, 2)
    late = jnp.concatenate([late, late], axis=0)

    same_core = [list(range(at, n_seq, 2)) for at in range(2)]
    spread = jnp.broadcast_to(own[None], (half,) + own.shape)
    first = lax.all_to_all(
        spread, "seq", split_axis=0, concat_axis=0, axis_index_groups=same_core, tiled=True
    )

    first, late, slot_ids, far_ids = lax.optimization_barrier((first, late, slot_ids, far_ids))
    slot_ids = slot_ids + by_slot(far_ids, core)
    late = lax.all_to_all(late, "seq", split_axis=0, concat_axis=0, tiled=True)

    third = lax.ppermute(first, "head", swap_heads)
    second = lax.ppermute(first, "seq", swap_cores)
    pieces = len(slot_ids)
    tok_tile = 2 * tok_rows
    features = expand(slot_ids[0], first, None, 0, pieces, tok_tile)
    features = expand(slot_ids[1], second, features, 1, pieces, tok_tile)
    features, third = lax.optimization_barrier((features, third))
    fourth = lax.ppermute(third, "seq", swap_cores)
    features = expand(slot_ids[2], third, features, 2, pieces, tok_tile)
    features = expand(slot_ids[3], fourth, features, 3, pieces, tok_tile)
    in_lower = seq_at < half
    early = jnp.where(
        in_lower, jnp.concatenate([early, crossed], axis=0), jnp.concatenate([crossed, early], axis=0)
    )
    places = jnp.stack([head_at, core]).astype(jnp.int32)
    near = project(places, features, early, late, tok_tile)
    mixed = lax.all_to_all(
        near.reshape(half, tok_rows, cols_each),
        "seq",
        split_axis=0,
        concat_axis=0,
        axis_index_groups=groups,
        tiled=True,
    )
    return mixed.transpose(1, 0, 2).reshape(tok_rows, cols)


def fits(queries, out_weight):
    n_seq = lax.axis_size("seq")
    tok_rows, head_count, e_width = queries.shape
    return (
        head_count == n_seq
        and lax.axis_size("head") == 2
        and n_seq >= 4
        and n_seq & (n_seq - 1) == 0
        and e_width == 128
        and tok_rows % e_width == 0
        and out_weight.shape[0] == 2 * e_width
        and out_weight.shape[1] == n_seq // 2 * tok_rows
        and out_weight.shape[1] % (n_seq // 2 * 128) == 0
    )


def on_device(queries, keys, values, cluster_ids, out_weight):
    if fits(queries, out_weight):
        return by_head(queries, keys, values, cluster_ids, out_weight)
    return by_reduction(queries, keys, values, cluster_ids, out_weight)


def solution(mesh):
    placed = (
        P("seq", "head", None),
        P("seq", "head", None),
        P("seq", "head", None),
        P("seq", "head"),
        P("seq", "head"),
    )
    return jax.shard_map(
        on_device, mesh=mesh, in_specs=placed, out_specs=P("seq", "head"), check_vma=False
    )
```

```python
import math

import jax
import jax.numpy as jnp
from jax import lax
from jax.experimental import pallas as pl
from jax.experimental.pallas import tpu as pltpu
from jax.sharding import PartitionSpec as P

C = 512


def expand_and_project(ids, attended, weight):
    tok_rows = ids.shape[0]
    heads, _, e_width = attended.shape
    labels = lax.broadcasted_iota(jnp.int32, (heads, tok_rows, C), 2)
    onehot = (ids.T[:, :, None] == labels).astype(jnp.bfloat16)
    features = jnp.einsum("htc,hce->the", onehot, attended, preferred_element_type=jnp.float32).astype(
        jnp.bfloat16
    )
    flat = features.reshape(tok_rows, heads * e_width)
    return jnp.dot(flat, weight, preferred_element_type=jnp.float32).astype(jnp.bfloat16)


def by_reduction(queries, keys, values, cluster_ids, out_weight):
    tok_rows, head_count, e_width = queries.shape
    score_scale = 1.0 / math.sqrt(e_width)
    labels = lax.broadcasted_iota(jnp.int32, (head_count, tok_rows, C), 2)
    onehot = (cluster_ids.T[:, :, None] == labels).astype(jnp.bfloat16)
    totals = jnp.einsum("htc,the->hce", onehot, queries, preferred_element_type=jnp.float32)
    counts = jnp.sum(onehot, axis=1, dtype=jnp.float32)
    all_totals, all_counts = lax.psum((totals, counts), "seq")
    centroid = (all_totals / jnp.maximum(all_counts, 1.0)[:, :, None]).astype(jnp.bfloat16)
    scores = jnp.einsum("hce,the->hct", centroid, keys, preferred_element_type=jnp.float32) * score_scale
    local_max = jnp.max(scores, axis=2)
    weights = jnp.exp(scores - local_max[:, :, None])
    local_total = jnp.sum(weights, axis=2)
    local_out = jnp.einsum(
        "hct,the->hce", weights.astype(jnp.bfloat16), values, preferred_element_type=jnp.float32
    )
    global_max = lax.pmax(local_max, "seq")
    factor = jnp.exp(local_max - global_max)
    share_out = lax.psum_scatter(local_out * factor[:, :, None], "seq", scatter_dimension=1, tiled=True)
    share_total = lax.psum_scatter(local_total * factor, "seq", scatter_dimension=1, tiled=True)
    share_attended = (share_out / share_total[:, :, None]).astype(jnp.bfloat16)
    attended = lax.all_gather(share_attended, "seq", axis=1, tiled=True)
    attended = lax.all_gather(attended, "head", axis=0, tiled=True)
    ids = lax.all_gather(cluster_ids, "head", axis=1, tiled=True)
    weight = lax.all_gather(out_weight, "seq", axis=0, tiled=True)
    return expand_and_project(ids, attended, weight)


def attend_kernel(tok_rows, moved_ref, out_ref, sums_ref, scores_ref, acc_ref):
    n_src, _, e_width = moved_ref.shape
    lanes = e_width
    blocks = tok_rows // lanes
    scale = 1.0 / math.sqrt(e_width)
    cluster = lax.broadcasted_iota(jnp.int32, (C, lanes), 0)
    ones = jnp.ones((tok_rows, e_width), jnp.bfloat16)

    sums_ref[...] = jnp.zeros_like(sums_ref)

    @pl.loop(0, n_src)
    def _(src):
        coded = moved_ref[src, 3 * tok_rows :, :].astype(jnp.float32).astype(jnp.int32)
        parts = []
        for i in range(blocks):
            ids = coded[i : i + 1] * 16 + coded[blocks + i : blocks + i + 1]
            parts.append(jnp.where(cluster == ids, 1.0, 0.0).astype(jnp.bfloat16))
        onehot = jnp.concatenate(parts, axis=1)
        wide = jnp.concatenate([moved_ref[src, :tok_rows, :], ones], axis=1)
        sums_ref[...] += jnp.dot(onehot, wide, preferred_element_type=jnp.float32)

    centroid = (sums_ref[:, :e_width] / jnp.maximum(sums_ref[:, e_width:], 1.0)).astype(jnp.bfloat16)

    def score(src, top):
        keys = moved_ref[src, tok_rows : 2 * tok_rows, :]
        scores = lax.dot_general(centroid, keys, (((1,), (1,)), ((), ())), preferred_element_type=jnp.float32)
        scores_ref[src] = scores
        for i in range(blocks):
            top = jnp.maximum(top, scores[:, i * lanes : (i + 1) * lanes])
        return top

    top = lax.fori_loop(0, n_src, score, jnp.full((C, lanes), -jnp.inf, jnp.float32))
    top = jnp.broadcast_to(jnp.max(top, axis=1, keepdims=True), (C, tok_rows))

    acc_ref[...] = jnp.zeros_like(acc_ref)

    def weigh(src, total):
        weights = jnp.exp((scores_ref[src] - top) * scale)
        for i in range(blocks):
            total += weights[:, i * lanes : (i + 1) * lanes]
        values = moved_ref[src, 2 * tok_rows : 3 * tok_rows, :]
        acc_ref[...] += jnp.dot(weights.astype(jnp.bfloat16), values, preferred_element_type=jnp.float32)
        return total

    total = lax.fori_loop(0, n_src, weigh, jnp.zeros((C, lanes), jnp.float32))
    out_ref[...] = (acc_ref[...] / jnp.sum(total, axis=1, keepdims=True)).astype(jnp.bfloat16)


def attend(moved, tok_rows):
    n_src, _, e_width = moved.shape
    tokens = n_src * tok_rows
    return pl.pallas_call(
        lambda *refs: attend_kernel(tok_rows, *refs),
        out_shape=jax.ShapeDtypeStruct((C, e_width), jnp.bfloat16),
        in_specs=[pl.BlockSpec(memory_space=pltpu.VMEM)],
        out_specs=pl.BlockSpec(memory_space=pltpu.VMEM),
        scratch_shapes=[
            pltpu.VMEM((C, 2 * e_width), jnp.float32),
            pltpu.VMEM((n_src, C, tok_rows), jnp.float32),
            pltpu.VMEM((C, e_width), jnp.float32),
        ],
        compiler_params=pltpu.CompilerParams(vmem_limit_bytes=24 * 2**20),
        cost_estimate=pl.CostEstimate(
            flops=8 * C * tokens * e_width, bytes_accessed=moved.size * 2, transcendentals=C * tokens
        ),
        name="attend",
    )(moved)


def expand_kernel(ids_ref, attended_ref, *refs):
    out_ref = refs[-1]
    heads, clusters, e_width = attended_ref.shape
    tok_tile = ids_ref.shape[2]
    labels = lax.broadcasted_iota(jnp.int32, (tok_tile, e_width), 1).astype(jnp.int16)
    one, zero = jnp.bfloat16(1.0), jnp.bfloat16(0.0)
    columns = ids_ref[0].T
    for h in range(heads):
        ids = jnp.broadcast_to(columns[:, h : h + 1], (tok_tile, e_width)).astype(jnp.int16)
        parts = [jnp.where(ids == labels + jnp.int16(at), one, zero) for at in range(0, clusters, e_width)]
        onehot = jnp.concatenate(parts, axis=1)
        found = jnp.dot(onehot, attended_ref[h], preferred_element_type=jnp.float32)
        out_ref[h] = found.astype(jnp.bfloat16)


def expand(ids, part, attended, store, piece, pieces, tok_tile):
    _, heads, tokens = ids.shape
    _, clusters, e_width = attended.shape
    held = () if store is None else (store,)
    return pl.pallas_call(
        expand_kernel,
        out_shape=jax.ShapeDtypeStruct((pieces * heads, tokens, e_width), jnp.bfloat16),
        grid=(tokens // tok_tile,),
        in_specs=[
            pl.BlockSpec((1, heads, tok_tile), lambda i: (part, 0, i)),
            pl.BlockSpec((heads, clusters, e_width), lambda i: (0, 0, 0)),
        ]
        + [pl.BlockSpec(memory_space=pl.ANY) for _ in held],
        out_specs=pl.BlockSpec((heads, tok_tile, e_width), lambda i: (piece, i, 0)),
        input_output_aliases={2: 0} if held else {},
        compiler_params=pltpu.CompilerParams(vmem_limit_bytes=50 * 2**20),
        cost_estimate=pl.CostEstimate(
            flops=4 * tokens * heads * clusters * e_width,
            bytes_accessed=2 * heads * (clusters + tokens) * e_width,
            transcendentals=0,
        ),
        name="expand",
    )(ids, attended, *held)


def project_kernel(places_ref, features_ref, near_ref, *refs):
    *far_refs, out_ref = refs
    heads, _, e_width = features_ref.shape
    each = heads // 4
    head_at, core, half_at = places_ref[0], places_ref[1], places_ref[2]
    total = None
    for plane, weight_refs in ((half_at, (near_ref,)), (1 - half_at, far_refs)):
        base = jnp.where(plane == head_at, 0, 2 * each)
        for i in range(each):
            slots = [base + at * each + i for at in (core, 1 - core)]
            left = jnp.concatenate([features_ref[at] for at in slots], axis=1)
            chip = jnp.bitwise_xor(half_at, i % 2) * (each // 2) + i // 2
            right = jnp.concatenate([x[chip] for x in weight_refs], axis=0)[: 2 * e_width]
            term = jnp.dot(left, right, preferred_element_type=jnp.float32)
            total = term if total is None else total + term
    out_ref[...] = total.astype(jnp.bfloat16)


def project(places, features, near, far, tok_tile):
    heads, tokens, e_width = features.shape
    cols = near.shape[2]
    return pl.pallas_call(
        project_kernel,
        out_shape=jax.ShapeDtypeStruct((tokens, cols), jnp.bfloat16),
        grid_spec=pltpu.PrefetchScalarGridSpec(
            num_scalar_prefetch=1,
            grid=(tokens // tok_tile,),
            in_specs=[
                pl.BlockSpec((heads, tok_tile, e_width), lambda i, _: (0, i, 0)),
                pl.BlockSpec(near.shape, lambda i, _: (0, 0, 0)),
            ]
            + [pl.BlockSpec(x.shape, lambda i, _: (0, 0, 0)) for x in far],
            out_specs=pl.BlockSpec((tok_tile, cols), lambda i, _: (i, 0)),
        ),
        compiler_params=pltpu.CompilerParams(vmem_limit_bytes=50 * 2**20),
        cost_estimate=pl.CostEstimate(
            flops=2 * tokens * heads * e_width * cols,
            bytes_accessed=2 * (features.size + heads * e_width * cols + tokens * cols),
            transcendentals=0,
        ),
        name="project",
    )(places, features, near, *far)


def by_slot(ids, half_at, core):
    sources, heads, tok_rows = ids.shape
    ids = ids.reshape(sources, 2, heads // 4, 2, tok_rows).transpose(3, 2, 1, 0, 4)
    ids = jnp.where(half_at == 0, ids, ids[:, :, ::-1])
    ids = jnp.where(core == 0, ids, ids[::-1])
    return ids.reshape(2, heads // 2, sources * tok_rows)


def by_head(queries, keys, values, cluster_ids, out_weight):
    tok_rows, head_count, e_width = queries.shape
    n_seq = lax.axis_size("seq")
    half = n_seq // 2
    rows, cols = out_weight.shape
    cols_each = cols // half
    seq_at = lax.axis_index("seq")
    head_at = lax.axis_index("head")
    half_at = seq_at // half
    core = lax.rem(seq_at, 2)
    swap_heads = [(0, 1), (1, 0)]
    swap_halves = [(i, (i + half) % n_seq) for i in range(n_seq)]
    swap_cores = [(i, i ^ 1) for i in range(n_seq)]
    halves = [list(range(half)), list(range(half, n_seq))]
    same_core = [list(range(at + core_of, at + half, 2)) for at in (0, half) for core_of in range(2)]

    ids_t = cluster_ids.T
    high, low = (ids_t // 16).astype(jnp.bfloat16), (ids_t % 16).astype(jnp.bfloat16)
    id_rows = -(-2 * tok_rows // (16 * e_width)) * 16
    coded = jnp.concatenate([high, low], axis=1)
    coded = jnp.pad(coded, ((0, 0), (0, id_rows * e_width - 2 * tok_rows)))
    packed = jnp.concatenate(
        [x.transpose(1, 0, 2) for x in (queries, keys, values)] + [coded.reshape(head_count, id_rows, e_width)],
        axis=1,
    )
    packed, out_weight, high, low = lax.optimization_barrier((packed, out_weight, high, low))
    moved = lax.all_to_all(packed, "seq", split_axis=0, concat_axis=0, tiled=True)

    blocks = out_weight.reshape(rows, half, cols_each).transpose(1, 0, 2)
    coded = jnp.broadcast_to(jnp.concatenate([high, low], axis=0)[None], (half, 2 * head_count, tok_rows))
    blocks = jnp.concatenate([blocks, coded], axis=1)
    moved, blocks = lax.optimization_barrier((moved, blocks))
    near = lax.all_to_all(blocks, "seq", split_axis=0, concat_axis=0, axis_index_groups=halves, tiled=True)
    own = attend(moved, tok_rows)
    own, near = lax.optimization_barrier((own, near))

    def spread(pair):
        copies = jnp.broadcast_to(pair[None], (half // 2,) + pair.shape)
        got = lax.all_to_all(
            copies, "seq", split_axis=0, concat_axis=0, axis_index_groups=same_core, tiled=True
        )
        return got.reshape((half,) + own.shape)

    pair = jnp.stack([own, lax.ppermute(own, "seq", swap_halves)])
    far_pair = lax.ppermute(pair, "head", swap_heads)
    cuts = [rows * share // 256 // 16 * 16 for share in (0, 112, 192, 256)]
    far = [lax.ppermute(near[:, a:b], "seq", swap_halves) for a, b in zip(cuts, cuts[1:])]
    first = spread(pair)

    coded = near[:, rows:].astype(jnp.int32)
    slot_ids = by_slot(coded[:, :head_count] * 16 + coded[:, head_count:], half_at, core)
    far_ids = lax.ppermute(slot_ids, "head", swap_heads)
    first, slot_ids, far_ids, far_pair, far[0] = lax.optimization_barrier(
        (first, slot_ids, far_ids, far_pair, far[0])
    )
    second = lax.ppermute(first, "seq", swap_cores)
    third = spread(far_pair)

    pieces = 4
    tok_tile = 2 * tok_rows
    features = expand(slot_ids, 0, first, None, 0, pieces, tok_tile)
    features = expand(slot_ids, 1, second, features, 1, pieces, tok_tile)
    features, third, far[1] = lax.optimization_barrier((features, third, far[1]))
    fourth = lax.ppermute(third, "seq", swap_cores)
    features = expand(far_ids, 0, third, features, 2, pieces, tok_tile)
    features = expand(far_ids, 1, fourth, features, 3, pieces, tok_tile)
    places = jnp.stack([head_at, core, half_at]).astype(jnp.int32)
    near_out = project(places, features, near, far, tok_tile)
    mixed = lax.all_to_all(
        near_out.reshape(half, tok_rows, cols_each),
        "seq",
        split_axis=0,
        concat_axis=0,
        axis_index_groups=halves,
        tiled=True,
    )
    return mixed.transpose(1, 0, 2).reshape(tok_rows, cols)


def fits(queries, out_weight):
    n_seq = lax.axis_size("seq")
    tok_rows, head_count, e_width = queries.shape
    return (
        head_count == n_seq
        and lax.axis_size("head") == 2
        and n_seq >= 8
        and n_seq & (n_seq - 1) == 0
        and e_width == 128
        and tok_rows % e_width == 0
        and out_weight.shape[0] == 2 * e_width
        and out_weight.shape[1] == n_seq // 2 * tok_rows
        and out_weight.shape[1] % (n_seq // 2 * 128) == 0
    )


def on_device(queries, keys, values, cluster_ids, out_weight):
    if fits(queries, out_weight):
        return by_head(queries, keys, values, cluster_ids, out_weight)
    return by_reduction(queries, keys, values, cluster_ids, out_weight)


def solution(mesh):
    placed = (
        P("seq", "head", None),
        P("seq", "head", None),
        P("seq", "head", None),
        P("seq", "head"),
        P("seq", "head"),
    )
    return jax.shard_map(
        on_device, mesh=mesh, in_specs=placed, out_specs=P("seq", "head"), check_vma=False
    )
```

```python
import math

import jax
import jax.numpy as jnp
from jax import lax
from jax.experimental import pallas as pl
from jax.experimental.pallas import tpu as pltpu
from jax.sharding import PartitionSpec as P

C = 512


def expand_and_project(ids, attended, weight):
    tok_rows = ids.shape[0]
    heads, _, e_width = attended.shape
    labels = lax.broadcasted_iota(jnp.int32, (heads, tok_rows, C), 2)
    onehot = (ids.T[:, :, None] == labels).astype(jnp.bfloat16)
    features = jnp.einsum("htc,hce->the", onehot, attended, preferred_element_type=jnp.float32).astype(
        jnp.bfloat16
    )
    flat = features.reshape(tok_rows, heads * e_width)
    return jnp.dot(flat, weight, preferred_element_type=jnp.float32).astype(jnp.bfloat16)


def by_reduction(queries, keys, values, cluster_ids, out_weight):
    tok_rows, head_count, e_width = queries.shape
    score_scale = 1.0 / math.sqrt(e_width)
    labels = lax.broadcasted_iota(jnp.int32, (head_count, tok_rows, C), 2)
    onehot = (cluster_ids.T[:, :, None] == labels).astype(jnp.bfloat16)
    totals = jnp.einsum("htc,the->hce", onehot, queries, preferred_element_type=jnp.float32)
    counts = jnp.sum(onehot, axis=1, dtype=jnp.float32)
    all_totals, all_counts = lax.psum((totals, counts), "seq")
    centroid = (all_totals / jnp.maximum(all_counts, 1.0)[:, :, None]).astype(jnp.bfloat16)
    scores = jnp.einsum("hce,the->hct", centroid, keys, preferred_element_type=jnp.float32) * score_scale
    local_max = jnp.max(scores, axis=2)
    weights = jnp.exp(scores - local_max[:, :, None])
    local_total = jnp.sum(weights, axis=2)
    local_out = jnp.einsum(
        "hct,the->hce", weights.astype(jnp.bfloat16), values, preferred_element_type=jnp.float32
    )
    global_max = lax.pmax(local_max, "seq")
    factor = jnp.exp(local_max - global_max)
    share_out = lax.psum_scatter(local_out * factor[:, :, None], "seq", scatter_dimension=1, tiled=True)
    share_total = lax.psum_scatter(local_total * factor, "seq", scatter_dimension=1, tiled=True)
    share_attended = (share_out / share_total[:, :, None]).astype(jnp.bfloat16)
    attended = lax.all_gather(share_attended, "seq", axis=1, tiled=True)
    attended = lax.all_gather(attended, "head", axis=0, tiled=True)
    ids = lax.all_gather(cluster_ids, "head", axis=1, tiled=True)
    weight = lax.all_gather(out_weight, "seq", axis=0, tiled=True)
    return expand_and_project(ids, attended, weight)


def attend_kernel(tok_rows, moved_ref, out_ref, sums_ref, scores_ref, acc_ref):
    n_src, _, e_width = moved_ref.shape
    lanes = e_width
    blocks = tok_rows // lanes
    scale = 1.0 / math.sqrt(e_width)
    cluster = lax.broadcasted_iota(jnp.int32, (C, lanes), 0)
    ones = jnp.ones((tok_rows, e_width), jnp.bfloat16)

    sums_ref[...] = jnp.zeros_like(sums_ref)

    @pl.loop(0, n_src)
    def _(src):
        coded = moved_ref[src, 3 * tok_rows :, :].astype(jnp.float32).astype(jnp.int32)
        parts = []
        for i in range(blocks):
            ids = coded[i : i + 1] * 16 + coded[blocks + i : blocks + i + 1]
            parts.append(jnp.where(cluster == ids, 1.0, 0.0).astype(jnp.bfloat16))
        onehot = jnp.concatenate(parts, axis=1)
        wide = jnp.concatenate([moved_ref[src, :tok_rows, :], ones], axis=1)
        sums_ref[...] += jnp.dot(onehot, wide, preferred_element_type=jnp.float32)

    centroid = (sums_ref[:, :e_width] / jnp.maximum(sums_ref[:, e_width:], 1.0)).astype(jnp.bfloat16)

    def score(src, top):
        keys = moved_ref[src, tok_rows : 2 * tok_rows, :]
        scores = lax.dot_general(centroid, keys, (((1,), (1,)), ((), ())), preferred_element_type=jnp.float32)
        scores_ref[src] = scores
        for i in range(blocks):
            top = jnp.maximum(top, scores[:, i * lanes : (i + 1) * lanes])
        return top

    top = lax.fori_loop(0, n_src, score, jnp.full((C, lanes), -jnp.inf, jnp.float32))
    top = jnp.broadcast_to(jnp.max(top, axis=1, keepdims=True), (C, tok_rows))

    acc_ref[...] = jnp.zeros_like(acc_ref)

    def weigh(src, total):
        weights = jnp.exp((scores_ref[src] - top) * scale)
        for i in range(blocks):
            total += weights[:, i * lanes : (i + 1) * lanes]
        values = moved_ref[src, 2 * tok_rows : 3 * tok_rows, :]
        acc_ref[...] += jnp.dot(weights.astype(jnp.bfloat16), values, preferred_element_type=jnp.float32)
        return total

    total = lax.fori_loop(0, n_src, weigh, jnp.zeros((C, lanes), jnp.float32))
    out_ref[...] = (acc_ref[...] / jnp.sum(total, axis=1, keepdims=True)).astype(jnp.bfloat16)


def attend(moved, tok_rows):
    n_src, _, e_width = moved.shape
    tokens = n_src * tok_rows
    return pl.pallas_call(
        lambda *refs: attend_kernel(tok_rows, *refs),
        out_shape=jax.ShapeDtypeStruct((C, e_width), jnp.bfloat16),
        in_specs=[pl.BlockSpec(memory_space=pltpu.VMEM)],
        out_specs=pl.BlockSpec(memory_space=pltpu.VMEM),
        scratch_shapes=[
            pltpu.VMEM((C, 2 * e_width), jnp.float32),
            pltpu.VMEM((n_src, C, tok_rows), jnp.float32),
            pltpu.VMEM((C, e_width), jnp.float32),
        ],
        compiler_params=pltpu.CompilerParams(vmem_limit_bytes=24 * 2**20),
        cost_estimate=pl.CostEstimate(
            flops=8 * C * tokens * e_width, bytes_accessed=moved.size * 2, transcendentals=C * tokens
        ),
        name="attend",
    )(moved)


def expand_kernel(ids_ref, attended_ref, *refs):
    out_ref = refs[-1]
    heads, clusters, e_width = attended_ref.shape
    tok_tile = ids_ref.shape[2]
    labels = lax.broadcasted_iota(jnp.int32, (tok_tile, e_width), 1).astype(jnp.int16)
    one, zero = jnp.bfloat16(1.0), jnp.bfloat16(0.0)
    columns = ids_ref[0].T
    for h in range(heads):
        ids = jnp.broadcast_to(columns[:, h : h + 1], (tok_tile, e_width)).astype(jnp.int16)
        parts = [jnp.where(ids == labels + jnp.int16(at), one, zero) for at in range(0, clusters, e_width)]
        onehot = jnp.concatenate(parts, axis=1)
        found = jnp.dot(onehot, attended_ref[h], preferred_element_type=jnp.float32)
        out_ref[h] = found.astype(jnp.bfloat16)


def expand(ids, part, attended, store, piece, pieces, tok_tile):
    _, heads, tokens = ids.shape
    _, clusters, e_width = attended.shape
    held = () if store is None else (store,)
    return pl.pallas_call(
        expand_kernel,
        out_shape=jax.ShapeDtypeStruct((pieces * heads, tokens, e_width), jnp.bfloat16),
        grid=(tokens // tok_tile,),
        in_specs=[
            pl.BlockSpec((1, heads, tok_tile), lambda i: (part, 0, i)),
            pl.BlockSpec((heads, clusters, e_width), lambda i: (0, 0, 0)),
        ]
        + [pl.BlockSpec(memory_space=pl.ANY) for _ in held],
        out_specs=pl.BlockSpec((heads, tok_tile, e_width), lambda i: (piece, i, 0)),
        input_output_aliases={2: 0} if held else {},
        compiler_params=pltpu.CompilerParams(vmem_limit_bytes=50 * 2**20),
        cost_estimate=pl.CostEstimate(
            flops=4 * tokens * heads * clusters * e_width,
            bytes_accessed=2 * heads * (clusters + tokens) * e_width,
            transcendentals=0,
        ),
        name="expand",
    )(ids, attended, *held)


def project_kernel(places_ref, features_ref, near_ref, *refs):
    *far_refs, out_ref = refs
    heads, _, e_width = features_ref.shape
    each = heads // 4
    head_at, core, half_at, place = (places_ref[i] for i in range(4))
    total = None
    for plane, weight_refs in ((half_at, (near_ref,)), (1 - half_at, far_refs)):
        base = jnp.where(plane == head_at, 0, 2 * each)
        blocks = [(x, i) for x in weight_refs for i in range(x.shape[0])]
        for k, (weight_ref, i) in enumerate(blocks):
            chip = jnp.bitwise_xor(place, k)
            slot = 2 * lax.rem(chip, each // 2) + jnp.bitwise_xor(half_at, lax.div(chip, each // 2))
            left = jnp.concatenate([features_ref[base + at * each + slot] for at in (core, 1 - core)], axis=1)
            right = weight_ref[i, : 2 * e_width, :]
            term = jnp.dot(left, right, preferred_element_type=jnp.float32)
            total = term if total is None else total + term
    out_ref[...] = total.astype(jnp.bfloat16)


def project(places, features, near, far, tok_tile):
    heads, tokens, e_width = features.shape
    cols = near.shape[2]
    return pl.pallas_call(
        project_kernel,
        out_shape=jax.ShapeDtypeStruct((tokens, cols), jnp.bfloat16),
        grid_spec=pltpu.PrefetchScalarGridSpec(
            num_scalar_prefetch=1,
            grid=(tokens // tok_tile,),
            in_specs=[
                pl.BlockSpec((heads, tok_tile, e_width), lambda i, _: (0, i, 0)),
                pl.BlockSpec(near.shape, lambda i, _: (0, 0, 0)),
            ]
            + [pl.BlockSpec(x.shape, lambda i, _: (0, 0, 0)) for x in far],
            out_specs=pl.BlockSpec((tok_tile, cols), lambda i, _: (i, 0)),
        ),
        compiler_params=pltpu.CompilerParams(vmem_limit_bytes=50 * 2**20),
        cost_estimate=pl.CostEstimate(
            flops=2 * tokens * heads * e_width * cols,
            bytes_accessed=2 * (features.size + heads * e_width * cols + tokens * cols),
            transcendentals=0,
        ),
        name="project",
    )(places, features, near, *far)


def by_slot(ids, half_at, core):
    sources, heads, tok_rows = ids.shape
    ids = ids.reshape(sources, 2, heads // 4, 2, tok_rows).transpose(3, 2, 1, 0, 4)
    ids = jnp.where(half_at == 0, ids, ids[:, :, ::-1])
    ids = jnp.where(core == 0, ids, ids[::-1])
    return ids.reshape(2, heads // 2, sources * tok_rows)


def by_head(queries, keys, values, cluster_ids, out_weight):
    tok_rows, head_count, e_width = queries.shape
    n_seq = lax.axis_size("seq")
    half = n_seq // 2
    rows, cols = out_weight.shape
    cols_each = cols // half
    seq_at = lax.axis_index("seq")
    head_at = lax.axis_index("head")
    half_at = seq_at // half
    core = lax.rem(seq_at, 2)
    place = lax.rem(seq_at, half)
    swap_heads = [(0, 1), (1, 0)]
    swap_halves = [(i, (i + half) % n_seq) for i in range(n_seq)]
    swap_cores = [(i, i ^ 1) for i in range(n_seq)]
    halves = [list(range(half)), list(range(half, n_seq))]
    same_core = [list(range(at + core_of, at + half, 2)) for at in (0, half) for core_of in range(2)]

    ids_t = cluster_ids.T
    high, low = (ids_t // 16).astype(jnp.bfloat16), (ids_t % 16).astype(jnp.bfloat16)
    id_rows = -(-2 * tok_rows // (16 * e_width)) * 16
    coded = jnp.concatenate([high, low], axis=1)
    coded = jnp.pad(coded, ((0, 0), (0, id_rows * e_width - 2 * tok_rows)))
    packed = jnp.concatenate(
        [x.transpose(1, 0, 2) for x in (queries, keys, values)] + [coded.reshape(head_count, id_rows, e_width)],
        axis=1,
    )
    packed, out_weight, high, low = lax.optimization_barrier((packed, out_weight, high, low))
    moved = lax.all_to_all(packed, "seq", split_axis=0, concat_axis=0, tiled=True)

    blocks = out_weight.reshape(rows, half, cols_each).transpose(1, 0, 2)
    coded = jnp.concatenate([high, low], axis=0)
    near = []
    for k in range(half):
        block = lax.dynamic_index_in_dim(blocks, jnp.bitwise_xor(place, k), 0, keepdims=False)
        block = jnp.concatenate([block, coded], axis=0)
        near.append(lax.ppermute(block, "seq", [(i, i ^ k) for i in range(n_seq)]) if k else block)
    near = jnp.stack(near)
    moved, near = lax.optimization_barrier((moved, near))
    cuts = [half * i // 4 for i in range(5)]
    far = [lax.ppermute(near[a:b, :rows], "seq", swap_halves) for a, b in zip(cuts[:1], cuts[1:])]
    own = attend(moved, tok_rows)
    own, near, far[0] = lax.optimization_barrier((own, near, far[0]))
    far += [lax.ppermute(near[a:b, :rows], "seq", swap_halves) for a, b in zip(cuts[1:], cuts[2:])]

    def copied(pair):
        return jnp.broadcast_to(pair[None], (half // 2,) + pair.shape)

    def spread(copies):
        got = lax.all_to_all(
            copies, "seq", split_axis=0, concat_axis=0, axis_index_groups=same_core, tiled=True
        )
        return got.reshape((half,) + own.shape)

    pair = jnp.stack([own, lax.ppermute(own, "seq", swap_halves)])
    far_pair = lax.ppermute(pair, "head", swap_heads)
    first = spread(copied(pair))

    coded = near[:, rows:].astype(jnp.int32)
    coded = coded[:, :head_count] * 16 + coded[:, head_count:]
    coded = jnp.concatenate(
        [lax.dynamic_slice_in_dim(coded, jnp.bitwise_xor(place, i), 1, axis=0) for i in range(half)], axis=0
    )
    slot_ids = by_slot(coded, half_at, core)
    far_ids = lax.ppermute(slot_ids, "head", swap_heads)
    far_copies = copied(far_pair)
    first, slot_ids, far_ids, far_copies, far[1] = lax.optimization_barrier(
        (first, slot_ids, far_ids, far_copies, far[1])
    )
    second = lax.ppermute(first, "seq", swap_cores)
    third = spread(far_copies)

    pieces = 4
    tok_tile = 2 * tok_rows
    features = expand(slot_ids, 0, first, None, 0, pieces, tok_tile)
    features = expand(slot_ids, 1, second, features, 1, pieces, tok_tile)
    features, third, far[2] = lax.optimization_barrier((features, third, far[2]))
    fourth = lax.ppermute(third, "seq", swap_cores)
    features = expand(far_ids, 0, third, features, 2, pieces, tok_tile)
    features = expand(far_ids, 1, fourth, features, 3, pieces, tok_tile)
    places = jnp.stack([head_at, core, half_at, place]).astype(jnp.int32)
    near_out = project(places, features, near, far, tok_tile)
    mixed = lax.all_to_all(
        near_out.reshape(half, tok_rows, cols_each),
        "seq",
        split_axis=0,
        concat_axis=0,
        axis_index_groups=halves,
        tiled=True,
    )
    return mixed.transpose(1, 0, 2).reshape(tok_rows, cols)


def fits(queries, out_weight):
    n_seq = lax.axis_size("seq")
    tok_rows, head_count, e_width = queries.shape
    return (
        head_count == n_seq
        and lax.axis_size("head") == 2
        and n_seq >= 8
        and n_seq & (n_seq - 1) == 0
        and e_width == 128
        and tok_rows % e_width == 0
        and out_weight.shape[0] == 2 * e_width
        and out_weight.shape[1] == n_seq // 2 * tok_rows
        and out_weight.shape[1] % (n_seq // 2 * 128) == 0
    )


def on_device(queries, keys, values, cluster_ids, out_weight):
    if fits(queries, out_weight):
        return by_head(queries, keys, values, cluster_ids, out_weight)
    return by_reduction(queries, keys, values, cluster_ids, out_weight)


def solution(mesh):
    placed = (
        P("seq", "head", None),
        P("seq", "head", None),
        P("seq", "head", None),
        P("seq", "head"),
        P("seq", "head"),
    )
    return jax.shard_map(
        on_device, mesh=mesh, in_specs=placed, out_specs=P("seq", "head"), check_vma=False
    )
```

```python
import math

import jax
import jax.numpy as jnp
from jax import lax
from jax.experimental import pallas as pl
from jax.experimental.pallas import tpu as pltpu
from jax.sharding import PartitionSpec as P

C = 512


def expand_and_project(ids, attended, weight):
    tok_rows = ids.shape[0]
    heads, _, e_width = attended.shape
    labels = lax.broadcasted_iota(jnp.int32, (heads, tok_rows, C), 2)
    onehot = (ids.T[:, :, None] == labels).astype(jnp.bfloat16)
    features = jnp.einsum("htc,hce->the", onehot, attended, preferred_element_type=jnp.float32).astype(
        jnp.bfloat16
    )
    flat = features.reshape(tok_rows, heads * e_width)
    return jnp.dot(flat, weight, preferred_element_type=jnp.float32).astype(jnp.bfloat16)


def by_reduction(queries, keys, values, cluster_ids, out_weight):
    tok_rows, head_count, e_width = queries.shape
    score_scale = 1.0 / math.sqrt(e_width)
    labels = lax.broadcasted_iota(jnp.int32, (head_count, tok_rows, C), 2)
    onehot = (cluster_ids.T[:, :, None] == labels).astype(jnp.bfloat16)
    totals = jnp.einsum("htc,the->hce", onehot, queries, preferred_element_type=jnp.float32)
    counts = jnp.sum(onehot, axis=1, dtype=jnp.float32)
    all_totals, all_counts = lax.psum((totals, counts), "seq")
    centroid = (all_totals / jnp.maximum(all_counts, 1.0)[:, :, None]).astype(jnp.bfloat16)
    scores = jnp.einsum("hce,the->hct", centroid, keys, preferred_element_type=jnp.float32) * score_scale
    local_max = jnp.max(scores, axis=2)
    weights = jnp.exp(scores - local_max[:, :, None])
    local_total = jnp.sum(weights, axis=2)
    local_out = jnp.einsum(
        "hct,the->hce", weights.astype(jnp.bfloat16), values, preferred_element_type=jnp.float32
    )
    global_max = lax.pmax(local_max, "seq")
    factor = jnp.exp(local_max - global_max)
    share_out = lax.psum_scatter(local_out * factor[:, :, None], "seq", scatter_dimension=1, tiled=True)
    share_total = lax.psum_scatter(local_total * factor, "seq", scatter_dimension=1, tiled=True)
    share_attended = (share_out / share_total[:, :, None]).astype(jnp.bfloat16)
    attended = lax.all_gather(share_attended, "seq", axis=1, tiled=True)
    attended = lax.all_gather(attended, "head", axis=0, tiled=True)
    ids = lax.all_gather(cluster_ids, "head", axis=1, tiled=True)
    weight = lax.all_gather(out_weight, "seq", axis=0, tiled=True)
    return expand_and_project(ids, attended, weight)


def attend_kernel(tok_rows, moved_ref, out_ref, sums_ref, scores_ref, acc_ref):
    n_src, _, e_width = moved_ref.shape
    lanes = e_width
    blocks = tok_rows // lanes
    scale = 1.0 / math.sqrt(e_width)
    cluster = lax.broadcasted_iota(jnp.int32, (C, lanes), 0)
    ones = jnp.ones((tok_rows, e_width), jnp.bfloat16)

    sums_ref[...] = jnp.zeros_like(sums_ref)

    @pl.loop(0, n_src, unroll=4)
    def _(src):
        coded = moved_ref[src, 3 * tok_rows :, :].astype(jnp.float32).astype(jnp.int32)
        parts = []
        for i in range(blocks):
            ids = coded[i : i + 1] * 16 + coded[blocks + i : blocks + i + 1]
            parts.append(jnp.where(cluster == ids, 1.0, 0.0).astype(jnp.bfloat16))
        onehot = jnp.concatenate(parts, axis=1)
        wide = jnp.concatenate([moved_ref[src, :tok_rows, :], ones], axis=1)
        sums_ref[...] += jnp.dot(onehot, wide, preferred_element_type=jnp.float32)

    centroid = (sums_ref[:, :e_width] / jnp.maximum(sums_ref[:, e_width:], 1.0)).astype(jnp.bfloat16)

    def score(src, top):
        keys = moved_ref[src, tok_rows : 2 * tok_rows, :]
        scores = lax.dot_general(centroid, keys, (((1,), (1,)), ((), ())), preferred_element_type=jnp.float32)
        scores_ref[src] = scores
        for i in range(blocks):
            top = jnp.maximum(top, scores[:, i * lanes : (i + 1) * lanes])
        return top

    top = lax.fori_loop(0, n_src, score, jnp.full((C, lanes), -jnp.inf, jnp.float32), unroll=4)
    top = jnp.broadcast_to(jnp.max(top, axis=1, keepdims=True), (C, tok_rows))

    acc_ref[...] = jnp.zeros_like(acc_ref)

    def weigh(src, total):
        weights = jnp.exp((scores_ref[src] - top) * scale)
        for i in range(blocks):
            total += weights[:, i * lanes : (i + 1) * lanes]
        values = moved_ref[src, 2 * tok_rows : 3 * tok_rows, :]
        acc_ref[...] += jnp.dot(weights.astype(jnp.bfloat16), values, preferred_element_type=jnp.float32)
        return total

    total = lax.fori_loop(0, n_src, weigh, jnp.zeros((C, lanes), jnp.float32), unroll=4)
    out_ref[...] = (acc_ref[...] / jnp.sum(total, axis=1, keepdims=True)).astype(jnp.bfloat16)


def attend(moved, tok_rows):
    n_src, _, e_width = moved.shape
    tokens = n_src * tok_rows
    return pl.pallas_call(
        lambda *refs: attend_kernel(tok_rows, *refs),
        out_shape=jax.ShapeDtypeStruct((C, e_width), jnp.bfloat16),
        in_specs=[pl.BlockSpec(memory_space=pltpu.VMEM)],
        out_specs=pl.BlockSpec(memory_space=pltpu.VMEM),
        scratch_shapes=[
            pltpu.VMEM((C, 2 * e_width), jnp.float32),
            pltpu.VMEM((n_src, C, tok_rows), jnp.float32),
            pltpu.VMEM((C, e_width), jnp.float32),
        ],
        compiler_params=pltpu.CompilerParams(vmem_limit_bytes=24 * 2**20),
        cost_estimate=pl.CostEstimate(
            flops=8 * C * tokens * e_width, bytes_accessed=moved.size * 2, transcendentals=C * tokens
        ),
        name="attend",
    )(moved)


def one_hot(column, clusters, lanes):
    shape = (column.shape[0], lanes)
    labels = lax.broadcasted_iota(jnp.int32, shape, 1).astype(jnp.int16)
    ids = jnp.broadcast_to(column, shape).astype(jnp.int16)
    one, zero = jnp.bfloat16(1.0), jnp.bfloat16(0.0)
    parts = [jnp.where(ids == labels + jnp.int16(at), one, zero) for at in range(0, clusters, lanes)]
    return jnp.concatenate(parts, axis=1)


def expand_kernel(ids_ref, attended_ref, *refs):
    out_ref = refs[-1]
    heads, clusters, e_width = attended_ref.shape
    columns = ids_ref[0].T
    for h in range(heads):
        onehot = one_hot(columns[:, h : h + 1], clusters, e_width)
        found = jnp.dot(onehot, attended_ref[h], preferred_element_type=jnp.float32)
        out_ref[h] = found.astype(jnp.bfloat16)


def expand(ids, part, attended, store, piece, pieces, tok_tile):
    _, heads, tokens = ids.shape
    _, clusters, e_width = attended.shape
    held = () if store is None else (store,)
    return pl.pallas_call(
        expand_kernel,
        out_shape=jax.ShapeDtypeStruct((pieces * heads, tokens, e_width), jnp.bfloat16),
        grid=(tokens // tok_tile,),
        in_specs=[
            pl.BlockSpec((1, heads, tok_tile), lambda i: (part, 0, i)),
            pl.BlockSpec((heads, clusters, e_width), lambda i: (0, 0, 0)),
        ]
        + [pl.BlockSpec(memory_space=pl.ANY) for _ in held],
        out_specs=pl.BlockSpec((heads, tok_tile, e_width), lambda i: (piece, i, 0)),
        input_output_aliases={2: 0} if held else {},
        compiler_params=pltpu.CompilerParams(vmem_limit_bytes=50 * 2**20),
        cost_estimate=pl.CostEstimate(
            flops=4 * tokens * heads * clusters * e_width,
            bytes_accessed=2 * heads * (clusters + tokens) * e_width,
            transcendentals=0,
        ),
        name="expand",
    )(ids, attended, *held)


def slot_of(place, k, half_at, chips):
    chip = jnp.bitwise_xor(place, k)
    return 2 * lax.rem(chip, chips // 2) + jnp.bitwise_xor(half_at, lax.div(chip, chips // 2))


def project_kernel(places_ref, features_ref, near_ref, *refs):
    *far_refs, out_ref = refs
    heads, _, e_width = features_ref.shape
    chips = heads // 2
    head_at, core, half_at, place = (places_ref[i] for i in range(4))

    def add_up(weight_refs):
        total = None
        blocks = [(x, i) for x in weight_refs for i in range(x.shape[0])]
        for k, (weight_ref, i) in enumerate(blocks):
            slot = slot_of(place, k, half_at, chips)
            left = jnp.concatenate([features_ref[at * chips + slot] for at in (core, 1 - core)], axis=1)
            right = weight_ref[i, : 2 * e_width, :]
            term = jnp.dot(left, right, preferred_element_type=jnp.float32)
            total = term if total is None else total + term
        out_ref[...] = total

    @pl.when(half_at == head_at)
    def _():
        add_up((near_ref,))

    @pl.when(half_at != head_at)
    def _():
        add_up(far_refs)


def project(places, features, near, far, tok_tile):
    heads, tokens, e_width = features.shape
    cols = near.shape[2]
    return pl.pallas_call(
        project_kernel,
        out_shape=jax.ShapeDtypeStruct((tokens, cols), jnp.float32),
        grid_spec=pltpu.PrefetchScalarGridSpec(
            num_scalar_prefetch=1,
            grid=(tokens // tok_tile,),
            in_specs=[
                pl.BlockSpec((heads, tok_tile, e_width), lambda i, _: (0, i, 0)),
                pl.BlockSpec(near.shape, lambda i, _: (0, 0, 0)),
            ]
            + [pl.BlockSpec(x.shape, lambda i, _: (0, 0, 0)) for x in far],
            out_specs=pl.BlockSpec((tok_tile, cols), lambda i, _: (i, 0)),
        ),
        compiler_params=pltpu.CompilerParams(vmem_limit_bytes=50 * 2**20),
        cost_estimate=pl.CostEstimate(
            flops=2 * tokens * heads * e_width * cols,
            bytes_accessed=2 * (features.size + heads * e_width * cols + 2 * tokens * cols),
            transcendentals=0,
        ),
        name="project",
    )(places, features, near, *far)


def lookup_kernel(places_ref, ids_ref, same_ref, other_ref, sum_ref, near_ref, *refs):
    *far_refs, out_ref, table_ref = refs
    chips, clusters, e_width = same_ref.shape
    head_at, core, half_at, place = (places_ref[i] for i in range(4))

    def make_table(weight_refs):
        blocks = [(x, i) for x in weight_refs for i in range(x.shape[0])]
        for k, (weight_ref, i) in enumerate(blocks):
            slot = slot_of(place, k, half_at, chips)
            for part, (attended_ref, at) in enumerate(((same_ref, core), (other_ref, 1 - core))):
                right = weight_ref[i, pl.ds(pl.multiple_of(at * e_width, e_width), e_width), :]
                product = jnp.dot(attended_ref[slot], right, preferred_element_type=jnp.float32)
                table_ref[part * chips + slot] = product.astype(jnp.bfloat16)

    first = pl.program_id(0) == 0

    @pl.when(jnp.logical_and(first, half_at != head_at))
    def _():
        make_table((near_ref,))

    @pl.when(jnp.logical_and(first, half_at == head_at))
    def _():
        make_table(far_refs)

    total = sum_ref[...]
    for part in range(2):
        columns = ids_ref[part].T
        for h in range(0, chips, 2):
            onehot = jnp.concatenate(
                [one_hot(columns[:, i : i + 1], clusters, e_width) for i in (h, h + 1)], axis=1
            )
            right = jnp.concatenate([table_ref[part * chips + i] for i in (h, h + 1)], axis=0)
            total += jnp.dot(onehot, right, preferred_element_type=jnp.float32)
    out_ref[...] = total.astype(jnp.bfloat16)


def lookup(places, ids, same, other, sums, near, far, tok_tile):
    chips, clusters, e_width = same.shape
    tokens, cols = sums.shape
    return pl.pallas_call(
        lookup_kernel,
        out_shape=jax.ShapeDtypeStruct((tokens, cols), jnp.bfloat16),
        grid_spec=pltpu.PrefetchScalarGridSpec(
            num_scalar_prefetch=1,
            grid=(tokens // tok_tile,),
            in_specs=[
                pl.BlockSpec((2, chips, tok_tile), lambda i, _: (0, 0, i)),
                pl.BlockSpec(same.shape, lambda i, _: (0, 0, 0)),
                pl.BlockSpec(other.shape, lambda i, _: (0, 0, 0)),
                pl.BlockSpec((tok_tile, cols), lambda i, _: (i, 0)),
                pl.BlockSpec(near.shape, lambda i, _: (0, 0, 0)),
            ]
            + [pl.BlockSpec(x.shape, lambda i, _: (0, 0, 0)) for x in far],
            out_specs=pl.BlockSpec((tok_tile, cols), lambda i, _: (i, 0)),
            scratch_shapes=[pltpu.VMEM((2 * chips, clusters, cols), jnp.bfloat16)],
        ),
        compiler_params=pltpu.CompilerParams(vmem_limit_bytes=50 * 2**20),
        cost_estimate=pl.CostEstimate(
            flops=4 * tokens * chips * clusters * cols,
            bytes_accessed=4 * (same.size + near.size + 2 * tokens * cols),
            transcendentals=0,
        ),
        name="lookup",
    )(places, ids, same, other, sums, near, *far)


def by_slot(ids, half_at, core):
    sources, heads, tok_rows = ids.shape
    ids = ids.reshape(sources, 2, heads // 4, 2, tok_rows).transpose(3, 2, 1, 0, 4)
    ids = jnp.where(half_at == 0, ids, ids[:, :, ::-1])
    ids = jnp.where(core == 0, ids, ids[::-1])
    return ids.reshape(2, heads // 2, sources * tok_rows)


def by_head(queries, keys, values, cluster_ids, out_weight):
    tok_rows, head_count, e_width = queries.shape
    n_seq = lax.axis_size("seq")
    half = n_seq // 2
    rows, cols = out_weight.shape
    cols_each = cols // half
    seq_at = lax.axis_index("seq")
    head_at = lax.axis_index("head")
    half_at = seq_at // half
    core = lax.rem(seq_at, 2)
    place = lax.rem(seq_at, half)
    swap_heads = [(0, 1), (1, 0)]
    swap_halves = [(i, (i + half) % n_seq) for i in range(n_seq)]
    swap_cores = [(i, i ^ 1) for i in range(n_seq)]
    halves = [list(range(half)), list(range(half, n_seq))]
    same_core = [list(range(at + core_of, at + half, 2)) for at in (0, half) for core_of in range(2)]

    ids_t = cluster_ids.T
    high, low = (ids_t // 16).astype(jnp.bfloat16), (ids_t % 16).astype(jnp.bfloat16)
    id_rows = -(-2 * tok_rows // (16 * e_width)) * 16
    coded = jnp.concatenate([high, low], axis=1)
    coded = jnp.pad(coded, ((0, 0), (0, id_rows * e_width - 2 * tok_rows)))
    packed = jnp.concatenate(
        [x.transpose(1, 0, 2) for x in (queries, keys, values)] + [coded.reshape(head_count, id_rows, e_width)],
        axis=1,
    )
    packed, out_weight, high, low = lax.optimization_barrier((packed, out_weight, high, low))
    moved = lax.all_to_all(packed, "seq", split_axis=0, concat_axis=0, tiled=True)

    blocks = out_weight.reshape(rows, half, cols_each).transpose(1, 0, 2)
    coded = jnp.concatenate([high, low], axis=0)
    near = []
    for k in range(half):
        block = lax.dynamic_index_in_dim(blocks, jnp.bitwise_xor(place, k), 0, keepdims=False)
        block = jnp.concatenate([block, coded], axis=0)
        near.append(lax.ppermute(block, "seq", [(i, i ^ k) for i in range(n_seq)]) if k else block)
    near = jnp.stack(near)
    moved, near = lax.optimization_barrier((moved, near))
    cuts = [half * i // 8 for i in (0, 3, 5, 8)]
    far = [lax.ppermute(near[a:b, :rows], "seq", swap_halves) for a, b in zip(cuts[:1], cuts[1:])]
    own = attend(moved, tok_rows)
    own, near, far[0] = lax.optimization_barrier((own, near, far[0]))
    far += [lax.ppermute(near[a:b, :rows], "seq", swap_halves) for a, b in zip(cuts[1:], cuts[2:])]

    def copied(pair):
        return jnp.broadcast_to(pair[None], (half // 2,) + pair.shape)

    def spread(copies):
        got = lax.all_to_all(
            copies, "seq", split_axis=0, concat_axis=0, axis_index_groups=same_core, tiled=True
        )
        return got.reshape((half,) + own.shape)

    pair = jnp.stack([own, lax.ppermute(own, "seq", swap_halves)])
    far_pair = lax.ppermute(pair, "head", swap_heads)
    first = spread(copied(pair))

    coded = near[:, rows:].astype(jnp.int32)
    coded = coded[:, :head_count] * 16 + coded[:, head_count:]
    coded = jnp.concatenate(
        [lax.dynamic_slice_in_dim(coded, jnp.bitwise_xor(place, i), 1, axis=0) for i in range(half)], axis=0
    )
    slot_ids = by_slot(coded, half_at, core)
    far_ids = lax.ppermute(slot_ids, "head", swap_heads)
    far_copies = copied(far_pair)
    first, slot_ids, far_ids, far_copies, far[1] = lax.optimization_barrier(
        (first, slot_ids, far_ids, far_copies, far[1])
    )
    second = lax.ppermute(first, "seq", swap_cores)
    third = spread(far_copies)

    tok_tile = 2 * tok_rows
    features = expand(slot_ids, 0, first, None, 0, 2, tok_tile)
    features = expand(slot_ids, 1, second, features, 1, 2, tok_tile)
    features, third, far[2] = lax.optimization_barrier((features, third, far[2]))
    fourth = lax.ppermute(third, "seq", swap_cores)
    places = jnp.stack([head_at, core, half_at, place]).astype(jnp.int32)
    sums = project(places, features, near, far, tok_tile)
    near_out = lookup(places, far_ids, third, fourth, sums, near, far, tok_tile)
    mixed = lax.all_to_all(
        near_out.reshape(half, tok_rows, cols_each),
        "seq",
        split_axis=0,
        concat_axis=0,
        axis_index_groups=halves,
        tiled=True,
    )
    return mixed.transpose(1, 0, 2).reshape(tok_rows, cols)


def fits(queries, out_weight):
    n_seq = lax.axis_size("seq")
    tok_rows, head_count, e_width = queries.shape
    return (
        head_count == n_seq
        and lax.axis_size("head") == 2
        and n_seq >= 8
        and n_seq & (n_seq - 1) == 0
        and e_width == 128
        and tok_rows % e_width == 0
        and out_weight.shape[0] == 2 * e_width
        and out_weight.shape[1] == n_seq // 2 * tok_rows
        and out_weight.shape[1] % (n_seq // 2 * 128) == 0
    )


def on_device(queries, keys, values, cluster_ids, out_weight):
    if fits(queries, out_weight):
        return by_head(queries, keys, values, cluster_ids, out_weight)
    return by_reduction(queries, keys, values, cluster_ids, out_weight)


def solution(mesh):
    placed = (
        P("seq", "head", None),
        P("seq", "head", None),
        P("seq", "head", None),
        P("seq", "head"),
        P("seq", "head"),
    )
    return jax.shard_map(
        on_device, mesh=mesh, in_specs=placed, out_specs=P("seq", "head"), check_vma=False
    )
```

```python
import math

import jax
import jax.numpy as jnp
from jax import lax
from jax.experimental import pallas as pl
from jax.experimental.pallas import tpu as pltpu
from jax.sharding import PartitionSpec as P

C = 512


def expand_and_project(ids, attended, weight):
    tok_rows = ids.shape[0]
    heads, _, e_width = attended.shape
    labels = lax.broadcasted_iota(jnp.int32, (heads, tok_rows, C), 2)
    onehot = (ids.T[:, :, None] == labels).astype(jnp.bfloat16)
    features = jnp.einsum("htc,hce->the", onehot, attended, preferred_element_type=jnp.float32).astype(
        jnp.bfloat16
    )
    flat = features.reshape(tok_rows, heads * e_width)
    return jnp.dot(flat, weight, preferred_element_type=jnp.float32).astype(jnp.bfloat16)


def by_reduction(queries, keys, values, cluster_ids, out_weight):
    tok_rows, head_count, e_width = queries.shape
    score_scale = 1.0 / math.sqrt(e_width)
    labels = lax.broadcasted_iota(jnp.int32, (head_count, tok_rows, C), 2)
    onehot = (cluster_ids.T[:, :, None] == labels).astype(jnp.bfloat16)
    totals = jnp.einsum("htc,the->hce", onehot, queries, preferred_element_type=jnp.float32)
    counts = jnp.sum(onehot, axis=1, dtype=jnp.float32)
    all_totals, all_counts = lax.psum((totals, counts), "seq")
    centroid = (all_totals / jnp.maximum(all_counts, 1.0)[:, :, None]).astype(jnp.bfloat16)
    scores = jnp.einsum("hce,the->hct", centroid, keys, preferred_element_type=jnp.float32) * score_scale
    local_max = jnp.max(scores, axis=2)
    weights = jnp.exp(scores - local_max[:, :, None])
    local_total = jnp.sum(weights, axis=2)
    local_out = jnp.einsum(
        "hct,the->hce", weights.astype(jnp.bfloat16), values, preferred_element_type=jnp.float32
    )
    global_max = lax.pmax(local_max, "seq")
    factor = jnp.exp(local_max - global_max)
    share_out = lax.psum_scatter(local_out * factor[:, :, None], "seq", scatter_dimension=1, tiled=True)
    share_total = lax.psum_scatter(local_total * factor, "seq", scatter_dimension=1, tiled=True)
    share_attended = (share_out / share_total[:, :, None]).astype(jnp.bfloat16)
    attended = lax.all_gather(share_attended, "seq", axis=1, tiled=True)
    attended = lax.all_gather(attended, "head", axis=0, tiled=True)
    ids = lax.all_gather(cluster_ids, "head", axis=1, tiled=True)
    weight = lax.all_gather(out_weight, "seq", axis=0, tiled=True)
    return expand_and_project(ids, attended, weight)


def attend_kernel(tok_rows, moved_ref, out_ref, sums_ref, scores_ref, acc_ref):
    n_src, _, e_width = moved_ref.shape
    lanes = e_width
    blocks = tok_rows // lanes
    scale = 1.0 / math.sqrt(e_width)
    cluster = lax.broadcasted_iota(jnp.int32, (C, lanes), 0)
    ones = jnp.ones((tok_rows, e_width), jnp.bfloat16)

    sums_ref[...] = jnp.zeros_like(sums_ref)

    @pl.loop(0, n_src, unroll=4)
    def _(src):
        coded = moved_ref[src, 3 * tok_rows :, :].astype(jnp.float32).astype(jnp.int32)
        parts = []
        for i in range(blocks):
            ids = coded[i : i + 1] * 16 + coded[blocks + i : blocks + i + 1]
            parts.append(jnp.where(cluster == ids, 1.0, 0.0).astype(jnp.bfloat16))
        onehot = jnp.concatenate(parts, axis=1)
        wide = jnp.concatenate([moved_ref[src, :tok_rows, :], ones], axis=1)
        sums_ref[...] += jnp.dot(onehot, wide, preferred_element_type=jnp.float32)

    centroid = (sums_ref[:, :e_width] / jnp.maximum(sums_ref[:, e_width:], 1.0)).astype(jnp.bfloat16)

    def score(src, top):
        keys = moved_ref[src, tok_rows : 2 * tok_rows, :]
        scores = lax.dot_general(centroid, keys, (((1,), (1,)), ((), ())), preferred_element_type=jnp.float32)
        scores_ref[src] = scores
        for i in range(blocks):
            top = jnp.maximum(top, scores[:, i * lanes : (i + 1) * lanes])
        return top

    top = lax.fori_loop(0, n_src, score, jnp.full((C, lanes), -jnp.inf, jnp.float32), unroll=4)
    top = jnp.broadcast_to(jnp.max(top, axis=1, keepdims=True), (C, tok_rows))

    acc_ref[...] = jnp.zeros_like(acc_ref)

    def weigh(src, total):
        weights = jnp.exp((scores_ref[src] - top) * scale)
        for i in range(blocks):
            total += weights[:, i * lanes : (i + 1) * lanes]
        values = moved_ref[src, 2 * tok_rows : 3 * tok_rows, :]
        acc_ref[...] += jnp.dot(weights.astype(jnp.bfloat16), values, preferred_element_type=jnp.float32)
        return total

    total = lax.fori_loop(0, n_src, weigh, jnp.zeros((C, lanes), jnp.float32), unroll=4)
    out_ref[...] = (acc_ref[...] / jnp.sum(total, axis=1, keepdims=True)).astype(jnp.bfloat16)


def attend(moved, tok_rows):
    n_src, _, e_width = moved.shape
    tokens = n_src * tok_rows
    return pl.pallas_call(
        lambda *refs: attend_kernel(tok_rows, *refs),
        out_shape=jax.ShapeDtypeStruct((C, e_width), jnp.bfloat16),
        in_specs=[pl.BlockSpec(memory_space=pltpu.VMEM)],
        out_specs=pl.BlockSpec(memory_space=pltpu.VMEM),
        scratch_shapes=[
            pltpu.VMEM((C, 2 * e_width), jnp.float32),
            pltpu.VMEM((n_src, C, tok_rows), jnp.float32),
            pltpu.VMEM((C, e_width), jnp.float32),
        ],
        compiler_params=pltpu.CompilerParams(vmem_limit_bytes=24 * 2**20),
        cost_estimate=pl.CostEstimate(
            flops=8 * C * tokens * e_width, bytes_accessed=moved.size * 2, transcendentals=C * tokens
        ),
        name="attend",
    )(moved)


def expand_kernel(ids_ref, attended_ref, *refs):
    out_ref = refs[-1]
    heads, clusters, e_width = attended_ref.shape
    tok_tile = ids_ref.shape[2]
    labels = lax.broadcasted_iota(jnp.int32, (tok_tile, e_width), 1).astype(jnp.int16)
    one, zero = jnp.bfloat16(1.0), jnp.bfloat16(0.0)
    columns = ids_ref[0].T
    for h in range(heads):
        ids = jnp.broadcast_to(columns[:, h : h + 1], (tok_tile, e_width)).astype(jnp.int16)
        parts = [jnp.where(ids == labels + jnp.int16(at), one, zero) for at in range(0, clusters, e_width)]
        onehot = jnp.concatenate(parts, axis=1)
        found = jnp.dot(onehot, attended_ref[h], preferred_element_type=jnp.float32)
        out_ref[h] = found.astype(jnp.bfloat16)


def expand(ids, part, attended, store, piece, pieces, tok_tile):
    _, heads, tokens = ids.shape
    _, clusters, e_width = attended.shape
    held = () if store is None else (store,)
    return pl.pallas_call(
        expand_kernel,
        out_shape=jax.ShapeDtypeStruct((pieces * heads, tokens, e_width), jnp.bfloat16),
        grid=(tokens // tok_tile,),
        in_specs=[
            pl.BlockSpec((1, heads, tok_tile), lambda i: (part, 0, i)),
            pl.BlockSpec((heads, clusters, e_width), lambda i: (0, 0, 0)),
        ]
        + [pl.BlockSpec(memory_space=pl.ANY) for _ in held],
        out_specs=pl.BlockSpec((heads, tok_tile, e_width), lambda i: (piece, i, 0)),
        input_output_aliases={2: 0} if held else {},
        compiler_params=pltpu.CompilerParams(vmem_limit_bytes=50 * 2**20),
        cost_estimate=pl.CostEstimate(
            flops=4 * tokens * heads * clusters * e_width,
            bytes_accessed=2 * heads * (clusters + tokens) * e_width,
            transcendentals=0,
        ),
        name="expand",
    )(ids, attended, *held)


def project_kernel(places_ref, features_ref, near_ref, *refs):
    *far_refs, out_ref = refs
    heads, _, e_width = features_ref.shape
    each = heads // 4
    head_at, core, half_at, place = (places_ref[i] for i in range(4))
    total = None
    for plane, weight_refs in ((half_at, (near_ref,)), (1 - half_at, far_refs)):
        base = jnp.where(plane == head_at, 0, 2 * each)
        blocks = [(x, i) for x in weight_refs for i in range(x.shape[0])]
        for k, (weight_ref, i) in enumerate(blocks):
            chip = jnp.bitwise_xor(place, k)
            slot = 2 * lax.rem(chip, each // 2) + jnp.bitwise_xor(half_at, lax.div(chip, each // 2))
            left = jnp.concatenate([features_ref[base + at * each + slot] for at in (core, 1 - core)], axis=1)
            right = weight_ref[i, : 2 * e_width, :]
            term = jnp.dot(left, right, preferred_element_type=jnp.float32)
            total = term if total is None else total + term
    out_ref[...] = total.astype(jnp.bfloat16)


def project(places, features, near, far, tok_tile):
    heads, tokens, e_width = features.shape
    cols = near.shape[2]
    return pl.pallas_call(
        project_kernel,
        out_shape=jax.ShapeDtypeStruct((tokens, cols), jnp.bfloat16),
        grid_spec=pltpu.PrefetchScalarGridSpec(
            num_scalar_prefetch=1,
            grid=(tokens // tok_tile,),
            in_specs=[
                pl.BlockSpec((heads, tok_tile, e_width), lambda i, _: (0, i, 0)),
                pl.BlockSpec(near.shape, lambda i, _: (0, 0, 0)),
            ]
            + [pl.BlockSpec(x.shape, lambda i, _: (0, 0, 0)) for x in far],
            out_specs=pl.BlockSpec((tok_tile, cols), lambda i, _: (i, 0)),
        ),
        compiler_params=pltpu.CompilerParams(vmem_limit_bytes=50 * 2**20),
        cost_estimate=pl.CostEstimate(
            flops=2 * tokens * heads * e_width * cols,
            bytes_accessed=2 * (features.size + heads * e_width * cols + tokens * cols),
            transcendentals=0,
        ),
        name="project",
    )(places, features, near, *far)


def by_slot(ids, half_at, core):
    sources, heads, tok_rows = ids.shape
    ids = ids.reshape(sources, 2, heads // 4, 2, tok_rows).transpose(3, 2, 1, 0, 4)
    ids = jnp.where(half_at == 0, ids, ids[:, :, ::-1])
    ids = jnp.where(core == 0, ids, ids[::-1])
    return ids.reshape(2, heads // 2, sources * tok_rows)


def by_head(queries, keys, values, cluster_ids, out_weight):
    tok_rows, head_count, e_width = queries.shape
    n_seq = lax.axis_size("seq")
    half = n_seq // 2
    rows, cols = out_weight.shape
    cols_each = cols // half
    seq_at = lax.axis_index("seq")
    head_at = lax.axis_index("head")
    half_at = seq_at // half
    core = lax.rem(seq_at, 2)
    place = lax.rem(seq_at, half)
    swap_heads = [(0, 1), (1, 0)]
    swap_halves = [(i, (i + half) % n_seq) for i in range(n_seq)]
    swap_cores = [(i, i ^ 1) for i in range(n_seq)]
    halves = [list(range(half)), list(range(half, n_seq))]
    same_core = [list(range(at + core_of, at + half, 2)) for at in (0, half) for core_of in range(2)]

    ids_t = cluster_ids.T
    high, low = (ids_t // 16).astype(jnp.bfloat16), (ids_t % 16).astype(jnp.bfloat16)
    id_rows = -(-2 * tok_rows // (16 * e_width)) * 16
    coded = jnp.concatenate([high, low], axis=1)
    coded = jnp.pad(coded, ((0, 0), (0, id_rows * e_width - 2 * tok_rows)))
    packed = jnp.concatenate(
        [x.transpose(1, 0, 2) for x in (queries, keys, values)] + [coded.reshape(head_count, id_rows, e_width)],
        axis=1,
    )
    packed, out_weight, high, low = lax.optimization_barrier((packed, out_weight, high, low))
    moved = lax.all_to_all(packed, "seq", split_axis=0, concat_axis=0, tiled=True)

    blocks = out_weight.reshape(rows, half, cols_each).transpose(1, 0, 2)
    coded = jnp.concatenate([high, low], axis=0)
    near = []
    for k in range(half):
        block = lax.dynamic_index_in_dim(blocks, jnp.bitwise_xor(place, k), 0, keepdims=False)
        block = jnp.concatenate([block, coded], axis=0)
        near.append(lax.ppermute(block, "seq", [(i, i ^ k) for i in range(n_seq)]) if k else block)
    near = jnp.stack(near)
    moved, near = lax.optimization_barrier((moved, near))
    cuts = [half * i // 8 for i in (0, 1, 2, 4, 6, 8)]
    far = [lax.ppermute(near[a:b, :rows], "seq", swap_halves) for a, b in zip(cuts[:1], cuts[1:])]
    own = attend(moved, tok_rows)
    own, near, far[0] = lax.optimization_barrier((own, near, far[0]))
    far += [lax.ppermute(near[a:b, :rows], "seq", swap_halves) for a, b in zip(cuts[1:], cuts[2:])]

    def copied(pair):
        return jnp.broadcast_to(pair[None], (half // 2,) + pair.shape)

    def spread(copies):
        got = lax.all_to_all(
            copies, "seq", split_axis=0, concat_axis=0, axis_index_groups=same_core, tiled=True
        )
        return got.reshape((half,) + own.shape)

    crossed, far[1] = lax.optimization_barrier((lax.ppermute(own, "seq", swap_halves), far[1]))
    pair = jnp.stack([own, crossed])
    far_pair = lax.ppermute(pair, "head", swap_heads)
    first = spread(copied(pair))

    coded = near[:, rows:].astype(jnp.int32)
    coded = coded[:, :head_count] * 16 + coded[:, head_count:]
    coded = jnp.concatenate(
        [lax.dynamic_slice_in_dim(coded, jnp.bitwise_xor(place, i), 1, axis=0) for i in range(half)], axis=0
    )
    slot_ids = by_slot(coded, half_at, core)
    far_ids = lax.ppermute(slot_ids, "head", swap_heads)
    far_copies = copied(far_pair)
    first, slot_ids, far_ids, far_copies, far[2] = lax.optimization_barrier(
        (first, slot_ids, far_ids, far_copies, far[2])
    )
    second = lax.ppermute(first, "seq", swap_cores)
    third = spread(far_copies)

    pieces = 4
    tok_tile = 2 * tok_rows
    features = expand(slot_ids, 0, first, None, 0, pieces, tok_tile)
    features = expand(slot_ids, 1, second, features, 1, pieces, tok_tile)
    features, third, far[3] = lax.optimization_barrier((features, third, far[3]))
    fourth = lax.ppermute(third, "seq", swap_cores)
    features = expand(far_ids, 0, third, features, 2, pieces, tok_tile)
    features = expand(far_ids, 1, fourth, features, 3, pieces, tok_tile)
    places = jnp.stack([head_at, core, half_at, place]).astype(jnp.int32)
    near_out = project(places, features, near, far, tok_tile)
    mixed = lax.all_to_all(
        near_out.reshape(half, tok_rows, cols_each),
        "seq",
        split_axis=0,
        concat_axis=0,
        axis_index_groups=halves,
        tiled=True,
    )
    return mixed.transpose(1, 0, 2).reshape(tok_rows, cols)


def fits(queries, out_weight):
    n_seq = lax.axis_size("seq")
    tok_rows, head_count, e_width = queries.shape
    return (
        head_count == n_seq
        and lax.axis_size("head") == 2
        and n_seq >= 8
        and n_seq & (n_seq - 1) == 0
        and e_width == 128
        and tok_rows % e_width == 0
        and out_weight.shape[0] == 2 * e_width
        and out_weight.shape[1] == n_seq // 2 * tok_rows
        and out_weight.shape[1] % (n_seq // 2 * 128) == 0
    )


def on_device(queries, keys, values, cluster_ids, out_weight):
    if fits(queries, out_weight):
        return by_head(queries, keys, values, cluster_ids, out_weight)
    return by_reduction(queries, keys, values, cluster_ids, out_weight)


def solution(mesh):
    placed = (
        P("seq", "head", None),
        P("seq", "head", None),
        P("seq", "head", None),
        P("seq", "head"),
        P("seq", "head"),
    )
    return jax.shard_map(
        on_device, mesh=mesh, in_specs=placed, out_specs=P("seq", "head"), check_vma=False
    )
```

```python
import math

import jax
import jax.numpy as jnp
from jax import lax
from jax.experimental import pallas as pl
from jax.experimental.pallas import tpu as pltpu
from jax.sharding import PartitionSpec as P

C = 512


def expand_and_project(ids, attended, weight):
    tok_rows = ids.shape[0]
    heads, _, e_width = attended.shape
    labels = lax.broadcasted_iota(jnp.int32, (heads, tok_rows, C), 2)
    onehot = (ids.T[:, :, None] == labels).astype(jnp.bfloat16)
    features = jnp.einsum("htc,hce->the", onehot, attended, preferred_element_type=jnp.float32).astype(
        jnp.bfloat16
    )
    flat = features.reshape(tok_rows, heads * e_width)
    return jnp.dot(flat, weight, preferred_element_type=jnp.float32).astype(jnp.bfloat16)


def by_reduction(queries, keys, values, cluster_ids, out_weight):
    tok_rows, head_count, e_width = queries.shape
    score_scale = 1.0 / math.sqrt(e_width)
    labels = lax.broadcasted_iota(jnp.int32, (head_count, tok_rows, C), 2)
    onehot = (cluster_ids.T[:, :, None] == labels).astype(jnp.bfloat16)
    totals = jnp.einsum("htc,the->hce", onehot, queries, preferred_element_type=jnp.float32)
    counts = jnp.sum(onehot, axis=1, dtype=jnp.float32)
    all_totals, all_counts = lax.psum((totals, counts), "seq")
    centroid = (all_totals / jnp.maximum(all_counts, 1.0)[:, :, None]).astype(jnp.bfloat16)
    scores = jnp.einsum("hce,the->hct", centroid, keys, preferred_element_type=jnp.float32) * score_scale
    local_max = jnp.max(scores, axis=2)
    weights = jnp.exp(scores - local_max[:, :, None])
    local_total = jnp.sum(weights, axis=2)
    local_out = jnp.einsum(
        "hct,the->hce", weights.astype(jnp.bfloat16), values, preferred_element_type=jnp.float32
    )
    global_max = lax.pmax(local_max, "seq")
    factor = jnp.exp(local_max - global_max)
    share_out = lax.psum_scatter(local_out * factor[:, :, None], "seq", scatter_dimension=1, tiled=True)
    share_total = lax.psum_scatter(local_total * factor, "seq", scatter_dimension=1, tiled=True)
    share_attended = (share_out / share_total[:, :, None]).astype(jnp.bfloat16)
    attended = lax.all_gather(share_attended, "seq", axis=1, tiled=True)
    attended = lax.all_gather(attended, "head", axis=0, tiled=True)
    ids = lax.all_gather(cluster_ids, "head", axis=1, tiled=True)
    weight = lax.all_gather(out_weight, "seq", axis=0, tiled=True)
    return expand_and_project(ids, attended, weight)


def attend_kernel(tok_rows, moved_ref, out_ref, sums_ref, scores_ref, acc_ref):
    n_src, _, e_width = moved_ref.shape
    lanes = e_width
    blocks = tok_rows // lanes
    scale = 1.0 / math.sqrt(e_width)
    cluster = lax.broadcasted_iota(jnp.int32, (C, lanes), 0)
    ones = jnp.ones((tok_rows, e_width), jnp.bfloat16)

    sums_ref[...] = jnp.zeros_like(sums_ref)

    @pl.loop(0, n_src, unroll=4)
    def _(src):
        coded = moved_ref[src, 3 * tok_rows :, :].astype(jnp.float32).astype(jnp.int32)
        parts = []
        for i in range(blocks):
            ids = coded[i : i + 1] * 16 + coded[blocks + i : blocks + i + 1]
            parts.append(jnp.where(cluster == ids, 1.0, 0.0).astype(jnp.bfloat16))
        onehot = jnp.concatenate(parts, axis=1)
        wide = jnp.concatenate([moved_ref[src, :tok_rows, :], ones], axis=1)
        sums_ref[...] += jnp.dot(onehot, wide, preferred_element_type=jnp.float32)

    centroid = (sums_ref[:, :e_width] / jnp.maximum(sums_ref[:, e_width:], 1.0)).astype(jnp.bfloat16)

    def score(src, top):
        keys = moved_ref[src, tok_rows : 2 * tok_rows, :]
        scores = lax.dot_general(centroid, keys, (((1,), (1,)), ((), ())), preferred_element_type=jnp.float32)
        scores_ref[src] = scores
        for i in range(blocks):
            top = jnp.maximum(top, scores[:, i * lanes : (i + 1) * lanes])
        return top

    top = lax.fori_loop(0, n_src, score, jnp.full((C, lanes), -jnp.inf, jnp.float32), unroll=4)
    top = jnp.broadcast_to(jnp.max(top, axis=1, keepdims=True), (C, tok_rows))

    acc_ref[...] = jnp.zeros_like(acc_ref)

    def weigh(src, total):
        weights = jnp.exp((scores_ref[src] - top) * scale)
        for i in range(blocks):
            total += weights[:, i * lanes : (i + 1) * lanes]
        values = moved_ref[src, 2 * tok_rows : 3 * tok_rows, :]
        acc_ref[...] += jnp.dot(weights.astype(jnp.bfloat16), values, preferred_element_type=jnp.float32)
        return total

    total = lax.fori_loop(0, n_src, weigh, jnp.zeros((C, lanes), jnp.float32), unroll=4)
    out_ref[...] = (acc_ref[...] / jnp.sum(total, axis=1, keepdims=True)).astype(jnp.bfloat16)


def attend(moved, tok_rows):
    n_src, _, e_width = moved.shape
    tokens = n_src * tok_rows
    return pl.pallas_call(
        lambda *refs: attend_kernel(tok_rows, *refs),
        out_shape=jax.ShapeDtypeStruct((C, e_width), jnp.bfloat16),
        in_specs=[pl.BlockSpec(memory_space=pltpu.VMEM)],
        out_specs=pl.BlockSpec(memory_space=pltpu.VMEM),
        scratch_shapes=[
            pltpu.VMEM((C, 2 * e_width), jnp.float32),
            pltpu.VMEM((n_src, C, tok_rows), jnp.float32),
            pltpu.VMEM((C, e_width), jnp.float32),
        ],
        compiler_params=pltpu.CompilerParams(vmem_limit_bytes=24 * 2**20),
        cost_estimate=pl.CostEstimate(
            flops=8 * C * tokens * e_width, bytes_accessed=moved.size * 2, transcendentals=C * tokens
        ),
        name="attend",
    )(moved)


def expand_kernel(ids_ref, attended_ref, *refs):
    out_ref = refs[-1]
    heads, clusters, e_width = attended_ref.shape
    tok_tile = ids_ref.shape[2]
    labels = lax.broadcasted_iota(jnp.int32, (tok_tile, e_width), 1).astype(jnp.int16)
    one, zero = jnp.bfloat16(1.0), jnp.bfloat16(0.0)
    columns = ids_ref[0].T
    for h in range(heads):
        ids = jnp.broadcast_to(columns[:, h : h + 1], (tok_tile, e_width)).astype(jnp.int16)
        parts = [jnp.where(ids == labels + jnp.int16(at), one, zero) for at in range(0, clusters, e_width)]
        onehot = jnp.concatenate(parts, axis=1)
        found = jnp.dot(onehot, attended_ref[h], preferred_element_type=jnp.float32)
        out_ref[h] = found.astype(jnp.bfloat16)


def expand(ids, part, attended, store, piece, pieces, tok_tile):
    _, heads, tokens = ids.shape
    _, clusters, e_width = attended.shape
    held = () if store is None else (store,)
    return pl.pallas_call(
        expand_kernel,
        out_shape=jax.ShapeDtypeStruct((pieces * heads, tokens, e_width), jnp.bfloat16),
        grid=(tokens // tok_tile,),
        in_specs=[
            pl.BlockSpec((1, heads, tok_tile), lambda i: (part, 0, i)),
            pl.BlockSpec((heads, clusters, e_width), lambda i: (0, 0, 0)),
        ]
        + [pl.BlockSpec(memory_space=pl.ANY) for _ in held],
        out_specs=pl.BlockSpec((heads, tok_tile, e_width), lambda i: (piece, i, 0)),
        input_output_aliases={2: 0} if held else {},
        compiler_params=pltpu.CompilerParams(vmem_limit_bytes=50 * 2**20),
        cost_estimate=pl.CostEstimate(
            flops=4 * tokens * heads * clusters * e_width,
            bytes_accessed=2 * heads * (clusters + tokens) * e_width,
            transcendentals=0,
        ),
        name="expand",
    )(ids, attended, *held)


def project_kernel(places_ref, features_ref, near_ref, *refs):
    *far_refs, out_ref = refs
    heads, _, e_width = features_ref.shape
    each = heads // 4
    head_at, core, half_at, place = (places_ref[i] for i in range(4))
    total = None
    for plane, weight_refs in ((half_at, (near_ref,)), (1 - half_at, far_refs)):
        base = jnp.where(plane == head_at, 0, 2 * each)
        blocks = [(x, i) for x in weight_refs for i in range(x.shape[0])]
        for k, (weight_ref, i) in enumerate(blocks):
            chip = jnp.bitwise_xor(place, k)
            slot = 2 * lax.rem(chip, each // 2) + jnp.bitwise_xor(half_at, lax.div(chip, each // 2))
            left = jnp.concatenate([features_ref[base + at * each + slot] for at in (core, 1 - core)], axis=1)
            right = weight_ref[i, : 2 * e_width, :]
            term = jnp.dot(left, right, preferred_element_type=jnp.float32)
            total = term if total is None else total + term
    out_ref[...] = total.astype(jnp.bfloat16)


def project(places, features, near, far, tok_tile):
    heads, tokens, e_width = features.shape
    cols = near.shape[2]
    return pl.pallas_call(
        project_kernel,
        out_shape=jax.ShapeDtypeStruct((tokens, cols), jnp.bfloat16),
        grid_spec=pltpu.PrefetchScalarGridSpec(
            num_scalar_prefetch=1,
            grid=(tokens // tok_tile,),
            in_specs=[
                pl.BlockSpec((heads, tok_tile, e_width), lambda i, _: (0, i, 0)),
                pl.BlockSpec(near.shape, lambda i, _: (0, 0, 0)),
            ]
            + [pl.BlockSpec(x.shape, lambda i, _: (0, 0, 0)) for x in far],
            out_specs=pl.BlockSpec((tok_tile, cols), lambda i, _: (i, 0)),
        ),
        compiler_params=pltpu.CompilerParams(vmem_limit_bytes=50 * 2**20),
        cost_estimate=pl.CostEstimate(
            flops=2 * tokens * heads * e_width * cols,
            bytes_accessed=2 * (features.size + heads * e_width * cols + tokens * cols),
            transcendentals=0,
        ),
        name="project",
    )(places, features, near, *far)


def by_slot(ids, half_at, core):
    sources, heads, tok_rows = ids.shape
    ids = ids.reshape(sources, 2, heads // 4, 2, tok_rows).transpose(3, 2, 1, 0, 4)
    ids = jnp.where(half_at == 0, ids, ids[:, :, ::-1])
    ids = jnp.where(core == 0, ids, ids[::-1])
    return ids.reshape(2, heads // 2, sources * tok_rows)


def by_head(queries, keys, values, cluster_ids, out_weight):
    tok_rows, head_count, e_width = queries.shape
    n_seq = lax.axis_size("seq")
    half = n_seq // 2
    rows, cols = out_weight.shape
    cols_each = cols // half
    seq_at = lax.axis_index("seq")
    head_at = lax.axis_index("head")
    half_at = seq_at // half
    core = lax.rem(seq_at, 2)
    place = lax.rem(seq_at, half)
    swap_heads = [(0, 1), (1, 0)]
    swap_halves = [(i, (i + half) % n_seq) for i in range(n_seq)]
    swap_cores = [(i, i ^ 1) for i in range(n_seq)]
    halves = [list(range(half)), list(range(half, n_seq))]
    same_core = [list(range(at + core_of, at + half, 2)) for at in (0, half) for core_of in range(2)]

    ids_t = cluster_ids.T
    high, low = (ids_t // 16).astype(jnp.bfloat16), (ids_t % 16).astype(jnp.bfloat16)
    id_rows = -(-2 * tok_rows // (16 * e_width)) * 16
    coded = jnp.concatenate([high, low], axis=1)
    coded = jnp.pad(coded, ((0, 0), (0, id_rows * e_width - 2 * tok_rows)))
    packed = jnp.concatenate(
        [x.transpose(1, 0, 2) for x in (queries, keys, values)] + [coded.reshape(head_count, id_rows, e_width)],
        axis=1,
    )
    packed, out_weight, high, low = lax.optimization_barrier((packed, out_weight, high, low))
    moved = lax.all_to_all(packed, "seq", split_axis=0, concat_axis=0, tiled=True)

    blocks = out_weight.reshape(rows, half, cols_each).transpose(1, 0, 2)
    coded = jnp.concatenate([high, low], axis=0)
    near = []
    for k in range(half):
        block = lax.dynamic_index_in_dim(blocks, jnp.bitwise_xor(place, k), 0, keepdims=False)
        block = jnp.concatenate([block, coded], axis=0)
        near.append(lax.ppermute(block, "seq", [(i, i ^ k) for i in range(n_seq)]) if k else block)
    near = jnp.stack(near)
    moved, near = lax.optimization_barrier((moved, near))
    cuts = [half * i // 8 for i in (0, 1, 3, 6, 8)]
    far = [lax.ppermute(near[a:b, :rows], "seq", swap_halves) for a, b in zip(cuts[:1], cuts[1:])]
    own = attend(moved, tok_rows)
    own, near, far[0] = lax.optimization_barrier((own, near, far[0]))
    far += [lax.ppermute(near[a:b, :rows], "seq", swap_halves) for a, b in zip(cuts[1:], cuts[2:])]

    def copied(pair):
        return jnp.broadcast_to(pair[None], (half // 2,) + pair.shape)

    def spread(copies):
        got = lax.all_to_all(
            copies, "seq", split_axis=0, concat_axis=0, axis_index_groups=same_core, tiled=True
        )
        return got.reshape((half,) + own.shape)

    pair = jnp.stack([own, lax.ppermute(own, "seq", swap_halves)])
    far_pair = lax.ppermute(pair, "head", swap_heads)
    first = spread(copied(pair))

    coded = near[:, rows:].astype(jnp.int32)
    coded = coded[:, :head_count] * 16 + coded[:, head_count:]
    coded = jnp.concatenate(
        [lax.dynamic_slice_in_dim(coded, jnp.bitwise_xor(place, i), 1, axis=0) for i in range(half)], axis=0
    )
    slot_ids = by_slot(coded, half_at, core)
    far_ids = lax.ppermute(slot_ids, "head", swap_heads)
    far_copies = copied(far_pair)
    first, slot_ids, far_ids, far_copies, far[1] = lax.optimization_barrier(
        (first, slot_ids, far_ids, far_copies, far[1])
    )
    second = lax.ppermute(first, "seq", swap_cores)
    third = spread(far_copies)

    pieces = 4
    tok_tile = 2 * tok_rows
    features = expand(slot_ids, 0, first, None, 0, pieces, tok_tile)
    features = expand(slot_ids, 1, second, features, 1, pieces, tok_tile)
    features, third, far[2] = lax.optimization_barrier((features, third, far[2]))
    fourth = lax.ppermute(third, "seq", swap_cores)
    features = expand(far_ids, 0, third, features, 2, pieces, tok_tile)
    features = expand(far_ids, 1, fourth, features, 3, pieces, tok_tile)
    places = jnp.stack([head_at, core, half_at, place]).astype(jnp.int32)
    near_out = project(places, features, near, far, tok_tile)
    mixed = lax.all_to_all(
        near_out.reshape(half, tok_rows, cols_each),
        "seq",
        split_axis=0,
        concat_axis=0,
        axis_index_groups=halves,
        tiled=True,
    )
    return mixed.transpose(1, 0, 2).reshape(tok_rows, cols)


def fits(queries, out_weight):
    n_seq = lax.axis_size("seq")
    tok_rows, head_count, e_width = queries.shape
    return (
        head_count == n_seq
        and lax.axis_size("head") == 2
        and n_seq >= 8
        and n_seq & (n_seq - 1) == 0
        and e_width == 128
        and tok_rows % e_width == 0
        and out_weight.shape[0] == 2 * e_width
        and out_weight.shape[1] == n_seq // 2 * tok_rows
        and out_weight.shape[1] % (n_seq // 2 * 128) == 0
    )


def on_device(queries, keys, values, cluster_ids, out_weight):
    if fits(queries, out_weight):
        return by_head(queries, keys, values, cluster_ids, out_weight)
    return by_reduction(queries, keys, values, cluster_ids, out_weight)


def solution(mesh):
    placed = (
        P("seq", "head", None),
        P("seq", "head", None),
        P("seq", "head", None),
        P("seq", "head"),
        P("seq", "head"),
    )
    return jax.shard_map(
        on_device, mesh=mesh, in_specs=placed, out_specs=P("seq", "head"), check_vma=False
    )
```

```python
import math

import jax
import jax.numpy as jnp
from jax import lax
from jax.experimental import pallas as pl
from jax.experimental.pallas import tpu as pltpu
from jax.sharding import PartitionSpec as P

C = 512


def expand_and_project(ids, attended, weight):
    tok_rows = ids.shape[0]
    heads, _, e_width = attended.shape
    labels = lax.broadcasted_iota(jnp.int32, (heads, tok_rows, C), 2)
    onehot = (ids.T[:, :, None] == labels).astype(jnp.bfloat16)
    features = jnp.einsum("htc,hce->the", onehot, attended, preferred_element_type=jnp.float32).astype(
        jnp.bfloat16
    )
    flat = features.reshape(tok_rows, heads * e_width)
    return jnp.dot(flat, weight, preferred_element_type=jnp.float32).astype(jnp.bfloat16)


def by_reduction(queries, keys, values, cluster_ids, out_weight):
    tok_rows, head_count, e_width = queries.shape
    score_scale = 1.0 / math.sqrt(e_width)
    labels = lax.broadcasted_iota(jnp.int32, (head_count, tok_rows, C), 2)
    onehot = (cluster_ids.T[:, :, None] == labels).astype(jnp.bfloat16)
    totals = jnp.einsum("htc,the->hce", onehot, queries, preferred_element_type=jnp.float32)
    counts = jnp.sum(onehot, axis=1, dtype=jnp.float32)
    all_totals, all_counts = lax.psum((totals, counts), "seq")
    centroid = (all_totals / jnp.maximum(all_counts, 1.0)[:, :, None]).astype(jnp.bfloat16)
    scores = jnp.einsum("hce,the->hct", centroid, keys, preferred_element_type=jnp.float32) * score_scale
    local_max = jnp.max(scores, axis=2)
    weights = jnp.exp(scores - local_max[:, :, None])
    local_total = jnp.sum(weights, axis=2)
    local_out = jnp.einsum(
        "hct,the->hce", weights.astype(jnp.bfloat16), values, preferred_element_type=jnp.float32
    )
    global_max = lax.pmax(local_max, "seq")
    factor = jnp.exp(local_max - global_max)
    share_out = lax.psum_scatter(local_out * factor[:, :, None], "seq", scatter_dimension=1, tiled=True)
    share_total = lax.psum_scatter(local_total * factor, "seq", scatter_dimension=1, tiled=True)
    share_attended = (share_out / share_total[:, :, None]).astype(jnp.bfloat16)
    attended = lax.all_gather(share_attended, "seq", axis=1, tiled=True)
    attended = lax.all_gather(attended, "head", axis=0, tiled=True)
    ids = lax.all_gather(cluster_ids, "head", axis=1, tiled=True)
    weight = lax.all_gather(out_weight, "seq", axis=0, tiled=True)
    return expand_and_project(ids, attended, weight)


def attend_kernel(tok_rows, moved_ref, out_ref, sums_ref, scores_ref, acc_ref):
    n_src, _, e_width = moved_ref.shape
    lanes = e_width
    blocks = tok_rows // lanes
    scale = 1.0 / math.sqrt(e_width)
    cluster = lax.broadcasted_iota(jnp.int32, (C, lanes), 0)
    ones = jnp.ones((tok_rows, e_width), jnp.bfloat16)

    sums_ref[...] = jnp.zeros_like(sums_ref)

    @pl.loop(0, n_src, unroll=8)
    def _(src):
        coded = moved_ref[src, 3 * tok_rows :, :].astype(jnp.float32).astype(jnp.int32)
        parts = []
        for i in range(blocks):
            ids = coded[i : i + 1] * 16 + coded[blocks + i : blocks + i + 1]
            parts.append(jnp.where(cluster == ids, 1.0, 0.0).astype(jnp.bfloat16))
        onehot = jnp.concatenate(parts, axis=1)
        wide = jnp.concatenate([moved_ref[src, :tok_rows, :], ones], axis=1)
        sums_ref[...] += jnp.dot(onehot, wide, preferred_element_type=jnp.float32)

    centroid = (sums_ref[:, :e_width] / jnp.maximum(sums_ref[:, e_width:], 1.0)).astype(jnp.bfloat16)

    def score(src, top):
        keys = moved_ref[src, tok_rows : 2 * tok_rows, :]
        scores = lax.dot_general(centroid, keys, (((1,), (1,)), ((), ())), preferred_element_type=jnp.float32)
        scores_ref[src] = scores
        for i in range(blocks):
            top = jnp.maximum(top, scores[:, i * lanes : (i + 1) * lanes])
        return top

    top = lax.fori_loop(0, n_src, score, jnp.full((C, lanes), -jnp.inf, jnp.float32), unroll=8)
    top = jnp.broadcast_to(jnp.max(top, axis=1, keepdims=True), (C, tok_rows))

    acc_ref[...] = jnp.zeros_like(acc_ref)

    def weigh(src, total):
        weights = jnp.exp((scores_ref[src] - top) * scale)
        for i in range(blocks):
            total += weights[:, i * lanes : (i + 1) * lanes]
        values = moved_ref[src, 2 * tok_rows : 3 * tok_rows, :]
        acc_ref[...] += jnp.dot(weights.astype(jnp.bfloat16), values, preferred_element_type=jnp.float32)
        return total

    total = lax.fori_loop(0, n_src, weigh, jnp.zeros((C, lanes), jnp.float32), unroll=8)
    out_ref[...] = (acc_ref[...] / jnp.sum(total, axis=1, keepdims=True)).astype(jnp.bfloat16)


def attend(moved, tok_rows):
    n_src, _, e_width = moved.shape
    tokens = n_src * tok_rows
    return pl.pallas_call(
        lambda *refs: attend_kernel(tok_rows, *refs),
        out_shape=jax.ShapeDtypeStruct((C, e_width), jnp.bfloat16),
        in_specs=[pl.BlockSpec(memory_space=pltpu.VMEM)],
        out_specs=pl.BlockSpec(memory_space=pltpu.VMEM),
        scratch_shapes=[
            pltpu.VMEM((C, 2 * e_width), jnp.float32),
            pltpu.VMEM((n_src, C, tok_rows), jnp.float32),
            pltpu.VMEM((C, e_width), jnp.float32),
        ],
        compiler_params=pltpu.CompilerParams(vmem_limit_bytes=24 * 2**20),
        cost_estimate=pl.CostEstimate(
            flops=8 * C * tokens * e_width, bytes_accessed=moved.size * 2, transcendentals=C * tokens
        ),
        name="attend",
    )(moved)


def expand_kernel(ids_ref, attended_ref, *refs):
    out_ref = refs[-1]
    heads, clusters, e_width = attended_ref.shape
    tok_tile = ids_ref.shape[2]
    labels = lax.broadcasted_iota(jnp.int32, (tok_tile, e_width), 1).astype(jnp.int16)
    one, zero = jnp.bfloat16(1.0), jnp.bfloat16(0.0)
    columns = ids_ref[0].T
    for h in range(heads):
        ids = jnp.broadcast_to(columns[:, h : h + 1], (tok_tile, e_width)).astype(jnp.int16)
        parts = [jnp.where(ids == labels + jnp.int16(at), one, zero) for at in range(0, clusters, e_width)]
        onehot = jnp.concatenate(parts, axis=1)
        found = jnp.dot(onehot, attended_ref[h], preferred_element_type=jnp.float32)
        out_ref[h] = found.astype(jnp.bfloat16)


def expand(ids, part, attended, store, piece, pieces, tok_tile):
    _, heads, tokens = ids.shape
    _, clusters, e_width = attended.shape
    held = () if store is None else (store,)
    return pl.pallas_call(
        expand_kernel,
        out_shape=jax.ShapeDtypeStruct((pieces * heads, tokens, e_width), jnp.bfloat16),
        grid=(tokens // tok_tile,),
        in_specs=[
            pl.BlockSpec((1, heads, tok_tile), lambda i: (part, 0, i)),
            pl.BlockSpec((heads, clusters, e_width), lambda i: (0, 0, 0)),
        ]
        + [pl.BlockSpec(memory_space=pl.ANY) for _ in held],
        out_specs=pl.BlockSpec((heads, tok_tile, e_width), lambda i: (piece, i, 0)),
        input_output_aliases={2: 0} if held else {},
        compiler_params=pltpu.CompilerParams(vmem_limit_bytes=50 * 2**20),
        cost_estimate=pl.CostEstimate(
            flops=4 * tokens * heads * clusters * e_width,
            bytes_accessed=2 * heads * (clusters + tokens) * e_width,
            transcendentals=0,
        ),
        name="expand",
    )(ids, attended, *held)


def project_kernel(places_ref, features_ref, near_ref, *refs):
    *far_refs, out_ref = refs
    heads, _, e_width = features_ref.shape
    each = heads // 4
    head_at, core, half_at, place = (places_ref[i] for i in range(4))
    total = None
    for plane, weight_refs in ((half_at, (near_ref,)), (1 - half_at, far_refs)):
        base = jnp.where(plane == head_at, 0, 2 * each)
        blocks = [(x, i) for x in weight_refs for i in range(x.shape[0])]
        for k, (weight_ref, i) in enumerate(blocks):
            chip = jnp.bitwise_xor(place, k)
            slot = 2 * lax.rem(chip, each // 2) + jnp.bitwise_xor(half_at, lax.div(chip, each // 2))
            left = jnp.concatenate([features_ref[base + at * each + slot] for at in (core, 1 - core)], axis=1)
            right = weight_ref[i, : 2 * e_width, :]
            term = jnp.dot(left, right, preferred_element_type=jnp.float32)
            total = term if total is None else total + term
    out_ref[...] = total.astype(jnp.bfloat16)


def project(places, features, near, far, tok_tile):
    heads, tokens, e_width = features.shape
    cols = near.shape[2]
    return pl.pallas_call(
        project_kernel,
        out_shape=jax.ShapeDtypeStruct((tokens, cols), jnp.bfloat16),
        grid_spec=pltpu.PrefetchScalarGridSpec(
            num_scalar_prefetch=1,
            grid=(tokens // tok_tile,),
            in_specs=[
                pl.BlockSpec((heads, tok_tile, e_width), lambda i, _: (0, i, 0)),
                pl.BlockSpec(near.shape, lambda i, _: (0, 0, 0)),
            ]
            + [pl.BlockSpec(x.shape, lambda i, _: (0, 0, 0)) for x in far],
            out_specs=pl.BlockSpec((tok_tile, cols), lambda i, _: (i, 0)),
        ),
        compiler_params=pltpu.CompilerParams(vmem_limit_bytes=50 * 2**20),
        cost_estimate=pl.CostEstimate(
            flops=2 * tokens * heads * e_width * cols,
            bytes_accessed=2 * (features.size + heads * e_width * cols + tokens * cols),
            transcendentals=0,
        ),
        name="project",
    )(places, features, near, *far)


def by_slot(ids, half_at, core):
    sources, heads, tok_rows = ids.shape
    ids = ids.reshape(sources, 2, heads // 4, 2, tok_rows).transpose(3, 2, 1, 0, 4)
    ids = jnp.where(half_at == 0, ids, ids[:, :, ::-1])
    ids = jnp.where(core == 0, ids, ids[::-1])
    return ids.reshape(2, heads // 2, sources * tok_rows)


def by_head(queries, keys, values, cluster_ids, out_weight):
    tok_rows, head_count, e_width = queries.shape
    n_seq = lax.axis_size("seq")
    half = n_seq // 2
    rows, cols = out_weight.shape
    cols_each = cols // half
    seq_at = lax.axis_index("seq")
    head_at = lax.axis_index("head")
    half_at = seq_at // half
    core = lax.rem(seq_at, 2)
    place = lax.rem(seq_at, half)
    swap_heads = [(0, 1), (1, 0)]
    swap_halves = [(i, (i + half) % n_seq) for i in range(n_seq)]
    swap_cores = [(i, i ^ 1) for i in range(n_seq)]
    halves = [list(range(half)), list(range(half, n_seq))]
    same_core = [list(range(at + core_of, at + half, 2)) for at in (0, half) for core_of in range(2)]

    ids_t = cluster_ids.T
    high, low = (ids_t // 16).astype(jnp.bfloat16), (ids_t % 16).astype(jnp.bfloat16)
    id_rows = -(-2 * tok_rows // (16 * e_width)) * 16
    coded = jnp.concatenate([high, low], axis=1)
    coded = jnp.pad(coded, ((0, 0), (0, id_rows * e_width - 2 * tok_rows)))
    packed = jnp.concatenate(
        [x.transpose(1, 0, 2) for x in (queries, keys, values)] + [coded.reshape(head_count, id_rows, e_width)],
        axis=1,
    )
    packed, out_weight, high, low = lax.optimization_barrier((packed, out_weight, high, low))
    moved = lax.all_to_all(packed, "seq", split_axis=0, concat_axis=0, tiled=True)

    blocks = out_weight.reshape(rows, half, cols_each).transpose(1, 0, 2)
    coded = jnp.concatenate([high, low], axis=0)
    near = []
    for k in range(half):
        block = lax.dynamic_index_in_dim(blocks, jnp.bitwise_xor(place, k), 0, keepdims=False)
        block = jnp.concatenate([block, coded], axis=0)
        near.append(lax.ppermute(block, "seq", [(i, i ^ k) for i in range(n_seq)]) if k else block)
    near = jnp.stack(near)
    moved, near = lax.optimization_barrier((moved, near))
    cuts = [half * i // 8 for i in (0, 3, 6, 8)]
    own = attend(moved, tok_rows)
    own, near = lax.optimization_barrier((own, near))
    far = [lax.ppermute(near[a:b, :rows], "seq", swap_halves) for a, b in zip(cuts, cuts[1:])]

    def copied(pair):
        return jnp.broadcast_to(pair[None], (half // 2,) + pair.shape)

    def spread(copies):
        got = lax.all_to_all(
            copies, "seq", split_axis=0, concat_axis=0, axis_index_groups=same_core, tiled=True
        )
        return got.reshape((half,) + own.shape)

    pair = jnp.stack([own, lax.ppermute(own, "seq", swap_halves)])
    first = spread(copied(pair))

    coded = near[:, rows:].astype(jnp.int32)
    coded = coded[:, :head_count] * 16 + coded[:, head_count:]
    coded = jnp.concatenate(
        [lax.dynamic_slice_in_dim(coded, jnp.bitwise_xor(place, i), 1, axis=0) for i in range(half)], axis=0
    )
    slot_ids = by_slot(coded, half_at, core)
    far_ids = lax.ppermute(slot_ids, "head", swap_heads)
    first, slot_ids, far_ids, far[0] = lax.optimization_barrier((first, slot_ids, far_ids, far[0]))
    second = lax.ppermute(first, "seq", swap_cores)
    third = lax.ppermute(first, "head", swap_heads)

    pieces = 4
    tok_tile = 2 * tok_rows
    features = expand(slot_ids, 0, first, None, 0, pieces, tok_tile)
    features = expand(slot_ids, 1, second, features, 1, pieces, tok_tile)
    features, third, far[1] = lax.optimization_barrier((features, third, far[1]))
    fourth = lax.ppermute(third, "seq", swap_cores)
    features = expand(far_ids, 0, third, features, 2, pieces, tok_tile)
    features = expand(far_ids, 1, fourth, features, 3, pieces, tok_tile)
    places = jnp.stack([head_at, core, half_at, place]).astype(jnp.int32)
    near_out = project(places, features, near, far, tok_tile)
    mixed = lax.all_to_all(
        near_out.reshape(half, tok_rows, cols_each),
        "seq",
        split_axis=0,
        concat_axis=0,
        axis_index_groups=halves,
        tiled=True,
    )
    return mixed.transpose(1, 0, 2).reshape(tok_rows, cols)


def fits(queries, out_weight):
    n_seq = lax.axis_size("seq")
    tok_rows, head_count, e_width = queries.shape
    return (
        head_count == n_seq
        and lax.axis_size("head") == 2
        and n_seq >= 8
        and n_seq & (n_seq - 1) == 0
        and e_width == 128
        and tok_rows % e_width == 0
        and out_weight.shape[0] == 2 * e_width
        and out_weight.shape[1] == n_seq // 2 * tok_rows
        and out_weight.shape[1] % (n_seq // 2 * 128) == 0
    )


def on_device(queries, keys, values, cluster_ids, out_weight):
    if fits(queries, out_weight):
        return by_head(queries, keys, values, cluster_ids, out_weight)
    return by_reduction(queries, keys, values, cluster_ids, out_weight)


def solution(mesh):
    placed = (
        P("seq", "head", None),
        P("seq", "head", None),
        P("seq", "head", None),
        P("seq", "head"),
        P("seq", "head"),
    )
    return jax.shard_map(
        on_device, mesh=mesh, in_specs=placed, out_specs=P("seq", "head"), check_vma=False
    )
```

```python
import math

import jax
import jax.numpy as jnp
from jax import lax
from jax.experimental import pallas as pl
from jax.experimental.pallas import tpu as pltpu
from jax.sharding import PartitionSpec as P

C = 512


def expand_and_project(ids, attended, weight):
    tok_rows = ids.shape[0]
    heads, _, e_width = attended.shape
    labels = lax.broadcasted_iota(jnp.int32, (heads, tok_rows, C), 2)
    onehot = (ids.T[:, :, None] == labels).astype(jnp.bfloat16)
    features = jnp.einsum("htc,hce->the", onehot, attended, preferred_element_type=jnp.float32).astype(
        jnp.bfloat16
    )
    flat = features.reshape(tok_rows, heads * e_width)
    return jnp.dot(flat, weight, preferred_element_type=jnp.float32).astype(jnp.bfloat16)


def by_reduction(queries, keys, values, cluster_ids, out_weight):
    tok_rows, head_count, e_width = queries.shape
    score_scale = 1.0 / math.sqrt(e_width)
    labels = lax.broadcasted_iota(jnp.int32, (head_count, tok_rows, C), 2)
    onehot = (cluster_ids.T[:, :, None] == labels).astype(jnp.bfloat16)
    totals = jnp.einsum("htc,the->hce", onehot, queries, preferred_element_type=jnp.float32)
    counts = jnp.sum(onehot, axis=1, dtype=jnp.float32)
    all_totals, all_counts = lax.psum((totals, counts), "seq")
    centroid = (all_totals / jnp.maximum(all_counts, 1.0)[:, :, None]).astype(jnp.bfloat16)
    scores = jnp.einsum("hce,the->hct", centroid, keys, preferred_element_type=jnp.float32) * score_scale
    local_max = jnp.max(scores, axis=2)
    weights = jnp.exp(scores - local_max[:, :, None])
    local_total = jnp.sum(weights, axis=2)
    local_out = jnp.einsum(
        "hct,the->hce", weights.astype(jnp.bfloat16), values, preferred_element_type=jnp.float32
    )
    global_max = lax.pmax(local_max, "seq")
    factor = jnp.exp(local_max - global_max)
    share_out = lax.psum_scatter(local_out * factor[:, :, None], "seq", scatter_dimension=1, tiled=True)
    share_total = lax.psum_scatter(local_total * factor, "seq", scatter_dimension=1, tiled=True)
    share_attended = (share_out / share_total[:, :, None]).astype(jnp.bfloat16)
    attended = lax.all_gather(share_attended, "seq", axis=1, tiled=True)
    attended = lax.all_gather(attended, "head", axis=0, tiled=True)
    ids = lax.all_gather(cluster_ids, "head", axis=1, tiled=True)
    weight = lax.all_gather(out_weight, "seq", axis=0, tiled=True)
    return expand_and_project(ids, attended, weight)


def attend_kernel(tok_rows, moved_ref, out_ref, sums_ref, scores_ref, acc_ref):
    n_src, _, e_width = moved_ref.shape
    lanes = e_width
    blocks = tok_rows // lanes
    scale = 1.0 / math.sqrt(e_width)
    cluster = lax.broadcasted_iota(jnp.int32, (C, lanes), 0)
    ones = jnp.ones((tok_rows, e_width), jnp.bfloat16)

    sums_ref[...] = jnp.zeros_like(sums_ref)

    @pl.loop(0, n_src, unroll=8)
    def _(src):
        coded = moved_ref[src, 3 * tok_rows :, :].astype(jnp.float32).astype(jnp.int32)
        parts = []
        for i in range(blocks):
            ids = coded[i : i + 1] * 16 + coded[blocks + i : blocks + i + 1]
            parts.append(jnp.where(cluster == ids, 1.0, 0.0).astype(jnp.bfloat16))
        onehot = jnp.concatenate(parts, axis=1)
        wide = jnp.concatenate([moved_ref[src, :tok_rows, :], ones], axis=1)
        sums_ref[...] += jnp.dot(onehot, wide, preferred_element_type=jnp.float32)

    centroid = (sums_ref[:, :e_width] / jnp.maximum(sums_ref[:, e_width:], 1.0)).astype(jnp.bfloat16)

    def score(src, top):
        keys = moved_ref[src, tok_rows : 2 * tok_rows, :]
        scores = lax.dot_general(centroid, keys, (((1,), (1,)), ((), ())), preferred_element_type=jnp.float32)
        scores_ref[src] = scores
        for i in range(blocks):
            top = jnp.maximum(top, scores[:, i * lanes : (i + 1) * lanes])
        return top

    top = lax.fori_loop(0, n_src, score, jnp.full((C, lanes), -jnp.inf, jnp.float32), unroll=8)
    top = jnp.broadcast_to(jnp.max(top, axis=1, keepdims=True), (C, tok_rows))

    acc_ref[...] = jnp.zeros_like(acc_ref)

    def weigh(src, total):
        weights = jnp.exp((scores_ref[src] - top) * scale)
        for i in range(blocks):
            total += weights[:, i * lanes : (i + 1) * lanes]
        values = moved_ref[src, 2 * tok_rows : 3 * tok_rows, :]
        acc_ref[...] += jnp.dot(weights.astype(jnp.bfloat16), values, preferred_element_type=jnp.float32)
        return total

    total = lax.fori_loop(0, n_src, weigh, jnp.zeros((C, lanes), jnp.float32), unroll=8)
    out_ref[...] = (acc_ref[...] / jnp.sum(total, axis=1, keepdims=True)).astype(jnp.bfloat16)


def attend(moved, tok_rows):
    n_src, _, e_width = moved.shape
    tokens = n_src * tok_rows
    return pl.pallas_call(
        lambda *refs: attend_kernel(tok_rows, *refs),
        out_shape=jax.ShapeDtypeStruct((C, e_width), jnp.bfloat16),
        in_specs=[pl.BlockSpec(memory_space=pltpu.VMEM)],
        out_specs=pl.BlockSpec(memory_space=pltpu.VMEM),
        scratch_shapes=[
            pltpu.VMEM((C, 2 * e_width), jnp.float32),
            pltpu.VMEM((n_src, C, tok_rows), jnp.float32),
            pltpu.VMEM((C, e_width), jnp.float32),
        ],
        compiler_params=pltpu.CompilerParams(vmem_limit_bytes=24 * 2**20),
        cost_estimate=pl.CostEstimate(
            flops=8 * C * tokens * e_width, bytes_accessed=moved.size * 2, transcendentals=C * tokens
        ),
        name="attend",
    )(moved)


def expand_kernel(offset, order, ids_ref, attended_ref, *refs):
    out_ref = refs[-1]
    heads, clusters, e_width = attended_ref.shape
    tok_tile = ids_ref.shape[2]
    labels = lax.broadcasted_iota(jnp.int32, (tok_tile, e_width), 1).astype(jnp.int16)
    one, zero = jnp.bfloat16(1.0), jnp.bfloat16(0.0)
    columns = ids_ref[0].T
    for h in range(heads):
        ids = jnp.broadcast_to(columns[:, offset + h : offset + h + 1], (tok_tile, e_width)).astype(jnp.int16)
        parts = [jnp.where(ids == labels + jnp.int16(at), one, zero) for at in range(0, clusters, e_width)]
        onehot = jnp.concatenate(parts, axis=1)
        found = jnp.dot(onehot, attended_ref[order[h]], preferred_element_type=jnp.float32)
        out_ref[h] = found.astype(jnp.bfloat16)


def expand(ids, part, offset, attended, order, store, slot, slots, tok_tile):
    _, rows, tokens = ids.shape
    heads, clusters, e_width = attended.shape
    held = () if store is None else (store,)
    return pl.pallas_call(
        lambda *refs: expand_kernel(offset, order, *refs),
        out_shape=jax.ShapeDtypeStruct((slots, tokens, e_width), jnp.bfloat16),
        grid=(tokens // tok_tile,),
        in_specs=[
            pl.BlockSpec((1, rows, tok_tile), lambda i: (part, 0, i)),
            pl.BlockSpec((heads, clusters, e_width), lambda i: (0, 0, 0)),
        ]
        + [pl.BlockSpec(memory_space=pl.ANY) for _ in held],
        out_specs=pl.BlockSpec((heads, tok_tile, e_width), lambda i: (slot // heads, i, 0)),
        input_output_aliases={2: 0} if held else {},
        compiler_params=pltpu.CompilerParams(vmem_limit_bytes=50 * 2**20),
        cost_estimate=pl.CostEstimate(
            flops=4 * tokens * heads * clusters * e_width,
            bytes_accessed=2 * heads * (clusters + tokens) * e_width,
            transcendentals=0,
        ),
        name="expand",
    )(ids, attended, *held)


def project_kernel(places_ref, features_ref, near_ref, *refs):
    *far_refs, out_ref = refs
    heads, _, e_width = features_ref.shape
    each = heads // 4
    head_at, core, half_at, place = (places_ref[i] for i in range(4))
    total = None
    for plane, weight_refs in ((half_at, (near_ref,)), (1 - half_at, far_refs)):
        base = jnp.where(plane == head_at, 0, 2 * each)
        blocks = [(x, i) for x in weight_refs for i in range(x.shape[0])]
        for k, (weight_ref, i) in enumerate(blocks):
            chip = jnp.bitwise_xor(place, k)
            slot = lax.rem(chip, each // 2) + each // 2 * jnp.bitwise_xor(half_at, lax.div(chip, each // 2))
            left = jnp.concatenate([features_ref[base + at * each + slot] for at in (core, 1 - core)], axis=1)
            right = weight_ref[i, : 2 * e_width, :]
            term = jnp.dot(left, right, preferred_element_type=jnp.float32)
            total = term if total is None else total + term
    out_ref[...] = total.astype(jnp.bfloat16)


def project(places, features, near, far, tok_tile):
    heads, tokens, e_width = features.shape
    cols = near.shape[2]
    return pl.pallas_call(
        project_kernel,
        out_shape=jax.ShapeDtypeStruct((tokens, cols), jnp.bfloat16),
        grid_spec=pltpu.PrefetchScalarGridSpec(
            num_scalar_prefetch=1,
            grid=(tokens // tok_tile,),
            in_specs=[
                pl.BlockSpec((heads, tok_tile, e_width), lambda i, _: (0, i, 0)),
                pl.BlockSpec(near.shape, lambda i, _: (0, 0, 0)),
            ]
            + [pl.BlockSpec(x.shape, lambda i, _: (0, 0, 0)) for x in far],
            out_specs=pl.BlockSpec((tok_tile, cols), lambda i, _: (i, 0)),
        ),
        compiler_params=pltpu.CompilerParams(vmem_limit_bytes=50 * 2**20),
        cost_estimate=pl.CostEstimate(
            flops=2 * tokens * heads * e_width * cols,
            bytes_accessed=2 * (features.size + heads * e_width * cols + tokens * cols),
            transcendentals=0,
        ),
        name="project",
    )(places, features, near, *far)


def by_slot(ids, half_at, core):
    sources, heads, tok_rows = ids.shape
    ids = ids.reshape(sources, 2, heads // 4, 2, tok_rows).transpose(3, 1, 2, 0, 4)
    ids = jnp.where(half_at == 0, ids, ids[:, ::-1])
    ids = jnp.where(core == 0, ids, ids[::-1])
    return ids.reshape(2, heads // 2, sources * tok_rows)


def by_head(queries, keys, values, cluster_ids, out_weight):
    tok_rows, head_count, e_width = queries.shape
    n_seq = lax.axis_size("seq")
    half = n_seq // 2
    rows, cols = out_weight.shape
    cols_each = cols // half
    seq_at = lax.axis_index("seq")
    head_at = lax.axis_index("head")
    half_at = seq_at // half
    core = lax.rem(seq_at, 2)
    place = lax.rem(seq_at, half)
    swap_heads = [(0, 1), (1, 0)]
    swap_halves = [(i, (i + half) % n_seq) for i in range(n_seq)]
    swap_cores = [(i, i ^ 1) for i in range(n_seq)]
    halves = [list(range(half)), list(range(half, n_seq))]
    same_core = [list(range(at + core_of, at + half, 2)) for at in (0, half) for core_of in range(2)]

    ids_t = cluster_ids.T
    high, low = (ids_t // 16).astype(jnp.bfloat16), (ids_t % 16).astype(jnp.bfloat16)
    id_rows = -(-2 * tok_rows // (16 * e_width)) * 16
    coded = jnp.concatenate([high, low], axis=1)
    coded = jnp.pad(coded, ((0, 0), (0, id_rows * e_width - 2 * tok_rows)))
    packed = jnp.concatenate(
        [x.transpose(1, 0, 2) for x in (queries, keys, values)] + [coded.reshape(head_count, id_rows, e_width)],
        axis=1,
    )
    packed, out_weight, high, low = lax.optimization_barrier((packed, out_weight, high, low))
    moved = lax.all_to_all(packed, "seq", split_axis=0, concat_axis=0, tiled=True)

    blocks = out_weight.reshape(rows, half, cols_each).transpose(1, 0, 2)
    coded = jnp.concatenate([high, low], axis=0)
    near = []
    for k in range(half):
        block = lax.dynamic_index_in_dim(blocks, jnp.bitwise_xor(place, k), 0, keepdims=False)
        block = jnp.concatenate([block, coded], axis=0)
        near.append(lax.ppermute(block, "seq", [(i, i ^ k) for i in range(n_seq)]) if k else block)
    near = jnp.stack(near)
    moved, near = lax.optimization_barrier((moved, near))
    cuts = [half * i // 8 for i in (0, 1, 3, 6, 8)]
    far = [lax.ppermute(near[a:b, :rows], "seq", swap_halves) for a, b in zip(cuts[:1], cuts[1:])]
    own = attend(moved, tok_rows)
    own, near, far[0] = lax.optimization_barrier((own, near, far[0]))
    far += [lax.ppermute(near[a:b, :rows], "seq", swap_halves) for a, b in zip(cuts[1:], cuts[2:])]

    def copied(pair):
        return jnp.broadcast_to(pair[None], (half // 2,) + pair.shape)

    def spread(copies):
        got = lax.all_to_all(
            copies, "seq", split_axis=0, concat_axis=0, axis_index_groups=same_core, tiled=True
        )
        return got.reshape((-1,) + own.shape)

    crossed = lax.ppermute(own, "seq", swap_halves)
    pair = jnp.stack([own, crossed])
    far_pair = lax.ppermute(pair, "head", swap_heads)
    first = spread(copied(own))

    coded = near[:, rows:].astype(jnp.int32)
    coded = coded[:, :head_count] * 16 + coded[:, head_count:]
    coded = jnp.concatenate(
        [lax.dynamic_slice_in_dim(coded, jnp.bitwise_xor(place, i), 1, axis=0) for i in range(half)], axis=0
    )
    slot_ids = by_slot(coded, half_at, core)
    far_ids = lax.ppermute(slot_ids, "head", swap_heads)
    first, slot_ids, crossed = lax.optimization_barrier((first, slot_ids, crossed))
    other_first = spread(copied(crossed))
    second = lax.ppermute(first, "seq", swap_cores)

    share = half // 2
    slots = 4 * half
    tok_tile = 2 * tok_rows
    alone = list(range(share))
    paired = [2 * (i % share) + i // share for i in range(half)]
    features = expand(slot_ids, 0, 0, first, alone, None, 0, slots, tok_tile)
    features = expand(slot_ids, 1, 0, second, alone, features, half, slots, tok_tile)
    far_copies = copied(far_pair)
    features, other_first, far_ids, far_copies, far[1] = lax.optimization_barrier(
        (features, other_first, far_ids, far_copies, far[1])
    )
    other_second = lax.ppermute(other_first, "seq", swap_cores)
    third = spread(far_copies)
    features = expand(slot_ids, 0, share, other_first, alone, features, share, slots, tok_tile)
    features = expand(slot_ids, 1, share, other_second, alone, features, half + share, slots, tok_tile)
    features, third, far[2] = lax.optimization_barrier((features, third, far[2]))
    fourth = lax.ppermute(third, "seq", swap_cores)
    features = expand(far_ids, 0, 0, third, paired, features, 2 * half, slots, tok_tile)
    features = expand(far_ids, 1, 0, fourth, paired, features, 3 * half, slots, tok_tile)
    places = jnp.stack([head_at, core, half_at, place]).astype(jnp.int32)
    near_out = project(places, features, near, far, tok_tile)
    mixed = lax.all_to_all(
        near_out.reshape(half, tok_rows, cols_each),
        "seq",
        split_axis=0,
        concat_axis=0,
        axis_index_groups=halves,
        tiled=True,
    )
    return mixed.transpose(1, 0, 2).reshape(tok_rows, cols)


def fits(queries, out_weight):
    n_seq = lax.axis_size("seq")
    tok_rows, head_count, e_width = queries.shape
    return (
        head_count == n_seq
        and lax.axis_size("head") == 2
        and n_seq >= 8
        and n_seq & (n_seq - 1) == 0
        and e_width == 128
        and tok_rows % e_width == 0
        and out_weight.shape[0] == 2 * e_width
        and out_weight.shape[1] == n_seq // 2 * tok_rows
        and out_weight.shape[1] % (n_seq // 2 * 128) == 0
    )


def on_device(queries, keys, values, cluster_ids, out_weight):
    if fits(queries, out_weight):
        return by_head(queries, keys, values, cluster_ids, out_weight)
    return by_reduction(queries, keys, values, cluster_ids, out_weight)


def solution(mesh):
    placed = (
        P("seq", "head", None),
        P("seq", "head", None),
        P("seq", "head", None),
        P("seq", "head"),
        P("seq", "head"),
    )
    return jax.shard_map(
        on_device, mesh=mesh, in_specs=placed, out_specs=P("seq", "head"), check_vma=False
    )
```

```python
import math

import jax
import jax.numpy as jnp
from jax import lax
from jax.experimental import pallas as pl
from jax.experimental.pallas import tpu as pltpu
from jax.sharding import PartitionSpec as P

C = 512


def expand_and_project(ids, attended, weight):
    tok_rows = ids.shape[0]
    heads, _, e_width = attended.shape
    labels = lax.broadcasted_iota(jnp.int32, (heads, tok_rows, C), 2)
    onehot = (ids.T[:, :, None] == labels).astype(jnp.bfloat16)
    features = jnp.einsum("htc,hce->the", onehot, attended, preferred_element_type=jnp.float32).astype(
        jnp.bfloat16
    )
    flat = features.reshape(tok_rows, heads * e_width)
    return jnp.dot(flat, weight, preferred_element_type=jnp.float32).astype(jnp.bfloat16)


def by_reduction(queries, keys, values, cluster_ids, out_weight):
    tok_rows, head_count, e_width = queries.shape
    score_scale = 1.0 / math.sqrt(e_width)
    labels = lax.broadcasted_iota(jnp.int32, (head_count, tok_rows, C), 2)
    onehot = (cluster_ids.T[:, :, None] == labels).astype(jnp.bfloat16)
    totals = jnp.einsum("htc,the->hce", onehot, queries, preferred_element_type=jnp.float32)
    counts = jnp.sum(onehot, axis=1, dtype=jnp.float32)
    all_totals, all_counts = lax.psum((totals, counts), "seq")
    centroid = (all_totals / jnp.maximum(all_counts, 1.0)[:, :, None]).astype(jnp.bfloat16)
    scores = jnp.einsum("hce,the->hct", centroid, keys, preferred_element_type=jnp.float32) * score_scale
    local_max = jnp.max(scores, axis=2)
    weights = jnp.exp(scores - local_max[:, :, None])
    local_total = jnp.sum(weights, axis=2)
    local_out = jnp.einsum(
        "hct,the->hce", weights.astype(jnp.bfloat16), values, preferred_element_type=jnp.float32
    )
    global_max = lax.pmax(local_max, "seq")
    factor = jnp.exp(local_max - global_max)
    share_out = lax.psum_scatter(local_out * factor[:, :, None], "seq", scatter_dimension=1, tiled=True)
    share_total = lax.psum_scatter(local_total * factor, "seq", scatter_dimension=1, tiled=True)
    share_attended = (share_out / share_total[:, :, None]).astype(jnp.bfloat16)
    attended = lax.all_gather(share_attended, "seq", axis=1, tiled=True)
    attended = lax.all_gather(attended, "head", axis=0, tiled=True)
    ids = lax.all_gather(cluster_ids, "head", axis=1, tiled=True)
    weight = lax.all_gather(out_weight, "seq", axis=0, tiled=True)
    return expand_and_project(ids, attended, weight)


def attend_kernel(tok_rows, moved_ref, out_ref, sums_ref, scores_ref, acc_ref):
    n_src, _, e_width = moved_ref.shape
    lanes = e_width
    blocks = tok_rows // lanes
    scale = 1.0 / math.sqrt(e_width)
    cluster = lax.broadcasted_iota(jnp.int32, (C, lanes), 0)
    ones = jnp.ones((tok_rows, e_width), jnp.bfloat16)

    sums_ref[...] = jnp.zeros_like(sums_ref)

    @pl.loop(0, n_src, unroll=8)
    def _(src):
        coded = moved_ref[src, 3 * tok_rows :, :].astype(jnp.float32).astype(jnp.int32)
        parts = []
        for i in range(blocks):
            ids = coded[i : i + 1] * 16 + coded[blocks + i : blocks + i + 1]
            parts.append(jnp.where(cluster == ids, 1.0, 0.0).astype(jnp.bfloat16))
        onehot = jnp.concatenate(parts, axis=1)
        wide = jnp.concatenate([moved_ref[src, :tok_rows, :], ones], axis=1)
        sums_ref[...] += jnp.dot(onehot, wide, preferred_element_type=jnp.float32)

    centroid = (sums_ref[:, :e_width] / jnp.maximum(sums_ref[:, e_width:], 1.0)).astype(jnp.bfloat16)

    def score(src, top):
        keys = moved_ref[src, tok_rows : 2 * tok_rows, :]
        scores = lax.dot_general(centroid, keys, (((1,), (1,)), ((), ())), preferred_element_type=jnp.float32)
        scores_ref[src] = scores
        for i in range(blocks):
            top = jnp.maximum(top, scores[:, i * lanes : (i + 1) * lanes])
        return top

    top = lax.fori_loop(0, n_src, score, jnp.full((C, lanes), -jnp.inf, jnp.float32), unroll=8)
    top = jnp.broadcast_to(jnp.max(top, axis=1, keepdims=True), (C, tok_rows))

    acc_ref[...] = jnp.zeros_like(acc_ref)

    def weigh(src, total):
        weights = jnp.exp((scores_ref[src] - top) * scale)
        for i in range(blocks):
            total += weights[:, i * lanes : (i + 1) * lanes]
        values = moved_ref[src, 2 * tok_rows : 3 * tok_rows, :]
        acc_ref[...] += jnp.dot(weights.astype(jnp.bfloat16), values, preferred_element_type=jnp.float32)
        return total

    total = lax.fori_loop(0, n_src, weigh, jnp.zeros((C, lanes), jnp.float32), unroll=8)
    out_ref[...] = (acc_ref[...] / jnp.sum(total, axis=1, keepdims=True)).astype(jnp.bfloat16)


def attend(moved, tok_rows):
    n_src, _, e_width = moved.shape
    tokens = n_src * tok_rows
    return pl.pallas_call(
        lambda *refs: attend_kernel(tok_rows, *refs),
        out_shape=jax.ShapeDtypeStruct((C, e_width), jnp.bfloat16),
        in_specs=[pl.BlockSpec(memory_space=pltpu.VMEM)],
        out_specs=pl.BlockSpec(memory_space=pltpu.VMEM),
        scratch_shapes=[
            pltpu.VMEM((C, 2 * e_width), jnp.float32),
            pltpu.VMEM((n_src, C, tok_rows), jnp.float32),
            pltpu.VMEM((C, e_width), jnp.float32),
        ],
        compiler_params=pltpu.CompilerParams(vmem_limit_bytes=24 * 2**20),
        cost_estimate=pl.CostEstimate(
            flops=8 * C * tokens * e_width, bytes_accessed=moved.size * 2, transcendentals=C * tokens
        ),
        name="attend",
    )(moved)


def expand_kernel(ids_ref, attended_ref, *refs):
    out_ref = refs[-1]
    heads, clusters, e_width = attended_ref.shape
    tok_tile = ids_ref.shape[2]
    labels = lax.broadcasted_iota(jnp.int32, (tok_tile, e_width), 1).astype(jnp.int16)
    one, zero = jnp.bfloat16(1.0), jnp.bfloat16(0.0)
    columns = ids_ref[0].T
    for h in range(heads):
        ids = jnp.broadcast_to(columns[:, h : h + 1], (tok_tile, e_width)).astype(jnp.int16)
        parts = [jnp.where(ids == labels + jnp.int16(at), one, zero) for at in range(0, clusters, e_width)]
        onehot = jnp.concatenate(parts, axis=1)
        found = jnp.dot(onehot, attended_ref[h], preferred_element_type=jnp.float32)
        out_ref[h] = found.astype(jnp.bfloat16)


def expand(ids, part, attended, store, piece, pieces, tok_tile):
    _, heads, tokens = ids.shape
    _, clusters, e_width = attended.shape
    held = () if store is None else (store,)
    return pl.pallas_call(
        expand_kernel,
        out_shape=jax.ShapeDtypeStruct((pieces * heads, tokens, e_width), jnp.bfloat16),
        grid=(tokens // tok_tile,),
        in_specs=[
            pl.BlockSpec((1, heads, tok_tile), lambda i: (part, 0, i)),
            pl.BlockSpec((heads, clusters, e_width), lambda i: (0, 0, 0)),
        ]
        + [pl.BlockSpec(memory_space=pl.ANY) for _ in held],
        out_specs=pl.BlockSpec((heads, tok_tile, e_width), lambda i: (piece, i, 0)),
        input_output_aliases={2: 0} if held else {},
        compiler_params=pltpu.CompilerParams(vmem_limit_bytes=50 * 2**20),
        cost_estimate=pl.CostEstimate(
            flops=4 * tokens * heads * clusters * e_width,
            bytes_accessed=2 * heads * (clusters + tokens) * e_width,
            transcendentals=0,
        ),
        name="expand",
    )(ids, attended, *held)


def project_kernel(places_ref, features_ref, near_ref, *refs):
    *far_refs, out_ref = refs
    heads, _, e_width = features_ref.shape
    each = heads // 4
    head_at, core, half_at, place = (places_ref[i] for i in range(4))
    total = None
    for plane, weight_refs in ((half_at, (near_ref,)), (1 - half_at, far_refs)):
        base = jnp.where(plane == head_at, 0, 2 * each)
        blocks = [(x, i) for x in weight_refs for i in range(x.shape[0])]
        for k, (weight_ref, i) in enumerate(blocks):
            chip = jnp.bitwise_xor(place, k)
            slot = 2 * lax.rem(chip, each // 2) + jnp.bitwise_xor(half_at, lax.div(chip, each // 2))
            left = jnp.concatenate([features_ref[base + at * each + slot] for at in (core, 1 - core)], axis=1)
            right = weight_ref[i, : 2 * e_width, :]
            term = jnp.dot(left, right, preferred_element_type=jnp.float32)
            total = term if total is None else total + term
    out_ref[...] = total.astype(jnp.bfloat16)


def project(places, features, near, far, tok_tile):
    heads, tokens, e_width = features.shape
    cols = near.shape[2]
    return pl.pallas_call(
        project_kernel,
        out_shape=jax.ShapeDtypeStruct((tokens, cols), jnp.bfloat16),
        grid_spec=pltpu.PrefetchScalarGridSpec(
            num_scalar_prefetch=1,
            grid=(tokens // tok_tile,),
            in_specs=[
                pl.BlockSpec((heads, tok_tile, e_width), lambda i, _: (0, i, 0)),
                pl.BlockSpec(near.shape, lambda i, _: (0, 0, 0)),
            ]
            + [pl.BlockSpec(x.shape, lambda i, _: (0, 0, 0)) for x in far],
            out_specs=pl.BlockSpec((tok_tile, cols), lambda i, _: (i, 0)),
        ),
        compiler_params=pltpu.CompilerParams(vmem_limit_bytes=50 * 2**20),
        cost_estimate=pl.CostEstimate(
            flops=2 * tokens * heads * e_width * cols,
            bytes_accessed=2 * (features.size + heads * e_width * cols + tokens * cols),
            transcendentals=0,
        ),
        name="project",
    )(places, features, near, *far)


def by_slot(ids, half_at, core):
    sources, heads, tok_rows = ids.shape
    ids = ids.reshape(sources, 2, heads // 4, 2, tok_rows).transpose(3, 2, 1, 0, 4)
    ids = jnp.where(half_at == 0, ids, ids[:, :, ::-1])
    ids = jnp.where(core == 0, ids, ids[::-1])
    return ids.reshape(2, heads // 2, sources * tok_rows)


def by_head(queries, keys, values, cluster_ids, out_weight):
    tok_rows, head_count, e_width = queries.shape
    n_seq = lax.axis_size("seq")
    half = n_seq // 2
    rows, cols = out_weight.shape
    cols_each = cols // half
    seq_at = lax.axis_index("seq")
    head_at = lax.axis_index("head")
    half_at = seq_at // half
    core = lax.rem(seq_at, 2)
    place = lax.rem(seq_at, half)
    swap_heads = [(0, 1), (1, 0)]
    swap_halves = [(i, (i + half) % n_seq) for i in range(n_seq)]
    swap_cores = [(i, i ^ 1) for i in range(n_seq)]
    halves = [list(range(half)), list(range(half, n_seq))]
    same_core = [list(range(at + core_of, at + half, 2)) for at in (0, half) for core_of in range(2)]

    ids_t = cluster_ids.T
    high, low = (ids_t // 16).astype(jnp.bfloat16), (ids_t % 16).astype(jnp.bfloat16)
    id_rows = -(-2 * tok_rows // (16 * e_width)) * 16
    coded = jnp.concatenate([high, low], axis=1)
    coded = jnp.pad(coded, ((0, 0), (0, id_rows * e_width - 2 * tok_rows)))
    packed = jnp.concatenate(
        [x.transpose(1, 0, 2) for x in (queries, keys, values)] + [coded.reshape(head_count, id_rows, e_width)],
        axis=1,
    )
    packed, out_weight, high, low = lax.optimization_barrier((packed, out_weight, high, low))
    moved = lax.all_to_all(packed, "seq", split_axis=0, concat_axis=0, tiled=True)

    blocks = out_weight.reshape(rows, half, cols_each).transpose(1, 0, 2)
    coded = jnp.concatenate([high, low], axis=0)
    near = []
    for k in range(half):
        block = lax.dynamic_index_in_dim(blocks, jnp.bitwise_xor(place, k), 0, keepdims=False)
        block = jnp.concatenate([block, coded], axis=0)
        near.append(lax.ppermute(block, "seq", [(i, i ^ k) for i in range(n_seq)]) if k else block)
    near = jnp.stack(near)
    moved, near = lax.optimization_barrier((moved, near))
    cuts = [half * i // 8 for i in (0, 1, 3, 6, 8)]
    far = [lax.ppermute(near[a:b, :rows], "seq", swap_halves) for a, b in zip(cuts[:1], cuts[1:])]
    own = attend(moved, tok_rows)
    own, near, far[0] = lax.optimization_barrier((own, near, far[0]))
    far += [lax.ppermute(near[a:b, :rows], "seq", swap_halves) for a, b in zip(cuts[1:], cuts[2:])]

    def copied(pair):
        return jnp.broadcast_to(pair[None], (half // 2,) + pair.shape)

    def spread(copies):
        got = lax.all_to_all(
            copies, "seq", split_axis=0, concat_axis=0, axis_index_groups=same_core, tiled=True
        )
        return got.reshape((half,) + own.shape)

    pair = jnp.stack([own, lax.ppermute(own, "seq", swap_halves)])
    far_pair = lax.ppermute(pair, "head", swap_heads)
    first = spread(copied(pair))

    coded = near[:, rows:].astype(jnp.int32)
    coded = coded[:, :head_count] * 16 + coded[:, head_count:]
    coded = jnp.concatenate(
        [lax.dynamic_slice_in_dim(coded, jnp.bitwise_xor(place, i), 1, axis=0) for i in range(half)], axis=0
    )
    slot_ids = by_slot(coded, half_at, core)
    far_ids = lax.ppermute(slot_ids, "head", swap_heads)
    far_copies = copied(far_pair)
    first, slot_ids, far_ids, far_copies, far[1] = lax.optimization_barrier(
        (first, slot_ids, far_ids, far_copies, far[1])
    )
    second = lax.ppermute(first, "seq", swap_cores)
    third = spread(far_copies)

    pieces = 4
    tok_tile = 2 * tok_rows
    features = expand(slot_ids, 0, first, None, 0, pieces, 2 * tok_tile)
    features = expand(slot_ids, 1, second, features, 1, pieces, 2 * tok_tile)
    features, third, far[2] = lax.optimization_barrier((features, third, far[2]))
    fourth = lax.ppermute(third, "seq", swap_cores)
    features = expand(far_ids, 0, third, features, 2, pieces, 2 * tok_tile)
    features = expand(far_ids, 1, fourth, features, 3, pieces, 2 * tok_tile)
    places = jnp.stack([head_at, core, half_at, place]).astype(jnp.int32)
    near_out = project(places, features, near, far, tok_tile)
    mixed = lax.all_to_all(
        near_out.reshape(half, tok_rows, cols_each),
        "seq",
        split_axis=0,
        concat_axis=0,
        axis_index_groups=halves,
        tiled=True,
    )
    return mixed.transpose(1, 0, 2).reshape(tok_rows, cols)


def fits(queries, out_weight):
    n_seq = lax.axis_size("seq")
    tok_rows, head_count, e_width = queries.shape
    return (
        head_count == n_seq
        and lax.axis_size("head") == 2
        and n_seq >= 8
        and n_seq & (n_seq - 1) == 0
        and e_width == 128
        and tok_rows % e_width == 0
        and out_weight.shape[0] == 2 * e_width
        and out_weight.shape[1] == n_seq // 2 * tok_rows
        and out_weight.shape[1] % (n_seq // 2 * 128) == 0
    )


def on_device(queries, keys, values, cluster_ids, out_weight):
    if fits(queries, out_weight):
        return by_head(queries, keys, values, cluster_ids, out_weight)
    return by_reduction(queries, keys, values, cluster_ids, out_weight)


def solution(mesh):
    placed = (
        P("seq", "head", None),
        P("seq", "head", None),
        P("seq", "head", None),
        P("seq", "head"),
        P("seq", "head"),
    )
    return jax.shard_map(
        on_device, mesh=mesh, in_specs=placed, out_specs=P("seq", "head"), check_vma=False
    )
```

```python
import math

import jax
import jax.numpy as jnp
from jax import lax
from jax.experimental import pallas as pl
from jax.experimental.pallas import tpu as pltpu
from jax.sharding import PartitionSpec as P

C = 512


def expand_and_project(ids, attended, weight):
    tok_rows = ids.shape[0]
    heads, _, e_width = attended.shape
    labels = lax.broadcasted_iota(jnp.int32, (heads, tok_rows, C), 2)
    onehot = (ids.T[:, :, None] == labels).astype(jnp.bfloat16)
    features = jnp.einsum("htc,hce->the", onehot, attended, preferred_element_type=jnp.float32).astype(
        jnp.bfloat16
    )
    flat = features.reshape(tok_rows, heads * e_width)
    return jnp.dot(flat, weight, preferred_element_type=jnp.float32).astype(jnp.bfloat16)


def by_reduction(queries, keys, values, cluster_ids, out_weight):
    tok_rows, head_count, e_width = queries.shape
    score_scale = 1.0 / math.sqrt(e_width)
    labels = lax.broadcasted_iota(jnp.int32, (head_count, tok_rows, C), 2)
    onehot = (cluster_ids.T[:, :, None] == labels).astype(jnp.bfloat16)
    totals = jnp.einsum("htc,the->hce", onehot, queries, preferred_element_type=jnp.float32)
    counts = jnp.sum(onehot, axis=1, dtype=jnp.float32)
    all_totals, all_counts = lax.psum((totals, counts), "seq")
    centroid = (all_totals / jnp.maximum(all_counts, 1.0)[:, :, None]).astype(jnp.bfloat16)
    scores = jnp.einsum("hce,the->hct", centroid, keys, preferred_element_type=jnp.float32) * score_scale
    local_max = jnp.max(scores, axis=2)
    weights = jnp.exp(scores - local_max[:, :, None])
    local_total = jnp.sum(weights, axis=2)
    local_out = jnp.einsum(
        "hct,the->hce", weights.astype(jnp.bfloat16), values, preferred_element_type=jnp.float32
    )
    global_max = lax.pmax(local_max, "seq")
    factor = jnp.exp(local_max - global_max)
    share_out = lax.psum_scatter(local_out * factor[:, :, None], "seq", scatter_dimension=1, tiled=True)
    share_total = lax.psum_scatter(local_total * factor, "seq", scatter_dimension=1, tiled=True)
    share_attended = (share_out / share_total[:, :, None]).astype(jnp.bfloat16)
    attended = lax.all_gather(share_attended, "seq", axis=1, tiled=True)
    attended = lax.all_gather(attended, "head", axis=0, tiled=True)
    ids = lax.all_gather(cluster_ids, "head", axis=1, tiled=True)
    weight = lax.all_gather(out_weight, "seq", axis=0, tiled=True)
    return expand_and_project(ids, attended, weight)


def attend_kernel(tok_rows, source_ref, out_ref, sums_ref, scores_ref, acc_ref, moved_ref, sems):
    rows = source_ref.shape[1]
    spans = [(0, tok_rows), (3 * tok_rows, rows), (tok_rows, 2 * tok_rows), (2 * tok_rows, 3 * tok_rows)]
    loads = [
        pltpu.make_async_copy(source_ref.at[:, a:b], moved_ref.at[:, a:b], sems.at[i])
        for i, (a, b) in enumerate(spans)
    ]
    for load in loads:
        load.start()
    n_src, _, e_width = moved_ref.shape
    lanes = e_width
    blocks = tok_rows // lanes
    scale = 1.0 / math.sqrt(e_width)
    cluster = lax.broadcasted_iota(jnp.int32, (C, lanes), 0)
    ones = jnp.ones((tok_rows, e_width), jnp.bfloat16)

    sums_ref[...] = jnp.zeros_like(sums_ref)
    loads[0].wait()
    loads[1].wait()

    @pl.loop(0, n_src, unroll=16)
    def _(src):
        coded = moved_ref[src, 3 * tok_rows :, :].astype(jnp.float32).astype(jnp.int32)
        parts = []
        for i in range(blocks):
            ids = coded[i : i + 1] * 16 + coded[blocks + i : blocks + i + 1]
            parts.append(jnp.where(cluster == ids, 1.0, 0.0).astype(jnp.bfloat16))
        onehot = jnp.concatenate(parts, axis=1)
        wide = jnp.concatenate([moved_ref[src, :tok_rows, :], ones], axis=1)
        sums_ref[...] += jnp.dot(onehot, wide, preferred_element_type=jnp.float32)

    centroid = (sums_ref[:, :e_width] / jnp.maximum(sums_ref[:, e_width:], 1.0)).astype(jnp.bfloat16)

    loads[2].wait()

    def score(src, top):
        keys = moved_ref[src, tok_rows : 2 * tok_rows, :]
        scores = lax.dot_general(centroid, keys, (((1,), (1,)), ((), ())), preferred_element_type=jnp.float32)
        scores_ref[src] = scores
        for i in range(blocks):
            top = jnp.maximum(top, scores[:, i * lanes : (i + 1) * lanes])
        return top

    top = lax.fori_loop(0, n_src, score, jnp.full((C, lanes), -jnp.inf, jnp.float32), unroll=16)
    top = jnp.broadcast_to(jnp.max(top, axis=1, keepdims=True), (C, tok_rows))

    acc_ref[...] = jnp.zeros_like(acc_ref)
    loads[3].wait()

    def weigh(src, total):
        weights = jnp.exp((scores_ref[src] - top) * scale)
        for i in range(blocks):
            total += weights[:, i * lanes : (i + 1) * lanes]
        values = moved_ref[src, 2 * tok_rows : 3 * tok_rows, :]
        acc_ref[...] += jnp.dot(weights.astype(jnp.bfloat16), values, preferred_element_type=jnp.float32)
        return total

    total = lax.fori_loop(0, n_src, weigh, jnp.zeros((C, lanes), jnp.float32), unroll=16)
    out_ref[...] = (acc_ref[...] / jnp.sum(total, axis=1, keepdims=True)).astype(jnp.bfloat16)


def attend(moved, tok_rows):
    n_src, _, e_width = moved.shape
    tokens = n_src * tok_rows
    return pl.pallas_call(
        lambda *refs: attend_kernel(tok_rows, *refs),
        out_shape=jax.ShapeDtypeStruct((C, e_width), jnp.bfloat16),
        in_specs=[pl.BlockSpec(memory_space=pl.ANY)],
        out_specs=pl.BlockSpec(memory_space=pltpu.VMEM),
        scratch_shapes=[
            pltpu.VMEM((C, 2 * e_width), jnp.float32),
            pltpu.VMEM((n_src, C, tok_rows), jnp.float32),
            pltpu.VMEM((C, e_width), jnp.float32),
            pltpu.VMEM(moved.shape, moved.dtype),
            pltpu.SemaphoreType.DMA((4,)),
        ],
        compiler_params=pltpu.CompilerParams(vmem_limit_bytes=24 * 2**20),
        cost_estimate=pl.CostEstimate(
            flops=8 * C * tokens * e_width, bytes_accessed=moved.size * 2, transcendentals=C * tokens
        ),
        name="attend",
    )(moved)


def expand_kernel(ids_ref, attended_ref, *refs):
    out_ref = refs[-1]
    heads, clusters, e_width = attended_ref.shape
    tok_tile = ids_ref.shape[2]
    labels = lax.broadcasted_iota(jnp.int32, (tok_tile, e_width), 1).astype(jnp.int16)
    one, zero = jnp.bfloat16(1.0), jnp.bfloat16(0.0)
    columns = ids_ref[0].T
    for h in range(heads):
        ids = jnp.broadcast_to(columns[:, h : h + 1], (tok_tile, e_width)).astype(jnp.int16)
        parts = [jnp.where(ids == labels + jnp.int16(at), one, zero) for at in range(0, clusters, e_width)]
        onehot = jnp.concatenate(parts, axis=1)
        found = jnp.dot(onehot, attended_ref[h], preferred_element_type=jnp.float32)
        out_ref[h] = found.astype(jnp.bfloat16)


def expand(ids, part, attended, store, piece, pieces, tok_tile):
    _, heads, tokens = ids.shape
    _, clusters, e_width = attended.shape
    held = () if store is None else (store,)
    return pl.pallas_call(
        expand_kernel,
        out_shape=jax.ShapeDtypeStruct((pieces * heads, tokens, e_width), jnp.bfloat16),
        grid=(tokens // tok_tile,),
        in_specs=[
            pl.BlockSpec((1, heads, tok_tile), lambda i: (part, 0, i)),
            pl.BlockSpec((heads, clusters, e_width), lambda i: (0, 0, 0)),
        ]
        + [pl.BlockSpec(memory_space=pl.ANY) for _ in held],
        out_specs=pl.BlockSpec((heads, tok_tile, e_width), lambda i: (piece, i, 0)),
        input_output_aliases={2: 0} if held else {},
        compiler_params=pltpu.CompilerParams(vmem_limit_bytes=50 * 2**20),
        cost_estimate=pl.CostEstimate(
            flops=4 * tokens * heads * clusters * e_width,
            bytes_accessed=2 * heads * (clusters + tokens) * e_width,
            transcendentals=0,
        ),
        name="expand",
    )(ids, attended, *held)


def project_kernel(places_ref, features_ref, near_ref, *refs):
    *far_refs, out_ref = refs
    heads, _, e_width = features_ref.shape
    each = heads // 4
    head_at, core, half_at, place = (places_ref[i] for i in range(4))
    total = None
    for plane, weight_refs in ((half_at, (near_ref,)), (1 - half_at, far_refs)):
        base = jnp.where(plane == head_at, 0, 2 * each)
        blocks = [(x, i) for x in weight_refs for i in range(x.shape[0])]
        for k, (weight_ref, i) in enumerate(blocks):
            chip = jnp.bitwise_xor(place, k)
            slot = 2 * lax.rem(chip, each // 2) + jnp.bitwise_xor(half_at, lax.div(chip, each // 2))
            left = jnp.concatenate([features_ref[base + at * each + slot] for at in (core, 1 - core)], axis=1)
            right = weight_ref[i, : 2 * e_width, :]
            term = jnp.dot(left, right, preferred_element_type=jnp.float32)
            total = term if total is None else total + term
    out_ref[...] = total.astype(jnp.bfloat16)


def project(places, features, near, far, tok_tile):
    heads, tokens, e_width = features.shape
    cols = near.shape[2]
    return pl.pallas_call(
        project_kernel,
        out_shape=jax.ShapeDtypeStruct((tokens, cols), jnp.bfloat16),
        grid_spec=pltpu.PrefetchScalarGridSpec(
            num_scalar_prefetch=1,
            grid=(tokens // tok_tile,),
            in_specs=[
                pl.BlockSpec((heads, tok_tile, e_width), lambda i, _: (0, i, 0)),
                pl.BlockSpec(near.shape, lambda i, _: (0, 0, 0)),
            ]
            + [pl.BlockSpec(x.shape, lambda i, _: (0, 0, 0)) for x in far],
            out_specs=pl.BlockSpec((tok_tile, cols), lambda i, _: (i, 0)),
        ),
        compiler_params=pltpu.CompilerParams(vmem_limit_bytes=50 * 2**20),
        cost_estimate=pl.CostEstimate(
            flops=2 * tokens * heads * e_width * cols,
            bytes_accessed=2 * (features.size + heads * e_width * cols + tokens * cols),
            transcendentals=0,
        ),
        name="project",
    )(places, features, near, *far)


def by_slot(ids, half_at, core):
    sources, heads, tok_rows = ids.shape
    ids = ids.reshape(sources, 2, heads // 4, 2, tok_rows).transpose(3, 2, 1, 0, 4)
    ids = jnp.where(half_at == 0, ids, ids[:, :, ::-1])
    ids = jnp.where(core == 0, ids, ids[::-1])
    return ids.reshape(2, heads // 2, sources * tok_rows)


def by_head(queries, keys, values, cluster_ids, out_weight):
    tok_rows, head_count, e_width = queries.shape
    n_seq = lax.axis_size("seq")
    half = n_seq // 2
    rows, cols = out_weight.shape
    cols_each = cols // half
    seq_at = lax.axis_index("seq")
    head_at = lax.axis_index("head")
    half_at = seq_at // half
    core = lax.rem(seq_at, 2)
    place = lax.rem(seq_at, half)
    swap_heads = [(0, 1), (1, 0)]
    swap_halves = [(i, (i + half) % n_seq) for i in range(n_seq)]
    swap_cores = [(i, i ^ 1) for i in range(n_seq)]
    halves = [list(range(half)), list(range(half, n_seq))]
    same_core = [list(range(at + core_of, at + half, 2)) for at in (0, half) for core_of in range(2)]

    ids_t = cluster_ids.T
    high, low = (ids_t // 16).astype(jnp.bfloat16), (ids_t % 16).astype(jnp.bfloat16)
    id_rows = -(-2 * tok_rows // (16 * e_width)) * 16
    coded = jnp.concatenate([high, low], axis=1)
    coded = jnp.pad(coded, ((0, 0), (0, id_rows * e_width - 2 * tok_rows)))
    packed = jnp.concatenate(
        [x.transpose(1, 0, 2) for x in (queries, keys, values)] + [coded.reshape(head_count, id_rows, e_width)],
        axis=1,
    )
    packed, out_weight, high, low = lax.optimization_barrier((packed, out_weight, high, low))
    moved = lax.all_to_all(packed, "seq", split_axis=0, concat_axis=0, tiled=True)

    blocks = out_weight.reshape(rows, half, cols_each).transpose(1, 0, 2)
    coded = jnp.concatenate([high, low], axis=0)
    near = []
    for k in range(half):
        block = lax.dynamic_index_in_dim(blocks, jnp.bitwise_xor(place, k), 0, keepdims=False)
        block = jnp.concatenate([block, coded], axis=0)
        near.append(lax.ppermute(block, "seq", [(i, i ^ k) for i in range(n_seq)]) if k else block)
    near = jnp.stack(near)
    moved, near = lax.optimization_barrier((moved, near))
    cuts = [half * i // 8 for i in (0, 1, 3, 6, 8)]
    far = [lax.ppermute(near[a:b, :rows], "seq", swap_halves) for a, b in zip(cuts[:1], cuts[1:])]
    own = attend(moved, tok_rows)
    own, near, far[0] = lax.optimization_barrier((own, near, far[0]))
    far += [lax.ppermute(near[a:b, :rows], "seq", swap_halves) for a, b in zip(cuts[1:], cuts[2:])]

    def copied(pair):
        return jnp.broadcast_to(pair[None], (half // 2,) + pair.shape)

    def spread(copies):
        got = lax.all_to_all(
            copies, "seq", split_axis=0, concat_axis=0, axis_index_groups=same_core, tiled=True
        )
        return got.reshape((half,) + own.shape)

    pair = jnp.stack([own, lax.ppermute(own, "seq", swap_halves)])
    far_pair = lax.ppermute(pair, "head", swap_heads)
    first = spread(copied(pair))

    coded = near[:, rows:].astype(jnp.int32)
    coded = coded[:, :head_count] * 16 + coded[:, head_count:]
    coded = jnp.concatenate(
        [lax.dynamic_slice_in_dim(coded, jnp.bitwise_xor(place, i), 1, axis=0) for i in range(half)], axis=0
    )
    slot_ids = by_slot(coded, half_at, core)
    far_ids = lax.ppermute(slot_ids, "head", swap_heads)
    far_copies = copied(far_pair)
    first, slot_ids, far_ids, far_copies, far[1] = lax.optimization_barrier(
        (first, slot_ids, far_ids, far_copies, far[1])
    )
    second = lax.ppermute(first, "seq", swap_cores)
    third = spread(far_copies)

    pieces = 4
    tok_tile = 2 * tok_rows
    features = expand(slot_ids, 0, first, None, 0, pieces, 2 * tok_tile)
    features = expand(slot_ids, 1, second, features, 1, pieces, 2 * tok_tile)
    features, third, far[2] = lax.optimization_barrier((features, third, far[2]))
    fourth = lax.ppermute(third, "seq", swap_cores)
    features = expand(far_ids, 0, third, features, 2, pieces, 2 * tok_tile)
    features = expand(far_ids, 1, fourth, features, 3, pieces, 2 * tok_tile)
    places = jnp.stack([head_at, core, half_at, place]).astype(jnp.int32)
    near_out = project(places, features, near, far, tok_tile)
    mixed = lax.all_to_all(
        near_out.reshape(half, tok_rows, cols_each),
        "seq",
        split_axis=0,
        concat_axis=0,
        axis_index_groups=halves,
        tiled=True,
    )
    return mixed.transpose(1, 0, 2).reshape(tok_rows, cols)


def fits(queries, out_weight):
    n_seq = lax.axis_size("seq")
    tok_rows, head_count, e_width = queries.shape
    return (
        head_count == n_seq
        and lax.axis_size("head") == 2
        and n_seq >= 8
        and n_seq & (n_seq - 1) == 0
        and e_width == 128
        and tok_rows % e_width == 0
        and out_weight.shape[0] == 2 * e_width
        and out_weight.shape[1] == n_seq // 2 * tok_rows
        and out_weight.shape[1] % (n_seq // 2 * 128) == 0
    )


def on_device(queries, keys, values, cluster_ids, out_weight):
    if fits(queries, out_weight):
        return by_head(queries, keys, values, cluster_ids, out_weight)
    return by_reduction(queries, keys, values, cluster_ids, out_weight)


def solution(mesh):
    placed = (
        P("seq", "head", None),
        P("seq", "head", None),
        P("seq", "head", None),
        P("seq", "head"),
        P("seq", "head"),
    )
    return jax.shard_map(
        on_device, mesh=mesh, in_specs=placed, out_specs=P("seq", "head"), check_vma=False
    )
```

```python
import math

import jax
import jax.numpy as jnp
from jax import lax
from jax.experimental import pallas as pl
from jax.experimental.pallas import tpu as pltpu
from jax.sharding import PartitionSpec as P

C = 512


def expand_and_project(ids, attended, weight):
    tok_rows = ids.shape[0]
    heads, _, e_width = attended.shape
    labels = lax.broadcasted_iota(jnp.int32, (heads, tok_rows, C), 2)
    onehot = (ids.T[:, :, None] == labels).astype(jnp.bfloat16)
    features = jnp.einsum("htc,hce->the", onehot, attended, preferred_element_type=jnp.float32).astype(
        jnp.bfloat16
    )
    flat = features.reshape(tok_rows, heads * e_width)
    return jnp.dot(flat, weight, preferred_element_type=jnp.float32).astype(jnp.bfloat16)


def by_reduction(queries, keys, values, cluster_ids, out_weight):
    tok_rows, head_count, e_width = queries.shape
    score_scale = 1.0 / math.sqrt(e_width)
    labels = lax.broadcasted_iota(jnp.int32, (head_count, tok_rows, C), 2)
    onehot = (cluster_ids.T[:, :, None] == labels).astype(jnp.bfloat16)
    totals = jnp.einsum("htc,the->hce", onehot, queries, preferred_element_type=jnp.float32)
    counts = jnp.sum(onehot, axis=1, dtype=jnp.float32)
    all_totals, all_counts = lax.psum((totals, counts), "seq")
    centroid = (all_totals / jnp.maximum(all_counts, 1.0)[:, :, None]).astype(jnp.bfloat16)
    scores = jnp.einsum("hce,the->hct", centroid, keys, preferred_element_type=jnp.float32) * score_scale
    local_max = jnp.max(scores, axis=2)
    weights = jnp.exp(scores - local_max[:, :, None])
    local_total = jnp.sum(weights, axis=2)
    local_out = jnp.einsum(
        "hct,the->hce", weights.astype(jnp.bfloat16), values, preferred_element_type=jnp.float32
    )
    global_max = lax.pmax(local_max, "seq")
    factor = jnp.exp(local_max - global_max)
    share_out = lax.psum_scatter(local_out * factor[:, :, None], "seq", scatter_dimension=1, tiled=True)
    share_total = lax.psum_scatter(local_total * factor, "seq", scatter_dimension=1, tiled=True)
    share_attended = (share_out / share_total[:, :, None]).astype(jnp.bfloat16)
    attended = lax.all_gather(share_attended, "seq", axis=1, tiled=True)
    attended = lax.all_gather(attended, "head", axis=0, tiled=True)
    ids = lax.all_gather(cluster_ids, "head", axis=1, tiled=True)
    weight = lax.all_gather(out_weight, "seq", axis=0, tiled=True)
    return expand_and_project(ids, attended, weight)


def attend_kernel(tok_rows, moved_ref, out_ref, sums_ref, scores_ref, acc_ref):
    n_src, _, e_width = moved_ref.shape
    lanes = e_width
    blocks = tok_rows // lanes
    scale = 1.0 / math.sqrt(e_width)
    cluster = lax.broadcasted_iota(jnp.int32, (C, lanes), 0)
    ones = jnp.ones((tok_rows, e_width), jnp.bfloat16)

    sums_ref[...] = jnp.zeros_like(sums_ref)

    @pl.loop(0, n_src, unroll=8)
    def _(src):
        coded = moved_ref[src, 3 * tok_rows :, :].astype(jnp.float32).astype(jnp.int32)
        parts = []
        for i in range(blocks):
            ids = coded[i : i + 1] * 16 + coded[blocks + i : blocks + i + 1]
            parts.append(jnp.where(cluster == ids, 1.0, 0.0).astype(jnp.bfloat16))
        onehot = jnp.concatenate(parts, axis=1)
        wide = jnp.concatenate([moved_ref[src, :tok_rows, :], ones], axis=1)
        sums_ref[...] += jnp.dot(onehot, wide, preferred_element_type=jnp.float32)

    centroid = (sums_ref[:, :e_width] / jnp.maximum(sums_ref[:, e_width:], 1.0)).astype(jnp.bfloat16)

    def score(src, top):
        keys = moved_ref[src, tok_rows : 2 * tok_rows, :]
        scores = lax.dot_general(centroid, keys, (((1,), (1,)), ((), ())), preferred_element_type=jnp.float32)
        scores_ref[src] = scores
        for i in range(blocks):
            top = jnp.maximum(top, scores[:, i * lanes : (i + 1) * lanes])
        return top

    top = lax.fori_loop(0, n_src, score, jnp.full((C, lanes), -jnp.inf, jnp.float32), unroll=8)
    top = jnp.broadcast_to(jnp.max(top, axis=1, keepdims=True), (C, tok_rows))

    acc_ref[...] = jnp.zeros_like(acc_ref)

    def weigh(src, total):
        weights = jnp.exp((scores_ref[src] - top) * scale)
        for i in range(blocks):
            total += weights[:, i * lanes : (i + 1) * lanes]
        values = moved_ref[src, 2 * tok_rows : 3 * tok_rows, :]
        acc_ref[...] += jnp.dot(weights.astype(jnp.bfloat16), values, preferred_element_type=jnp.float32)
        return total

    total = lax.fori_loop(0, n_src, weigh, jnp.zeros((C, lanes), jnp.float32), unroll=8)
    out_ref[...] = (acc_ref[...] / jnp.sum(total, axis=1, keepdims=True)).astype(jnp.bfloat16)


def attend(moved, tok_rows):
    n_src, _, e_width = moved.shape
    tokens = n_src * tok_rows
    return pl.pallas_call(
        lambda *refs: attend_kernel(tok_rows, *refs),
        out_shape=jax.ShapeDtypeStruct((C, e_width), jnp.bfloat16),
        in_specs=[pl.BlockSpec(memory_space=pltpu.VMEM)],
        out_specs=pl.BlockSpec(memory_space=pltpu.VMEM),
        scratch_shapes=[
            pltpu.VMEM((C, 2 * e_width), jnp.float32),
            pltpu.VMEM((n_src, C, tok_rows), jnp.float32),
            pltpu.VMEM((C, e_width), jnp.float32),
        ],
        compiler_params=pltpu.CompilerParams(vmem_limit_bytes=24 * 2**20),
        cost_estimate=pl.CostEstimate(
            flops=8 * C * tokens * e_width, bytes_accessed=moved.size * 2, transcendentals=C * tokens
        ),
        name="attend",
    )(moved)


def expand_kernel(ids_ref, attended_ref, *refs):
    out_ref = refs[-1]
    heads, clusters, e_width = attended_ref.shape
    tok_tile = ids_ref.shape[2]
    labels = lax.broadcasted_iota(jnp.int32, (tok_tile, e_width), 1).astype(jnp.int16)
    one, zero = jnp.bfloat16(1.0), jnp.bfloat16(0.0)
    columns = ids_ref[0].T
    for h in range(heads):
        ids = jnp.broadcast_to(columns[:, h : h + 1], (tok_tile, e_width)).astype(jnp.int16)
        parts = [jnp.where(ids == labels + jnp.int16(at), one, zero) for at in range(0, clusters, e_width)]
        onehot = jnp.concatenate(parts, axis=1)
        found = jnp.dot(onehot, attended_ref[h], preferred_element_type=jnp.float32)
        out_ref[h] = found.astype(jnp.bfloat16)


def expand(ids, part, attended, store, piece, pieces, tok_tile):
    _, heads, tokens = ids.shape
    _, clusters, e_width = attended.shape
    held = () if store is None else (store,)
    return pl.pallas_call(
        expand_kernel,
        out_shape=jax.ShapeDtypeStruct((pieces * heads, tokens, e_width), jnp.bfloat16),
        grid=(tokens // tok_tile,),
        in_specs=[
            pl.BlockSpec((1, heads, tok_tile), lambda i: (part, 0, i)),
            pl.BlockSpec((heads, clusters, e_width), lambda i: (0, 0, 0)),
        ]
        + [pl.BlockSpec(memory_space=pl.ANY) for _ in held],
        out_specs=pl.BlockSpec((heads, tok_tile, e_width), lambda i: (piece, i, 0)),
        input_output_aliases={2: 0} if held else {},
        compiler_params=pltpu.CompilerParams(vmem_limit_bytes=50 * 2**20),
        cost_estimate=pl.CostEstimate(
            flops=4 * tokens * heads * clusters * e_width,
            bytes_accessed=2 * heads * (clusters + tokens) * e_width,
            transcendentals=0,
        ),
        name="expand",
    )(ids, attended, *held)


def project_kernel(places_ref, features_ref, near_ref, *refs):
    *far_refs, out_ref = refs
    heads, _, e_width = features_ref.shape
    each = heads // 4
    head_at, core, half_at, place = (places_ref[i] for i in range(4))
    total = None
    for plane, weight_refs in ((half_at, (near_ref,)), (1 - half_at, far_refs)):
        base = jnp.where(plane == head_at, 0, 2 * each)
        blocks = [(x, i) for x in weight_refs for i in range(x.shape[0])]
        for k, (weight_ref, i) in enumerate(blocks):
            chip = jnp.bitwise_xor(place, k)
            slot = 2 * lax.rem(chip, each // 2) + jnp.bitwise_xor(half_at, lax.div(chip, each // 2))
            left = jnp.concatenate([features_ref[base + at * each + slot] for at in (core, 1 - core)], axis=1)
            right = weight_ref[i, : 2 * e_width, :]
            term = jnp.dot(left, right, preferred_element_type=jnp.float32)
            total = term if total is None else total + term
    out_ref[...] = total.astype(jnp.bfloat16)


def project(places, features, near, far, tok_tile):
    heads, tokens, e_width = features.shape
    cols = near.shape[2]
    return pl.pallas_call(
        project_kernel,
        out_shape=jax.ShapeDtypeStruct((tokens, cols), jnp.bfloat16),
        grid_spec=pltpu.PrefetchScalarGridSpec(
            num_scalar_prefetch=1,
            grid=(tokens // tok_tile,),
            in_specs=[
                pl.BlockSpec((heads, tok_tile, e_width), lambda i, _: (0, i, 0)),
                pl.BlockSpec(near.shape, lambda i, _: (0, 0, 0)),
            ]
            + [pl.BlockSpec(x.shape, lambda i, _: (0, 0, 0)) for x in far],
            out_specs=pl.BlockSpec((tok_tile, cols), lambda i, _: (i, 0)),
        ),
        compiler_params=pltpu.CompilerParams(vmem_limit_bytes=50 * 2**20),
        cost_estimate=pl.CostEstimate(
            flops=2 * tokens * heads * e_width * cols,
            bytes_accessed=2 * (features.size + heads * e_width * cols + tokens * cols),
            transcendentals=0,
        ),
        name="project",
    )(places, features, near, *far)


def by_slot(ids, half_at, core):
    sources, heads, tok_rows = ids.shape
    ids = ids.reshape(sources, 2, heads // 4, 2, tok_rows).transpose(3, 2, 1, 0, 4)
    ids = jnp.where(half_at == 0, ids, ids[:, :, ::-1])
    ids = jnp.where(core == 0, ids, ids[::-1])
    return ids.reshape(2, heads // 2, sources * tok_rows)


def by_head(queries, keys, values, cluster_ids, out_weight):
    tok_rows, head_count, e_width = queries.shape
    n_seq = lax.axis_size("seq")
    half = n_seq // 2
    rows, cols = out_weight.shape
    cols_each = cols // half
    seq_at = lax.axis_index("seq")
    head_at = lax.axis_index("head")
    half_at = seq_at // half
    core = lax.rem(seq_at, 2)
    place = lax.rem(seq_at, half)
    swap_heads = [(0, 1), (1, 0)]
    swap_halves = [(i, (i + half) % n_seq) for i in range(n_seq)]
    swap_cores = [(i, i ^ 1) for i in range(n_seq)]
    halves = [list(range(half)), list(range(half, n_seq))]
    same_core = [list(range(at + core_of, at + half, 2)) for at in (0, half) for core_of in range(2)]

    ids_t = cluster_ids.T
    high, low = (ids_t // 16).astype(jnp.bfloat16), (ids_t % 16).astype(jnp.bfloat16)
    id_rows = -(-2 * tok_rows // (16 * e_width)) * 16
    coded = jnp.concatenate([high, low], axis=1)
    coded = jnp.pad(coded, ((0, 0), (0, id_rows * e_width - 2 * tok_rows)))
    coded = coded.reshape(head_count, id_rows, e_width).transpose(1, 0, 2)
    packed = jnp.concatenate([queries, keys, values, coded], axis=0).transpose(1, 0, 2)
    packed, out_weight, high, low = lax.optimization_barrier((packed, out_weight, high, low))
    moved = lax.all_to_all(packed, "seq", split_axis=0, concat_axis=0, tiled=True)

    blocks = out_weight.reshape(rows, half, cols_each).transpose(1, 0, 2)
    coded = jnp.concatenate([high, low], axis=0)
    near = []
    for k in range(half):
        block = lax.dynamic_index_in_dim(blocks, jnp.bitwise_xor(place, k), 0, keepdims=False)
        block = jnp.concatenate([block, coded], axis=0)
        near.append(lax.ppermute(block, "seq", [(i, i ^ k) for i in range(n_seq)]) if k else block)
    near = jnp.stack(near)
    moved, near = lax.optimization_barrier((moved, near))
    cuts = [half * i // 8 for i in (0, 1, 3, 6, 8)]
    far = [lax.ppermute(near[a:b, :rows], "seq", swap_halves) for a, b in zip(cuts[:1], cuts[1:])]
    own = attend(moved, tok_rows)
    own, near, far[0] = lax.optimization_barrier((own, near, far[0]))
    far += [lax.ppermute(near[a:b, :rows], "seq", swap_halves) for a, b in zip(cuts[1:], cuts[2:])]

    def copied(pair):
        return jnp.broadcast_to(pair[None], (half // 2,) + pair.shape)

    def spread(copies):
        got = lax.all_to_all(
            copies, "seq", split_axis=0, concat_axis=0, axis_index_groups=same_core, tiled=True
        )
        return got.reshape((half,) + own.shape)

    pair = jnp.stack([own, lax.ppermute(own, "seq", swap_halves)])
    far_pair = lax.ppermute(pair, "head", swap_heads)
    first = spread(copied(pair))

    coded = near[:, rows:].astype(jnp.int32)
    coded = coded[:, :head_count] * 16 + coded[:, head_count:]
    coded = jnp.concatenate(
        [lax.dynamic_slice_in_dim(coded, jnp.bitwise_xor(place, i), 1, axis=0) for i in range(half)], axis=0
    )
    slot_ids = by_slot(coded, half_at, core)
    far_ids = lax.ppermute(slot_ids, "head", swap_heads)
    far_copies = copied(far_pair)
    first, slot_ids, far_ids, far_copies, far[1] = lax.optimization_barrier(
        (first, slot_ids, far_ids, far_copies, far[1])
    )
    second = lax.ppermute(first, "seq", swap_cores)
    third = spread(far_copies)

    pieces = 4
    tok_tile = 2 * tok_rows
    features = expand(slot_ids, 0, first, None, 0, pieces, 2 * tok_tile)
    features = expand(slot_ids, 1, second, features, 1, pieces, 2 * tok_tile)
    features, third, far[2] = lax.optimization_barrier((features, third, far[2]))
    fourth = lax.ppermute(third, "seq", swap_cores)
    features = expand(far_ids, 0, third, features, 2, pieces, 2 * tok_tile)
    features = expand(far_ids, 1, fourth, features, 3, pieces, 2 * tok_tile)
    places = jnp.stack([head_at, core, half_at, place]).astype(jnp.int32)
    near_out = project(places, features, near, far, tok_tile)
    mixed = lax.all_to_all(
        near_out.reshape(half, tok_rows, cols_each),
        "seq",
        split_axis=0,
        concat_axis=0,
        axis_index_groups=halves,
        tiled=True,
    )
    return mixed.transpose(1, 0, 2).reshape(tok_rows, cols)


def fits(queries, out_weight):
    n_seq = lax.axis_size("seq")
    tok_rows, head_count, e_width = queries.shape
    return (
        head_count == n_seq
        and lax.axis_size("head") == 2
        and n_seq >= 8
        and n_seq & (n_seq - 1) == 0
        and e_width == 128
        and tok_rows % e_width == 0
        and out_weight.shape[0] == 2 * e_width
        and out_weight.shape[1] == n_seq // 2 * tok_rows
        and out_weight.shape[1] % (n_seq // 2 * 128) == 0
    )


def on_device(queries, keys, values, cluster_ids, out_weight):
    if fits(queries, out_weight):
        return by_head(queries, keys, values, cluster_ids, out_weight)
    return by_reduction(queries, keys, values, cluster_ids, out_weight)


def solution(mesh):
    placed = (
        P("seq", "head", None),
        P("seq", "head", None),
        P("seq", "head", None),
        P("seq", "head"),
        P("seq", "head"),
    )
    return jax.shard_map(
        on_device, mesh=mesh, in_specs=placed, out_specs=P("seq", "head"), check_vma=False
    )
```
